32 devices in a mesh: dp: 16 (over z, x, core), mp: 2 (over y).
Axes of the slice: x: 2, y: 2, z: 4, core: 2. Of those that a mesh axis runs over, the one named last changes fastest.
Arguments:
- tokens: bfloat16 [24576, 768], P(('dp', 'mp')), may hold values from -6 to 6
- lengths: int32 [48, 4], P('dp'), may hold values from 0 to 512, as said below
- buckets: int32 [48], P('dp'), may hold values from 0 to 2, as said below
- w_query: bfloat16 [768, 768], P(None, 'mp'), may hold values from -0.3125 to 0.3125
- b_query: bfloat16 [768], P('mp'), may hold values from -2 to 2
- w_key: bfloat16 [768, 768], P(None, 'mp'), may hold values from -0.21875 to 0.21875
- w_value: bfloat16 [768, 768], P(None, 'mp'), may hold values from -0.21875 to 0.21875
- b_value: bfloat16 [768], P('mp'), may hold values from -1 to 1
- w_out: bfloat16 [768, 768], P('mp'), may hold values from -1.75 to 1.75
- b_out: bfloat16 [768], replicated, may hold values from -2 to 2
- norm1_gain: bfloat16 [768], replicated, may hold values from 0.5 to 1.5
- norm1_bias: bfloat16 [768], replicated, may hold values from -2 to 2
- w_up: bfloat16 [768, 3072], P(None, 'mp'), may hold values from -0.21875 to 0.21875
- b_up: bfloat16 [3072], P('mp'), may hold values from -2 to 2
- w_down: bfloat16 [3072, 768], P('mp'), may hold values from -0.109375 to 0.109375
- b_down: bfloat16 [768], replicated, may hold values from -2 to 2
- norm2_gain: bfloat16 [768], replicated, may hold values from 0.5 to 1.5
- norm2_bias: bfloat16 [768], replicated, may hold values from -2 to 2
- cotangent: bfloat16 [24576, 768], P(('dp', 'mp')), may hold values from -6 to 6
Outputs:
- output: bfloat16 [24576, 768], P(('dp', 'mp'))
- input_grad: float32 [24576, 768], P(('dp', 'mp'))
- w_query_grad: float32 [768, 768], P(None, 'mp')
- b_query_grad: float32 [768], P('mp')
- w_key_grad: float32 [768, 768], P(None, 'mp')
- w_value_grad: float32 [768, 768], P(None, 'mp')
- b_value_grad: float32 [768], P('mp')
- w_out_grad: float32 [768, 768], P('mp')
- b_out_grad: float32 [768], replicated
- norm1_gain_grad: float32 [768], replicated
- norm1_bias_grad: float32 [768], replicated
- w_up_grad: float32 [768, 3072], P(None, 'mp')
- b_up_grad: float32 [3072], P('mp')
- w_down_grad: float32 [3072, 768], P('mp')
- b_down_grad: float32 [768], replicated
- norm2_gain_grad: float32 [768], replicated
- norm2_bias_grad: float32 [768], replicated
The draws below stay inside these ranges and needn't reach their ends.
Inputs may be any that keep to these rules, and one draw needn't show every extreme that they name: `buckets`: each of the values 0, 1, 2 is taken by exactly 16 blocks. For block b with 2**buckets[b] rows, slots j < 2**buckets[b] hold lengths of 1 to 512 / 2**buckets[b], slot 0 always the full row size; the other slots are 0.
All inputs are finite; a program needn't handle non-finite values.
Results may differ from the reference program's by a relative error of at most 0.018.
Values may be sent and summed in bfloat16 or wider, within the bound.
A program may use at most 128 MiB of HBM per device.

```python
from functools import partial
import jax
import jax.numpy as jnp
from jax import lax

D = 768
HEADS = 12
FF = 3072
HEAD_DIM = 64
SEG = 512
BLOCKS = 48
TOKENS = 24576


def bucket_layout(key):
    base = jax.random.fold_in(key, 11)
    order = jax.random.permutation(jax.random.fold_in(base, 1), BLOCKS)
    bucket = (order % 3).astype(jnp.int32)
    span = jnp.where(bucket == 0, SEG, jnp.where(bucket == 1, SEG // 2, SEG // 4)).astype(jnp.int32)
    count = jnp.where(bucket == 0, 1, jnp.where(bucket == 1, 2, 4)).astype(jnp.int32)
    raw = jax.random.randint(jax.random.fold_in(base, 2), (BLOCKS, 4), 0, SEG).astype(jnp.int32)
    lens = raw % span[:, None] + 1
    slots = jnp.arange(4, dtype=jnp.int32)
    lens = jnp.where(slots[None, :] == 0, span[:, None], lens)
    lens = jnp.where(slots[None, :] < count[:, None], lens, 0)
    return (bucket, lens.astype(jnp.int32))


def draw_buckets(key, part):
    return bucket_layout(key)[0]


def draw_lengths(key, part):
    return bucket_layout(key)[1]


def shard_levels(own_key, dims, shards, least, largest):
    level = 1.0
    for dim, parts in shards:
        steps = jax.random.uniform(jax.random.fold_in(jax.random.fold_in(own_key, 6), dim), (parts,), jnp.float32, least / len(shards), largest / len(shards))
        level = level * jnp.repeat(jnp.exp(steps), dims[dim] // parts).reshape((-1,) + (1,) * (len(dims) - 1 - dim))
    return level


def normal_values(key, dims, scale, most, shards=(), kind=jnp.bfloat16):
    array = jax.random.normal(key, dims, jnp.float32) * scale
    if len(shards) > 0:
        array = shard_levels(key, dims, shards, -0.22, 0.18) * array
    return jnp.clip(array, min=-most, max=most).astype(kind)


def setup_inputs(seed: int = 0) -> dict:
    splits = jax.random.split(jax.random.key(seed), 20)
    tokens = normal_values(splits[0], (TOKENS, D), 1.0, 6.0, ((0, 32),))
    lengths = draw_lengths(jax.random.fold_in(splits[19], 71), 0)
    buckets = draw_buckets(jax.random.fold_in(splits[19], 71), 0)
    w_query = normal_values(splits[3], (D, D), (D // 2) ** -0.5, 0.3125, ((1, 2),))
    b_query = normal_values(splits[4], (D,), 0.3, 2.0, ((0, 2),))
    w_key = normal_values(splits[5], (D, D), D ** -0.5, 0.21875, ((1, 2),))
    w_value = normal_values(splits[6], (D, D), D ** -0.5, 0.21875, ((1, 2),))
    b_value = normal_values(splits[7], (D,), 0.1, 1.0, ((0, 2),))
    w_out = normal_values(splits[8], (D, D), (max(D // 64, 4)) ** -0.5, 1.75, ((0, 2),))
    b_out = normal_values(splits[9], (D,), 0.3, 2.0)
    norm1_gain = jnp.clip(1.0 + 0.1 * jax.random.normal(splits[10], (D,), jnp.float32), 0.5, 1.5).astype(jnp.bfloat16)
    norm1_bias = normal_values(splits[11], (D,), 0.3, 2.0)
    w_up = normal_values(splits[12], (D, FF), D ** -0.5, 0.21875, ((1, 2),))
    b_up = normal_values(splits[13], (FF,), 0.3, 2.0, ((0, 2),))
    w_down = normal_values(splits[14], (FF, D), FF ** -0.5, 0.109375, ((0, 2),))
    b_down = normal_values(splits[15], (D,), 0.3, 2.0)
    norm2_gain = jnp.clip(1.0 + 0.1 * jax.random.normal(splits[16], (D,), jnp.float32), 0.5, 1.5).astype(jnp.bfloat16)
    norm2_bias = normal_values(splits[17], (D,), 0.3, 2.0)
    cotangent = normal_values(splits[18], (TOKENS, D), 1.0, 6.0, ((0, 32),))
    return {"tokens": tokens, "lengths": lengths, "buckets": buckets, "w_query": w_query, "b_query": b_query, "w_key": w_key, "w_value": w_value, "b_value": b_value, "w_out": w_out, "b_out": b_out, "norm1_gain": norm1_gain, "norm1_bias": norm1_bias, "w_up": w_up, "b_up": b_up, "w_down": w_down, "b_down": b_down, "norm2_gain": norm2_gain, "norm2_bias": norm2_bias, "cotangent": cotangent}


@jax.custom_vjp
def low(v):
    return lax.optimization_barrier(v.astype(jnp.bfloat16)).astype(jnp.float32)

@jax.custom_vjp
def low_back(v):
    return v

def low_keep(v):
    return (low(v), None)

def low_pass(kept, grad):
    return (grad,)

def back_keep(v):
    return (v, None)

def back_low(kept, grad):
    return (low(grad),)
low.defvjp(low_keep, low_pass)
low_back.defvjp(back_keep, back_low)
NEG = -1e+30
EPS = 1e-12

def block_layout(bucket, lens):
    places = jnp.arange(SEG, dtype=jnp.int32)
    span = jnp.where(bucket == 0, SEG, jnp.where(bucket == 1, SEG // 2, SEG // 4)).astype(jnp.int32)
    row_ids = places // span
    inside = places - row_ids * span
    slots = jnp.arange(4, dtype=jnp.int32)
    row_len = lax.optimization_barrier(jnp.sum(jnp.where(row_ids[:, None] == slots[None, :], lens[None, :], 0), axis=1))
    return (row_ids, inside < row_len)

def layer_norm(value, gain, shift):
    centre = value - lax.optimization_barrier(jnp.mean(value, axis=-1, keepdims=True))
    spread = lax.optimization_barrier(jnp.mean(centre * centre, axis=-1, keepdims=True))
    return centre * lax.rsqrt(spread + EPS) * gain + shift

def matmul(left, right):
    return jnp.dot(left, right, precision=lax.Precision.HIGHEST, preferred_element_type=jnp.float32)

def attend_block(item):
    query, keys, values, bucket, lens = item
    row_ids, valid = block_layout(bucket, lens)
    allowed = (row_ids[:, None] == row_ids[None, :]) & valid[None, :]
    scores = low_back(jnp.einsum('qhe,khe->hqk', query, keys, precision=lax.Precision.HIGHEST) * HEAD_DIM ** (-0.5))
    scores = jnp.where(allowed[None], scores, NEG)
    probs = jnp.exp(scores - jax.nn.logsumexp(scores, axis=-1, keepdims=True))
    return jnp.einsum('hqk,khe->qhe', low(probs), values, precision=lax.Precision.HIGHEST).reshape(SEG, D)

def forward(buckets, lengths, tokens, w_query, b_query, w_key, w_value, b_value, w_out, b_out, norm1_gain, norm1_bias, w_up, b_up, w_down, b_down, norm2_gain, norm2_bias):
    query = low(low_back(matmul(tokens, w_query) + b_query))
    keys = low(low_back(matmul(tokens, w_key)))
    values = low(low_back(matmul(tokens, w_value) + b_value))
    shape = (BLOCKS, SEG, HEADS, HEAD_DIM)
    context = lax.map(jax.checkpoint(attend_block), (query.reshape(shape), keys.reshape(shape), values.reshape(shape), buckets, lengths))
    context = low(low_back(context.reshape(TOKENS, D)))
    attended = low_back(matmul(context, w_out)) + b_out
    hidden = low(layer_norm(tokens + attended, norm1_gain, norm1_bias))
    inner = low_back(matmul(hidden, w_up) + b_up)
    active = low(jax.nn.gelu(inner, approximate=False))
    branch = low_back(matmul(active, w_down)) + b_down
    valid = jax.vmap(block_layout)(buckets, lengths)[1].reshape(TOKENS)
    return layer_norm(hidden + branch, norm2_gain, norm2_bias) * valid.astype(jnp.float32)[:, None]

def reference(tokens, lengths, buckets, w_query, b_query, w_key, w_value, b_value, w_out, b_out, norm1_gain, norm1_bias, w_up, b_up, w_down, b_down, norm2_gain, norm2_bias, cotangent):
    floats = [item.astype(jnp.float32) for item in (tokens, w_query, b_query, w_key, w_value, b_value, w_out, b_out, norm1_gain, norm1_bias, w_up, b_up, w_down, b_down, norm2_gain, norm2_bias)]
    result, pull = jax.vjp(partial(forward, buckets, lengths), *floats)
    grads = pull(cotangent.astype(jnp.float32))
    return (result.astype(jnp.bfloat16), grads[0], grads[1], grads[2], grads[3], grads[4], grads[5], grads[6], grads[7], grads[8], grads[9], grads[10], grads[11], grads[12], grads[13], grads[14], grads[15])
```

```python
import functools

import jax
import jax.numpy as jnp
from jax import lax
from jax.experimental import pallas as pl
from jax.experimental.pallas import tpu as pltpu
from jax.sharding import Mesh, PartitionSpec as P

HEAD_DIM = 64
SEG = 512
PAIR = 2 * HEAD_DIM
NEG = -1e30
EPS = 1e-12
ROOT_HALF = 0.7071067811865476
INV_ROOT_TWO_PI = 0.3989422804014327
F32 = jnp.float32
BF16 = jnp.bfloat16
VMEM_LIMIT = 60 * 1024 * 1024
TILE = 256
FFN_PARTS = 4
ATT_PARTS = 2


def mm(left, right):
    return lax.dot_general(left, right, (((1,), (0,)), ((), ())), preferred_element_type=F32)


def mm_nt(left, right):
    return lax.dot_general(left, right, (((1,), (1,)), ((), ())), preferred_element_type=F32)


def call(body, grid, pos, inputs, in_specs, out_shape, out_specs, scratch, flops, name):
    moved = sum(v.size * v.dtype.itemsize for v in inputs) + sum(
        v.size * v.dtype.itemsize for v in out_shape
    )
    return pl.pallas_call(
        body,
        grid_spec=pltpu.PrefetchScalarGridSpec(
            num_scalar_prefetch=1,
            grid=grid,
            in_specs=in_specs,
            out_specs=out_specs,
            scratch_shapes=scratch,
        ),
        out_shape=out_shape,
        compiler_params=pltpu.CompilerParams(
            dimension_semantics=("arbitrary",) * len(grid), vmem_limit_bytes=VMEM_LIMIT
        ),
        cost_estimate=pl.CostEstimate(flops=flops, bytes_accessed=moved, transcendentals=0),
        name=name,
    )(pos, *inputs)


def whole(array):
    zeros = (0,) * array.ndim
    return pl.BlockSpec(array.shape, lambda j, pos: zeros)


def shape(dims, kind):
    return jax.ShapeDtypeStruct(dims, kind)


def gelu_parts(inner):
    erf = lax.erf(inner * ROOT_HALF)
    below = 0.5 + 0.5 * erf
    density = jnp.exp(inner * inner * -0.5) * INV_ROOT_TWO_PI
    return inner * below, below + inner * density


def attend_forward_body(gathered, pos_ref, x_ref, *refs):
    if gathered:
        (p0, p1, pc, bq, bv, qs_a, ks_a, qs_m, ks_m) = refs[:9]
        (q_o, k_o, v_o, ctx_o, pa_o, pm_o, w_o, mask_a, mask_m, w_s) = refs[9:]
    else:
        (wq, wk, wv, bq, bv, qs_a, ks_a, qs_m, ks_m) = refs[:9]
        (q_o, k_o, v_o, ctx_o, pa_o, pm_o, mask_a, mask_m) = refs[9:]
    j = pl.program_id(0)
    rows = q_o.shape[0]
    half = rows - SEG

    @pl.when(j == 0)
    def _():
        mask_a[...] = jnp.where(ks_a[...] == qs_a[...], 0.0, NEG)
        mask_m[...] = jnp.where(ks_m[...] == qs_m[...], 0.0, NEG)
        if gathered:
            quarter = p0.shape[0]
            width = p0.shape[1] // 3
            for rel, piece in enumerate((p0, p1, pc.at[0], pc.at[1])):
                row = pl.multiple_of((pos_ref[0] ^ rel) * quarter, 16)
                for pair in range(width // PAIR):
                    for part in range(3):
                        w_s[pair, pl.ds(row, quarter), part * PAIR : (part + 1) * PAIR] = piece[
                            :, part * width + pair * PAIR : part * width + (pair + 1) * PAIR
                        ]

    if gathered:
        w3 = w_s[j]
        w_o[0] = w3
    else:
        w3 = jnp.concatenate([wq[...], wk[...], wv[...]], axis=1)
    qkv = mm(x_ref[...], w3)
    query = ((qkv[:rows, :PAIR] + bq[...].astype(F32)) * HEAD_DIM**-0.5).astype(BF16)
    keys = qkv[:, PAIR : 2 * PAIR].astype(BF16)
    values = (qkv[:, 2 * PAIR :] + bv[...].astype(F32)).astype(BF16)
    q_o[...] = query
    k_o[...] = keys
    v_o[...] = values
    values_t = values.astype(F32).T.astype(BF16)
    lane = lax.broadcasted_iota(jnp.int32, (1, PAIR), 1) // HEAD_DIM
    for first, count, key_first, mask, p_o in (
        (0, SEG, 0, mask_a, pa_o),
        (SEG, half, SEG, mask_m, pm_o),
    ):
        parts = []
        for h in range(2):
            query_h = jnp.where(lane == h, query[first : first + count], jnp.zeros((), BF16))
            scores = mm_nt(keys[key_first : key_first + SEG], query_h) + mask[...]
            top = jnp.max(scores, axis=0, keepdims=True)
            grown = jnp.exp(scores - top)
            probs = (grown * (1.0 / jnp.sum(grown, axis=0, keepdims=True))).astype(BF16)
            p_o[h] = probs
            parts.append(
                mm(
                    values_t[h * HEAD_DIM : (h + 1) * HEAD_DIM, key_first : key_first + SEG],
                    probs,
                )
            )
        ctx_o[first : first + count] = jnp.concatenate(parts, axis=0).T.astype(BF16)


def attend_forward(pos, x, weights, bq, bv, segs, rows, gathered):
    total = x.shape[0]
    dim = x.shape[1]
    width = bq.shape[1]
    pairs = width // PAIR
    half = rows - SEG
    column = lambda n: pl.BlockSpec((n, PAIR), lambda j, pos: (0, j))
    out_shape = [
        shape((rows, width), BF16),
        shape((total, width), BF16),
        shape((total, width), BF16),
        shape((rows, width), BF16),
        shape((2 * pairs, SEG, SEG), BF16),
        shape((2 * pairs, SEG, half), BF16),
    ]
    out_specs = [
        column(rows),
        column(total),
        column(total),
        column(rows),
        pl.BlockSpec((2, SEG, SEG), lambda j, pos: (j, 0, 0)),
        pl.BlockSpec((2, SEG, half), lambda j, pos: (j, 0, 0)),
    ]
    scratch = [pltpu.VMEM((SEG, SEG), F32), pltpu.VMEM((SEG, half), F32)]
    if gathered:
        w_specs = [whole(w) for w in weights]
        out_shape.append(shape((pairs, dim, 3 * PAIR), BF16))
        out_specs.append(pl.BlockSpec((1, dim, 3 * PAIR), lambda j, pos: (j, 0, 0)))
        scratch.append(pltpu.VMEM((pairs, dim, 3 * PAIR), BF16))
    else:
        w_specs = [column(dim) for w in weights]
    inputs = [x, *weights, bq, bv, *segs]
    specs = [whole(x), *w_specs, column(1), column(1), *[whole(s) for s in segs]]
    flops = 2 * total * dim * 3 * width + 8 * 2 * SEG * rows * width
    return call(
        functools.partial(attend_forward_body, gathered),
        (pairs,),
        pos,
        inputs,
        specs,
        out_shape,
        out_specs,
        scratch,
        flops,
        "attend_fwd_other" if gathered else "attend_fwd_own",
    )


def up_body(
    pos_ref, x, ctx_i, ctx_o, wo_i, o0, o1, oc, b_out, gain, bias, wu, bu, wd,
    normed_o, inv_o, hidden_o, wo_all, active_o, slope_o, branch_o,
):
    j = pl.program_id(0)
    rows = x.shape[0]

    @pl.when(j == 0)
    def _():
        quarter = o0.shape[0]
        for rel, piece in enumerate((o0, o1, oc.at[0], oc.at[1])):
            row = pl.multiple_of((pos_ref[0] ^ rel) * quarter, 16)
            wo_all[pl.ds(row, quarter), :] = piece[...]
        for r in range(0, rows, TILE):
            at = slice(r, r + TILE)
            first = (
                x[at].astype(F32)
                + (mm(ctx_i[at], wo_i[...]) + mm(ctx_o[at], wo_all[...]))
                + b_out[...].astype(F32)
            )
            centre = first - jnp.mean(first, axis=-1, keepdims=True)
            inverse = lax.rsqrt(jnp.mean(centre * centre, axis=-1, keepdims=True) + EPS)
            normed = centre * inverse
            normed_o[at] = normed
            inv_o[at] = inverse
            hidden_o[at] = (normed * gain[...].astype(F32) + bias[...].astype(F32)).astype(BF16)

    for r in range(0, rows, TILE):
        at = slice(r, r + TILE)
        inner = mm(hidden_o[at], wu[...]) + bu[...].astype(F32)
        active, slope = gelu_parts(inner)
        active = active.astype(BF16)
        active_o[at] = active
        slope_o[at] = slope.astype(BF16)
        add = mm(active, wd[...])

        @pl.when(j == 0)
        def _():
            branch_o[at] = add

        @pl.when(j > 0)
        def _():
            branch_o[at] += add


def down_body(
    pos_ref, hidden, branch, u0, u1, uc, d0, d1, dc, bu, b_down, gain, bias, cot, keep,
    active_o, slope_o, out_o, grad_o, low_o, vec_o, wu, wd, acc,
):
    j = pl.program_id(0)
    rows = hidden.shape[0]

    @pl.when(j == 0)
    def _():
        wu[...] = u0[...]
        wd[...] = d0[...]
        acc[...] = branch[...]

    @pl.when(j == 1)
    def _():
        wu[...] = u1[...]
        wd[...] = d1[...]

    @pl.when(j > 1)
    def _():
        wu[...] = uc[0]
        wd[...] = dc[0]

    for r in range(0, rows, TILE):
        at = slice(r, r + TILE)
        inner = mm(hidden[at], wu[...]) + bu[...].astype(F32)
        active, slope = gelu_parts(inner)
        active = active.astype(BF16)
        active_o[at] = active
        slope_o[at] = slope.astype(BF16)
        acc[at] += mm(active, wd[...])

    @pl.when(j == pl.num_programs(0) - 1)
    def _():
        sums = [0.0, 0.0, 0.0]
        for r in range(0, rows, TILE):
            at = slice(r, r + TILE)
            second = hidden[at].astype(F32) + acc[at] + b_down[...].astype(F32)
            centre = second - jnp.mean(second, axis=-1, keepdims=True)
            inverse = lax.rsqrt(jnp.mean(centre * centre, axis=-1, keepdims=True) + EPS)
            normed = centre * inverse
            g = gain[...].astype(F32)
            out_o[at] = ((normed * g + bias[...].astype(F32)) * keep[at]).astype(BF16)
            upstream = cot[at].astype(F32) * keep[at]
            scaled = upstream * g
            grad = inverse * (
                scaled
                - jnp.mean(scaled, axis=-1, keepdims=True)
                - normed * jnp.mean(scaled * normed, axis=-1, keepdims=True)
            )
            grad_o[at] = grad
            low_o[at] = grad.astype(BF16)
            sums[0] += jnp.sum(upstream * normed, axis=0, keepdims=True)
            sums[1] += jnp.sum(upstream, axis=0, keepdims=True)
            sums[2] += jnp.sum(grad, axis=0, keepdims=True)
        for i, value in enumerate(sums):
            vec_o[i : i + 1] = value


def ffn_back_body(gathered, pos_ref, low, hidden, active, slope, *refs):
    if gathered:
        u0, u1, uc, d0, d1, dc, hg_in = refs[:7]
        hg, send, keep, bup, low_t, hidden_t, ig, grads, wu, wd = refs[7:]
    else:
        wu, wd, hg_in = refs[:3]
        hg, send, keep, bup, low_t, hidden_t, ig, grads = refs[3:]
    j = pl.program_id(0)
    rows = low.shape[0]
    dim = low.shape[1]

    @pl.when(j == 0)
    def _():
        low_t[...] = low[...].T
        hidden_t[...] = hidden[...].T
        hg[...] = hg_in[...]

    if gathered:

        @pl.when(j < 2)
        def _():
            wu[...] = uc[0]
            wd[...] = dc[0]

        @pl.when(j == 2)
        def _():
            wu[...] = u0[...]
            wd[...] = d0[...]

        @pl.when(j == 3)
        def _():
            wu[...] = u1[...]
            wd[...] = d1[...]

    total = 0.0
    for r in range(0, rows, TILE):
        at = slice(r, r + TILE)
        inner_grad = (mm_nt(low[at], wd[...]) * slope[at].astype(F32)).astype(BF16)
        ig[at] = inner_grad
        total += jnp.sum(inner_grad.astype(F32), axis=0, keepdims=True)
        hg[at] += mm_nt(inner_grad, wu[...])
    bup[0] = total
    for r in range(0, dim, TILE):
        grads[r : r + TILE] = mm(hidden_t[r : r + TILE], ig[...]).astype(BF16)
        grads[dim + r : dim + r + TILE] = mm(low_t[r : r + TILE], active[...]).astype(BF16)

    @pl.when(j < 2)
    def _():
        send[0] = grads[...]

    @pl.when(j >= 2)
    def _():
        keep[0] = grads[...]


def ffn_back(pos, low, hidden, active, slope, weights, hg_in, gathered):
    rows, dim = low.shape
    width = active.shape[1]
    quarter = width // 4
    chunk = lambda n: pl.BlockSpec((n, quarter), lambda j, pos: (0, j ^ 2))
    scratch = [
        pltpu.VMEM((dim, rows), BF16),
        pltpu.VMEM((dim, rows), BF16),
        pltpu.VMEM((rows, quarter), BF16),
        pltpu.VMEM((2 * dim, quarter), BF16),
    ]
    if gathered:
        u0, u1, uc, d0, d1, dc = weights
        w_specs = [
            whole(u0),
            whole(u1),
            pl.BlockSpec((1, dim, quarter), lambda j, pos: (jnp.minimum(j, 1), 0, 0)),
            whole(d0),
            whole(d1),
            pl.BlockSpec((1, quarter, dim), lambda j, pos: (jnp.minimum(j, 1), 0, 0)),
        ]
        scratch += [pltpu.VMEM((dim, quarter), BF16), pltpu.VMEM((quarter, dim), BF16)]
    else:
        w_specs = [
            pl.BlockSpec((dim, quarter), lambda j, pos: (0, pos[0] ^ j ^ 2)),
            pl.BlockSpec((quarter, dim), lambda j, pos: (pos[0] ^ j ^ 2, 0)),
        ]
    piece = (2, 2 * dim, quarter)
    return call(
        functools.partial(ffn_back_body, gathered),
        (4,),
        pos,
        [low, hidden, active, slope, *weights, hg_in],
        [whole(low), whole(hidden), chunk(rows), chunk(rows), *w_specs, whole(hg_in)],
        [
            shape((rows, dim), F32),
            shape(piece, BF16),
            shape(piece, BF16),
            shape((4, 1, quarter), F32),
        ],
        [
            pl.BlockSpec((rows, dim), lambda j, pos: (0, 0)),
            pl.BlockSpec((1, 2 * dim, quarter), lambda j, pos: (jnp.minimum(j, 1), 0, 0)),
            pl.BlockSpec((1, 2 * dim, quarter), lambda j, pos: (jnp.maximum(j - 2, 0), 0, 0)),
            pl.BlockSpec((1, 1, quarter), lambda j, pos: (pos[0] ^ j ^ 2, 0, 0)),
        ],
        scratch,
        8 * rows * dim * width,
        "ffn_back_other" if gathered else "ffn_back_own",
    )


def out_back_body(
    pos_ref, hg, normed, inv, gain, wo_i, wo_o, ctx_i, ctx_o,
    first_o, dctx_i, dctx_o, keep_i, send_i, keep_o, send_o, vec_o, low_s, low_t,
):
    rows, dim = hg.shape
    sums = [0.0, 0.0, 0.0]
    for r in range(0, rows, TILE):
        at = slice(r, r + TILE)
        grad_in = hg[at]
        n = normed[at]
        scaled = grad_in * gain[...].astype(F32)
        grad = inv[at] * (
            scaled
            - jnp.mean(scaled, axis=-1, keepdims=True)
            - n * jnp.mean(scaled * n, axis=-1, keepdims=True)
        )
        first_o[at] = grad
        low = grad.astype(BF16)
        low_s[at] = low
        dctx_i[at] = mm_nt(low, wo_i[...]).astype(BF16)
        dctx_o[at] = mm_nt(low, wo_o[...]).astype(BF16)
        sums[0] += jnp.sum(grad_in * n, axis=0, keepdims=True)
        sums[1] += jnp.sum(grad_in, axis=0, keepdims=True)
        sums[2] += jnp.sum(grad, axis=0, keepdims=True)
    for i, value in enumerate(sums):
        vec_o[i : i + 1] = value
    low_t[...] = low_s[...].T
    quarter = dim // 4
    for rel in range(4):
        row = pl.multiple_of((pos_ref[0] ^ rel) * quarter, 16)
        block = low_t[pl.ds(row, quarter), :]
        at = slice((rel % 2) * quarter, (rel % 2 + 1) * quarter)
        (keep_i if rel < 2 else send_i)[at] = mm(block, ctx_i[...]).astype(BF16)
        (keep_o if rel < 2 else send_o)[at] = mm(block, ctx_o[...]).astype(BF16)


def attend_back_body(
    gathered, last, pos_ref, x, q, k, v, p_a, p_m, dctx, ctx, *refs
):
    if gathered:
        w3, refs = refs[0], refs[1:]
    else:
        (wq, wk, wv), refs = refs[:3], refs[3:]
    if last:
        (tot_in, first), refs = refs[:2], refs[2:]
    gk, gs, tot, keep, send, bq, bv, x_tmp, x_t, d3 = refs
    j = pl.program_id(0)
    rows = q.shape[0]
    total, dim = x.shape
    half = rows - SEG
    quarter = dim // 4

    @pl.when(j == 0)
    def _():
        x_tmp[...] = x[...].T
        for rel in range(4):
            row = pl.multiple_of((pos_ref[0] ^ rel) * quarter, 16)
            x_t[rel * quarter : (rel + 1) * quarter] = x_tmp[pl.ds(row, quarter), :]
        if last:
            tot[...] = tot_in[...]
            tot[:rows] += first[...]
        else:
            tot[...] = jnp.zeros_like(tot)
        d3[rows:, :PAIR] = jnp.zeros((total - rows, PAIR), BF16)

    @pl.when(j < 3)
    def _():
        lane = lax.broadcasted_iota(jnp.int32, (1, PAIR), 1) // HEAD_DIM
        zero = jnp.zeros((), BF16)
        delta_t = (dctx[...].astype(F32) * ctx[...].astype(F32)).T
        keys_t = k[...].astype(F32).T.astype(BF16)
        for first_row, count, key_first, p in ((0, SEG, 0, p_a), (SEG, half, SEG, p_m)):
            at = slice(first_row, first_row + count)
            ks = slice(key_first, key_first + SEG)
            values_grad = keys_grad = 0.0
            query_parts = []
            for h in range(2):
                grad_h = jnp.where(lane == h, dctx[at], zero)
                query_h = jnp.where(lane == h, q[at], zero)
                probs = p[h]
                delta = jnp.sum(
                    delta_t[h * HEAD_DIM : (h + 1) * HEAD_DIM, at], axis=0, keepdims=True
                )
                prob_grad = mm_nt(v[ks], grad_h)
                score_grad = (probs.astype(F32) * (prob_grad - delta)).astype(BF16)
                values_grad += mm(probs, grad_h)
                keys_grad += mm(score_grad, query_h)
                query_parts.append(
                    mm(keys_t[h * HEAD_DIM : (h + 1) * HEAD_DIM, ks], score_grad)
                )
            query_grad = jnp.concatenate(query_parts, axis=0).T * HEAD_DIM**-0.5
            d3[at, :PAIR] = query_grad.astype(BF16)
            d3[ks, PAIR : 2 * PAIR] = keys_grad.astype(BF16)
            d3[ks, 2 * PAIR :] = values_grad.astype(BF16)
        bq[...] = jnp.sum(d3[:rows, :PAIR].astype(F32), axis=0, keepdims=True)
        bv[...] = jnp.sum(d3[:, 2 * PAIR :].astype(F32), axis=0, keepdims=True)
        if gathered:
            w = w3[0]
        else:
            w = jnp.concatenate([wq[...], wk[...], wv[...]], axis=1)
        tot[...] += mm_nt(d3[...], w)
        keep[...] = mm(x_t[: 2 * quarter], d3[...]).astype(BF16)
        send[...] = mm(x_t[2 * quarter :], d3[...]).astype(BF16)

    @pl.when(j == 3)
    def _():
        keep[...] = gk[...]
        send[...] = gs[...]


def attend_back(pos, x, saved, dctx, weights, sums, grads, gathered, last):
    q, k, v, ctx, p_a, p_m = saved
    rows, width = q.shape
    total, dim = x.shape
    half = rows - SEG
    pairs = width // PAIR
    column = lambda n: pl.BlockSpec((n, PAIR), lambda j, pos: (0, jnp.minimum(j, pairs - 1)))
    plane = lambda a, b, c: pl.BlockSpec(
        (a, b, c), lambda j, pos: (jnp.minimum(j, pairs - 1), 0, 0)
    )
    if gathered:
        w_specs = [plane(1, dim, 3 * PAIR)]
    else:
        w_specs = [column(dim)] * 3
    out = pl.BlockSpec((dim // 2, 3 * PAIR), lambda j, pos: (0, j))
    return call(
        functools.partial(attend_back_body, gathered, last),
        (pairs + 1,),
        pos,
        [x, q, k, v, p_a, p_m, dctx, ctx, *weights, *sums, *grads],
        [
            whole(x),
            column(rows),
            column(total),
            column(total),
            plane(2, SEG, SEG),
            plane(2, SEG, half),
            column(rows),
            column(rows),
            *w_specs,
            *[whole(s) for s in sums],
            *[whole(g) for g in grads],
        ],
        [
            shape((total, dim), F32),
            shape((dim // 2, 3 * width + 3 * PAIR), BF16),
            shape((dim // 2, 3 * width + 3 * PAIR), BF16),
            shape((1, width), F32),
            shape((1, width), F32),
        ],
        [
            pl.BlockSpec((total, dim), lambda j, pos: (0, 0)),
            out,
            out,
            column(1),
            column(1),
        ],
        [
            pltpu.VMEM((dim, total), BF16),
            pltpu.VMEM((dim, total), BF16),
            pltpu.VMEM((total, 3 * PAIR), BF16),
        ],
        2 * total * dim * 3 * width * 2 + 16 * 2 * SEG * rows * width,
        "attend_back_other" if gathered else "attend_back_own",
    )


def ffn_final_body(pos_ref, a, b, c, up_o, down_o):
    j = pl.program_id(0)
    dim = up_o.shape[0]

    def put(piece):
        up_o[...] = piece[:dim].astype(F32)
        down_o[...] = piece[dim:].astype(F32).T

    @pl.when(j == 0)
    def _():
        put(a)

    @pl.when(j == 1)
    def _():
        put(b)

    @pl.when(j > 1)
    def _():
        put(c.at[0])


def att_final_body(pos_ref, a, b, c, q_o, k_o, v_o, out_o, tmp):
    quarter = a.shape[0]
    width = q_o.shape[1]
    for rel, piece in enumerate((a, b, c.at[0], c.at[1])):
        row = pl.multiple_of((pos_ref[0] ^ rel) * quarter, 16)
        for part, ref in enumerate((q_o, k_o, v_o)):
            for pair in range(width // PAIR):
                ref[pl.ds(row, quarter), pair * PAIR : (pair + 1) * PAIR] = piece[
                    :, (3 * pair + part) * PAIR : (3 * pair + part + 1) * PAIR
                ].astype(F32)
        tmp[pl.ds(row, quarter), :] = piece[:, 3 * width :].astype(F32)
    out_o[...] = tmp[...].T


def row_layout(bucket, lens, places):
    span = jnp.where(bucket == 0, SEG, jnp.where(bucket == 1, SEG // 2, SEG // 4)).astype(jnp.int32)
    row_ids = places // span
    slots = jnp.arange(4, dtype=jnp.int32)
    row_len = jnp.sum(jnp.where(row_ids[:, None] == slots[None, :], lens[None, :], 0), axis=1)
    return row_ids, places - row_ids * span < row_len


def swap(value, axis):
    return lax.ppermute(value, axis, [(0, 1), (1, 0)])


def shards(
    depth,
    tokens, lengths, buckets, w_query, b_query, w_key, w_value, b_value, w_out, b_out,
    norm1_gain, norm1_bias, w_up, b_up, w_down, b_down, norm2_gain, norm2_bias, cotangent,
):
    iz, ix, ic, iy = (lax.axis_index(a) for a in ("z", "x", "c", "y"))
    place = 2 * ic + ix
    pos = place.astype(jnp.int32).reshape(1)
    rows, dim = tokens.shape
    half = rows - SEG
    width = w_query.shape[1]
    units = w_up.shape[1]
    chunk = units // 4
    same = ic == iy

    def own_rows(value):
        full = lax.dynamic_slice_in_dim(value, iy * half, SEG)
        middle = lax.dynamic_slice_in_dim(value, (1 - iy) * SEG, half)
        return full, middle

    x_full, x_mid = own_rows(tokens)
    from_y = lax.ppermute(x_mid, ("c", "y"), [(1, 0), (2, 3)])
    from_c = lax.ppermute(jnp.stack([x_mid, from_y]), ("c", "y"), [(0, 2), (3, 1)])
    x = jnp.concatenate(
        [x_full, jnp.where(same, x_mid, from_c[1]), jnp.where(same, from_y, from_c[0])]
    )

    def gather(piece):
        a = swap(piece, "y")
        b = swap(a, "x")
        return a, b, swap(jnp.stack([a, b]), "c")

    def rows_at(w):
        return lax.dynamic_slice_in_dim(w, place * (w.shape[0] // 4), w.shape[0] // 4)

    bias_own = jnp.concatenate([b_query, b_value, b_up])[None]
    bias_other = swap(bias_own, "y")
    w_qkv = gather(
        jnp.concatenate([rows_at(w_query), rows_at(w_key), rows_at(w_value)], axis=1)
    )
    w_o = gather(rows_at(w_out))
    w_u = gather(lax.dynamic_slice_in_dim(w_up, place * chunk, chunk, axis=1))
    w_d = gather(rows_at(w_down))

    info = jnp.concatenate([buckets[1:2], lengths[1]]).reshape(1, 5)
    info = jnp.where(same, info, swap(info, "c"))[0]
    places = jnp.arange(SEG, dtype=jnp.int32)
    block = 2 * iy
    ids_a, ok_a = row_layout(
        lax.dynamic_index_in_dim(buckets, block, keepdims=False),
        lax.dynamic_index_in_dim(lengths, block, keepdims=False),
        places,
    )
    ids_m, ok_m = row_layout(info[0], info[1:], (places + half * ic) % SEG)
    segs = (
        ids_a[None],
        jnp.where(ok_a, ids_a, -1)[:, None],
        ids_m[None, :half],
        jnp.where(ok_m, ids_m, -1)[:, None],
    )
    keep = jnp.concatenate([ok_a, ok_m[:half]]).astype(F32)[:, None]

    cot_full, cot_mid = own_rows(cotangent)
    crossed = lambda value: lax.ppermute(value, ("c", "y"), [(1, 2), (2, 1)])
    cot = jnp.concatenate([cot_full, jnp.where(same, cot_mid, crossed(cot_mid))])

    own = attend_forward(
        pos, x, (w_query, w_key, w_value), b_query[None], b_value[None], segs, rows, False
    )
    other = attend_forward(
        pos, x, w_qkv, bias_other[:, :width], bias_other[:, width : 2 * width], segs, rows, True
    )
    w3_other = other[6]
    ctx_i, ctx_o = own[3], other[3]
    row_vec = lambda v: v[None]
    const = lambda *dims: pl.BlockSpec(dims, lambda j, pos: (0,) * len(dims))
    cols = pl.BlockSpec((rows, chunk), lambda j, pos: (0, j))
    b_out1, g1, s1 = row_vec(b_out), row_vec(norm1_gain), row_vec(norm1_bias)
    normed1, inverse1, hidden, wo_other, act_i, slope_i, branch = call(
        up_body,
        (4,),
        pos,
        [x, ctx_i, ctx_o, w_out, *w_o, b_out1, g1, s1, w_up, b_up[None], w_down],
        [
            const(rows, dim),
            whole(ctx_i),
            whole(ctx_o),
            whole(w_out),
            *[whole(w) for w in w_o],
            whole(b_out1),
            whole(g1),
            whole(s1),
            pl.BlockSpec((dim, chunk), lambda j, pos: (0, pos[0] ^ j)),
            pl.BlockSpec((1, chunk), lambda j, pos: (0, pos[0] ^ j)),
            pl.BlockSpec((chunk, dim), lambda j, pos: (pos[0] ^ j, 0)),
        ],
        [
            shape((rows, dim), F32),
            shape((rows, 1), F32),
            shape((rows, dim), BF16),
            shape((width, dim), BF16),
            shape((rows, units), BF16),
            shape((rows, units), BF16),
            shape((rows, dim), F32),
        ],
        [const(rows, dim), const(rows, 1), const(rows, dim), const(width, dim), cols, cols, const(rows, dim)],
        [],
        2 * rows * dim * (dim + 2 * units),
        "ffn_fwd_own",
    )
    pick = lambda *dims: pl.BlockSpec((1, *dims), lambda j, pos: (jnp.maximum(j - 2, 0), 0, 0))
    b_down1, g2, s2 = row_vec(b_down), row_vec(norm2_gain), row_vec(norm2_bias)
    b_up_other = bias_other[:, 2 * width :]
    act_o, slope_o, output, second, low, vec2 = call(
        down_body,
        (4,),
        pos,
        [hidden, branch, *w_u, *w_d, b_up_other, b_down1, g2, s2, cot, keep],
        [
            whole(hidden),
            whole(branch),
            whole(w_u[0]),
            whole(w_u[1]),
            pick(dim, chunk),
            whole(w_d[0]),
            whole(w_d[1]),
            pick(chunk, dim),
            pl.BlockSpec((1, chunk), lambda j, pos: (0, pos[0] ^ j)),
            whole(b_down1),
            whole(g2),
            whole(s2),
            whole(cot),
            whole(keep),
        ],
        [
            shape((rows, units), BF16),
            shape((rows, units), BF16),
            shape((rows, dim), BF16),
            shape((rows, dim), F32),
            shape((rows, dim), BF16),
            shape((3, dim), F32),
        ],
        [cols, cols, const(rows, dim), const(rows, dim), const(rows, dim), const(3, dim)],
        [pltpu.VMEM((dim, chunk), BF16), pltpu.VMEM((chunk, dim), BF16), pltpu.VMEM((rows, dim), F32)],
        4 * rows * dim * units,
        "ffn_fwd_other",
    )
    out_mid = output[SEG:]
    out_mid = jnp.where(same, out_mid, crossed(out_mid))

    def place_rows(full, middle):
        return jnp.where(
            iy == 0, jnp.concatenate([full, middle]), jnp.concatenate([middle, full])
        )

    output = place_rows(output[:SEG], out_mid)

    def start_other(send, keep_part):
        return keep_part.astype(F32) + swap(send, "c").astype(F32)

    def z_sum(value):
        step = 1
        while step < depth:
            n = value.shape[0] // 2
            bit = (iz // step) % 2
            links = [(i, i ^ step) for i in range(depth)]
            out = lax.dynamic_slice_in_dim(value, (1 - bit) * n, n)
            kept = lax.dynamic_slice_in_dim(value, bit * n, n)
            got = lax.ppermute(out, "z", links)
            value = (kept.astype(F32) + got.astype(F32)).astype(BF16)
            step *= 2
        while step > 1:
            step //= 2
            bit = (iz // step) % 2
            got = lax.ppermute(value, "z", [(i, i ^ step) for i in range(depth)])
            value = jnp.where(
                bit == 0, jnp.concatenate([value, got]), jnp.concatenate([got, value])
            )
        return value

    def reduce_parts(own_grads, other_grads, parts, size):
        send_i, keep_i = own_grads
        send_o, keep_o = other_grads
        got_o = swap(send_o, "c")
        got_i = swap(send_i, "c")
        firsts, seconds = [], []
        for n in range(parts):
            at = slice(n * size // parts, (n + 1) * size // parts)
            mine = (keep_o[:, at].astype(F32) + got_o[:, at].astype(F32)).astype(BF16)
            got_y = swap(mine, "y").astype(F32)
            kept = keep_i[:, at].astype(F32) + got_i[:, at].astype(F32) + got_y
            kept0, kept1 = kept[0].astype(BF16), kept[1].astype(BF16)
            mine = (kept0.astype(F32) + swap(kept1, "x").astype(F32)).astype(BF16)
            mine = z_sum(mine)
            firsts.append(mine)
            seconds.append(swap(mine, "x"))
        a = jnp.concatenate(firsts)
        b = jnp.concatenate(seconds)
        return a, b, swap(jnp.stack([a, b]), "c")

    hg, send_o, keep_o, bup_o = ffn_back(
        pos, low, hidden, act_o, slope_o, (*w_u, *w_d), second, True
    )
    hg, send_i, keep_i, bup_i = ffn_back(
        pos, low, hidden, act_i, slope_i, (w_up, w_down), hg, False
    )
    ffn = reduce_parts((send_i, keep_i), (send_o, keep_o), FFN_PARTS, 2 * dim)
    quarter = dim // 4
    part = (2 * quarter, width)
    first, dctx_i, dctx_o, ko_i, so_i, ko_o, so_o, vec1 = call(
        out_back_body,
        (1,),
        pos,
        [hg, normed1, inverse1, g1, w_out, wo_other, ctx_i, ctx_o],
        [whole(v) for v in (hg, normed1, inverse1, g1, w_out, wo_other, ctx_i, ctx_o)],
        [
            shape((rows, dim), F32),
            shape((rows, width), BF16),
            shape((rows, width), BF16),
            shape(part, BF16),
            shape(part, BF16),
            shape(part, BF16),
            shape(part, BF16),
            shape((3, dim), F32),
        ],
        [
            const(rows, dim),
            const(rows, width),
            const(rows, width),
            const(*part),
            const(*part),
            const(*part),
            const(*part),
            const(3, dim),
        ],
        [pltpu.VMEM((rows, dim), BF16), pltpu.VMEM((dim, rows), BF16)],
        4 * rows * dim * dim,
        "out_back",
    )
    total, ak_o, as_o, bq_o, bv_o = attend_back(
        pos, x, other[:6], dctx_o, (w3_other,), (), (ko_o, so_o), True, False
    )
    total, ak_i, as_i, bq_i, bv_i = attend_back(
        pos, x, own[:6], dctx_i, (w_query, w_key, w_value), (total, first), (ko_i, so_i), False, True
    )
    pieces = lambda v: v.reshape(2, quarter, v.shape[1])
    att = reduce_parts(
        (pieces(as_i), pieces(ak_i)), (pieces(as_o), pieces(ak_o)), ATT_PARTS, quarter
    )

    in_mid = total[SEG:rows] + swap(total[rows:].astype(BF16), "c").astype(F32)
    in_mid = jnp.where(same, in_mid, crossed(in_mid.astype(BF16)).astype(F32))
    input_grad = place_rows(total[:SEG], in_mid)

    def both(mine, theirs):
        return jnp.where(iy == 0, jnp.concatenate([mine, theirs]), jnp.concatenate([theirs, mine]))

    vec = jnp.concatenate(
        [
            both(bup_i.reshape(-1), bup_o.reshape(-1)).reshape(-1, dim),
            both(bq_i[0], bq_o[0]).reshape(-1, dim),
            both(bv_i[0], bv_o[0]).reshape(-1, dim),
            vec1,
            vec2,
        ]
    )
    for axis in ("c", "y", "x"):
        vec = vec + swap(vec, axis)
    step = 1
    while step < depth:
        vec = vec + lax.ppermute(vec, "z", [(i, i ^ step) for i in range(depth)])
        step *= 2
    up_rows = 2 * units // dim
    split = lambda v: lax.dynamic_slice_in_dim(v.reshape(-1), iy * (v.size // 2), v.size // 2)
    b_up_grad = split(vec[:up_rows])
    b_query_grad = split(vec[up_rows : up_rows + 1])
    b_value_grad = split(vec[up_rows + 1 : up_rows + 2])
    rest = vec[up_rows + 2 :]

    w_up_grad, w_down_grad = call(
        ffn_final_body,
        (4,),
        pos,
        list(ffn),
        [whole(ffn[0]), whole(ffn[1]), pick(2 * dim, chunk)],
        [shape((dim, units), F32), shape((units, dim), F32)],
        [
            pl.BlockSpec((dim, chunk), lambda j, pos: (0, pos[0] ^ j)),
            pl.BlockSpec((chunk, dim), lambda j, pos: (pos[0] ^ j, 0)),
        ],
        [],
        0,
        "ffn_final",
    )
    w_query_grad, w_key_grad, w_value_grad, w_out_grad = call(
        att_final_body,
        (1,),
        pos,
        list(att),
        [whole(v) for v in att],
        [shape((dim, width), F32)] * 3 + [shape((width, dim), F32)],
        [const(dim, width)] * 3 + [const(width, dim)],
        [pltpu.VMEM((dim, width), F32)],
        0,
        "att_final",
    )
    return (
        output,
        input_grad,
        w_query_grad,
        b_query_grad,
        w_key_grad,
        w_value_grad,
        b_value_grad,
        w_out_grad,
        rest[2],
        rest[0],
        rest[1],
        w_up_grad,
        b_up_grad,
        w_down_grad,
        rest[5],
        rest[3],
        rest[4],
    )


def solution(mesh):
    depth = mesh.shape["dp"] // 4
    inner = Mesh(mesh.devices.reshape(depth, 2, 2, mesh.shape["mp"]), ("z", "x", "c", "y"))
    dp = ("z", "x", "c")
    every = (*dp, "y")
    placed = (
        P(every, None),
        P(dp, None),
        P(dp),
        P(None, "y"),
        P("y"),
        P(None, "y"),
        P(None, "y"),
        P("y"),
        P("y", None),
        P(),
        P(),
        P(),
        P(None, "y"),
        P("y"),
        P("y", None),
        P(),
        P(),
        P(),
        P(every, None),
    )
    return jax.shard_map(
        functools.partial(shards, depth),
        mesh=inner,
        in_specs=placed,
        out_specs=(
            P(every, None),
            P(every, None),
            P(None, "y"),
            P("y"),
            P(None, "y"),
            P(None, "y"),
            P("y"),
            P("y", None),
            P(),
            P(),
            P(),
            P(None, "y"),
            P("y"),
            P("y", None),
            P(),
            P(),
            P(),
        ),
        check_vma=False,
    )
```

```python
import functools

import jax
import jax.numpy as jnp
from jax import lax
from jax.experimental import pallas as pl
from jax.experimental.pallas import tpu as pltpu
from jax.sharding import Mesh, PartitionSpec as P

HEAD_DIM = 64
SEG = 512
PAIR = 2 * HEAD_DIM
NEG = -1e30
EPS = 1e-12
ROOT_HALF = 0.7071067811865476
INV_ROOT_TWO_PI = 0.3989422804014327
F32 = jnp.float32
BF16 = jnp.bfloat16
VMEM_LIMIT = 60 * 1024 * 1024
TILE = 256
CHUNK = 384
MESH_IDS = pl.DeviceIdType.MESH


def mm(left, right):
    return lax.dot_general(left, right, (((1,), (0,)), ((), ())), preferred_element_type=F32)


def mm_nt(left, right):
    return lax.dot_general(left, right, (((1,), (1,)), ((), ())), preferred_element_type=F32)


def call(body, grid, pos, inputs, in_specs, out_shape, out_specs, scratch, flops, name):
    moved = sum(v.size * v.dtype.itemsize for v in inputs) + sum(
        v.size * v.dtype.itemsize for v in out_shape
    )
    return pl.pallas_call(
        body,
        grid_spec=pltpu.PrefetchScalarGridSpec(
            num_scalar_prefetch=1,
            grid=grid,
            in_specs=in_specs,
            out_specs=out_specs,
            scratch_shapes=scratch,
        ),
        out_shape=out_shape,
        compiler_params=pltpu.CompilerParams(
            dimension_semantics=("arbitrary",) * len(grid), vmem_limit_bytes=VMEM_LIMIT
        ),
        cost_estimate=pl.CostEstimate(flops=flops, bytes_accessed=moved, transcendentals=0),
        name=name,
    )(pos, *inputs)


def whole(array):
    zeros = (0,) * array.ndim
    return pl.BlockSpec(array.shape, lambda j, pos: zeros)


def shape(dims, kind):
    return jax.ShapeDtypeStruct(dims, kind)


def gelu_parts(inner):
    erf = lax.erf(inner * ROOT_HALF)
    below = 0.5 + 0.5 * erf
    density = jnp.exp(inner * inner * -0.5) * INV_ROOT_TWO_PI
    return inner * below, below + inner * density


def row_ids(info, at, places):
    bucket = info[at : at + 1, 0:1]
    span = jnp.where(bucket < 0.5, 1.0 * SEG, jnp.where(bucket < 1.5, 0.5 * SEG, 0.25 * SEG))
    row = jnp.zeros_like(places)
    size = jnp.zeros_like(places) + info[at : at + 1, 1:2]
    for slot in range(1, 4):
        later = places >= span * slot
        row = jnp.where(later, 1.0 * slot, row)
        size = jnp.where(later, info[at : at + 1, slot + 1 : slot + 2], size)
    return row, places - row * span < size


def attend_forward_body(pos_ref, x_ref, wq, wk, wv, bq, bv, info, *refs):
    (q_o, k_o, v_o, ctx_o, pa_o, pm_o, keep_o, mask_a, mask_m) = refs
    j = pl.program_id(0)
    rows = q_o.shape[0]
    half = rows - SEG

    @pl.when(j == 0)
    def _():
        for at, count, mask in ((0, SEG, mask_a), (1, half, mask_m)):
            places = lax.broadcasted_iota(jnp.int32, (SEG, 1), 0)
            across = lax.broadcasted_iota(jnp.int32, (1, count), 1)
            if at == 1:
                places = (places + half * pos_ref[1]) % SEG
                across = across + half * pos_ref[1]
            key_row, valid = row_ids(info, at, places.astype(F32))
            query_row, _ = row_ids(info, at, across.astype(F32))
            allowed = jnp.where(valid, key_row, -1.0) == query_row
            mask[...] = jnp.where(allowed, 0.0, NEG)
            keep_o[at * SEG : at * SEG + count] = jnp.where(valid[:count], 1.0, 0.0)

    w3 = jnp.concatenate([wq[...], wk[...], wv[...]], axis=1)
    qkv = mm(x_ref[...], w3)
    query = ((qkv[:rows, :PAIR] + bq[...].astype(F32)) * HEAD_DIM**-0.5).astype(BF16)
    keys = qkv[:, PAIR : 2 * PAIR].astype(BF16)
    values = (qkv[:, 2 * PAIR :] + bv[...].astype(F32)).astype(BF16)
    q_o[...] = query
    k_o[...] = keys
    v_o[...] = values
    values_t = values.astype(F32).T.astype(BF16)
    lane = lax.broadcasted_iota(jnp.int32, (1, PAIR), 1) // HEAD_DIM
    for first, count, key_first, mask, p_o in (
        (0, SEG, 0, mask_a, pa_o),
        (SEG, half, SEG, mask_m, pm_o),
    ):
        parts = []
        for h in range(2):
            query_h = jnp.where(lane == h, query[first : first + count], jnp.zeros((), BF16))
            scores = mm_nt(keys[key_first : key_first + SEG], query_h) + mask[...]
            top = jnp.max(scores, axis=0, keepdims=True)
            grown = jnp.exp(scores - top)
            probs = (grown * (1.0 / jnp.sum(grown, axis=0, keepdims=True))).astype(BF16)
            p_o[h] = probs
            parts.append(
                mm(
                    values_t[h * HEAD_DIM : (h + 1) * HEAD_DIM, key_first : key_first + SEG],
                    probs,
                )
            )
        ctx_o[first : first + count] = jnp.concatenate(parts, axis=0).T.astype(BF16)


def attend_forward(pos, x, weights, bq, bv, info, rows, name):
    total = x.shape[0]
    dim = x.shape[1]
    width = bq.shape[1]
    pairs = width // PAIR
    half = rows - SEG
    column = lambda n: pl.BlockSpec((n, PAIR), lambda j, pos: (0, j))
    inputs = [x, *weights, bq, bv, info]
    return call(
        attend_forward_body,
        (pairs,),
        pos,
        inputs,
        [whole(x), *[column(dim)] * 3, column(1), column(1), whole(info)],
        [
            shape((rows, width), BF16),
            shape((total, width), BF16),
            shape((total, width), BF16),
            shape((rows, width), BF16),
            shape((2 * pairs, SEG, SEG), BF16),
            shape((2 * pairs, SEG, half), BF16),
            shape((rows, 1), F32),
        ],
        [
            column(rows),
            column(total),
            column(total),
            column(rows),
            pl.BlockSpec((2, SEG, SEG), lambda j, pos: (j, 0, 0)),
            pl.BlockSpec((2, SEG, half), lambda j, pos: (j, 0, 0)),
            pl.BlockSpec((rows, 1), lambda j, pos: (0, 0)),
        ],
        [pltpu.VMEM((SEG, SEG), F32), pltpu.VMEM((SEG, half), F32)],
        2 * total * dim * 3 * width + 8 * 2 * SEG * rows * width,
        name,
    )


def up_body(
    pos_ref, x, ctx_i, ctx_o, wo_i, wo_o, b_out, gain, bias, wu, bu, wd,
    normed_o, inv_o, hidden_o, active_o, slope_o, branch_o,
):
    j = pl.program_id(0)
    rows = x.shape[0]

    @pl.when(j == 0)
    def _():
        for r in range(0, rows, TILE):
            at = slice(r, r + TILE)
            first = (
                x[at].astype(F32)
                + (mm(ctx_i[at], wo_i[...]) + mm(ctx_o[at], wo_o[...]))
                + b_out[...].astype(F32)
            )
            centre = first - jnp.mean(first, axis=-1, keepdims=True)
            inverse = lax.rsqrt(jnp.mean(centre * centre, axis=-1, keepdims=True) + EPS)
            normed = centre * inverse
            normed_o[at] = normed
            inv_o[at] = inverse
            hidden_o[at] = (normed * gain[...].astype(F32) + bias[...].astype(F32)).astype(BF16)

    for r in range(0, rows, TILE):
        at = slice(r, r + TILE)
        inner = mm(hidden_o[at], wu[...]) + bu[...].astype(F32)
        active, slope = gelu_parts(inner)
        active = active.astype(BF16)
        active_o[at] = active
        slope_o[at] = slope.astype(BF16)
        add = mm(active, wd[...])

        @pl.when(j == 0)
        def _():
            branch_o[at] = add

        @pl.when(j > 0)
        def _():
            branch_o[at] += add


def down_body(
    pos_ref, hidden, branch, wu, wd, bu, b_down, gain, bias, cot, keep,
    active_o, slope_o, out_o, grad_o, low_o, vec_o, acc,
):
    j = pl.program_id(0)
    rows = hidden.shape[0]

    @pl.when(j == 0)
    def _():
        acc[...] = branch[...]

    for r in range(0, rows, TILE):
        at = slice(r, r + TILE)
        inner = mm(hidden[at], wu[...]) + bu[...].astype(F32)
        active, slope = gelu_parts(inner)
        active = active.astype(BF16)
        active_o[at] = active
        slope_o[at] = slope.astype(BF16)
        acc[at] += mm(active, wd[...])

    @pl.when(j == pl.num_programs(0) - 1)
    def _():
        sums = [0.0, 0.0, 0.0]
        for r in range(0, rows, TILE):
            at = slice(r, r + TILE)
            second = hidden[at].astype(F32) + acc[at] + b_down[...].astype(F32)
            centre = second - jnp.mean(second, axis=-1, keepdims=True)
            inverse = lax.rsqrt(jnp.mean(centre * centre, axis=-1, keepdims=True) + EPS)
            normed = centre * inverse
            g = gain[...].astype(F32)
            out_o[at] = ((normed * g + bias[...].astype(F32)) * keep[at]).astype(BF16)
            upstream = cot[at].astype(F32) * keep[at]
            scaled = upstream * g
            grad = inverse * (
                scaled
                - jnp.mean(scaled, axis=-1, keepdims=True)
                - normed * jnp.mean(scaled * normed, axis=-1, keepdims=True)
            )
            grad_o[at] = grad
            low_o[at] = grad.astype(BF16)
            sums[0] += jnp.sum(upstream * normed, axis=0, keepdims=True)
            sums[1] += jnp.sum(upstream, axis=0, keepdims=True)
            sums[2] += jnp.sum(grad, axis=0, keepdims=True)
        for i, value in enumerate(sums):
            vec_o[i : i + 1] = value


def ffn_back_body(
    pos_ref, low, hidden, active, slope, wu, wd, hg_in,
    hg, send, keep, bup, low_t, hidden_t, ig, grads,
):
    j = pl.program_id(0)
    rows = low.shape[0]
    dim = low.shape[1]

    @pl.when(j == 0)
    def _():
        low_t[...] = low[...].T
        hidden_t[...] = hidden[...].T
        hg[...] = hg_in[...]

    total = 0.0
    for r in range(0, rows, TILE):
        at = slice(r, r + TILE)
        inner_grad = (mm_nt(low[at], wd[...]) * slope[at].astype(F32)).astype(BF16)
        ig[at] = inner_grad
        total += jnp.sum(inner_grad.astype(F32), axis=0, keepdims=True)
        hg[at] += mm_nt(inner_grad, wu[...])
    bup[0] = total
    for r in range(0, dim, TILE):
        grads[r : r + TILE] = mm(hidden_t[r : r + TILE], ig[...]).astype(BF16)
        grads[dim + r : dim + r + TILE] = mm(low_t[r : r + TILE], active[...]).astype(BF16)

    @pl.when(j < 2)
    def _():
        send[0] = grads[...]

    @pl.when(j >= 2)
    def _():
        keep[0] = grads[...]


def ffn_back(pos, low, hidden, active, slope, weights, hg_in, name):
    rows, dim = low.shape
    width = active.shape[1]
    quarter = width // 4
    chunk = lambda n: pl.BlockSpec((n, quarter), lambda j, pos: (0, j ^ 2))
    scratch = [
        pltpu.VMEM((dim, rows), BF16),
        pltpu.VMEM((dim, rows), BF16),
        pltpu.VMEM((rows, quarter), BF16),
        pltpu.VMEM((2 * dim, quarter), BF16),
    ]
    w_specs = [
        pl.BlockSpec((dim, quarter), lambda j, pos: (0, pos[0] ^ j ^ 2)),
        pl.BlockSpec((quarter, dim), lambda j, pos: (pos[0] ^ j ^ 2, 0)),
    ]
    piece = (2, 2 * dim, quarter)
    return call(
        ffn_back_body,
        (4,),
        pos,
        [low, hidden, active, slope, *weights, hg_in],
        [whole(low), whole(hidden), chunk(rows), chunk(rows), *w_specs, whole(hg_in)],
        [
            shape((rows, dim), F32),
            shape(piece, BF16),
            shape(piece, BF16),
            shape((4, 1, quarter), F32),
        ],
        [
            pl.BlockSpec((rows, dim), lambda j, pos: (0, 0)),
            pl.BlockSpec((1, 2 * dim, quarter), lambda j, pos: (jnp.minimum(j, 1), 0, 0)),
            pl.BlockSpec((1, 2 * dim, quarter), lambda j, pos: (jnp.maximum(j - 2, 0), 0, 0)),
            pl.BlockSpec((1, 1, quarter), lambda j, pos: (pos[0] ^ j ^ 2, 0, 0)),
        ],
        scratch,
        8 * rows * dim * width,
        name,
    )


def out_back_body(
    pos_ref, hg, normed, inv, gain, wo_i, wo_o, ctx_i, ctx_o,
    first_o, dctx_i, dctx_o, keep_i, send_i, keep_o, send_o, vec_o, low_s, low_t,
):
    rows, dim = hg.shape
    sums = [0.0, 0.0, 0.0]
    for r in range(0, rows, TILE):
        at = slice(r, r + TILE)
        grad_in = hg[at]
        n = normed[at]
        scaled = grad_in * gain[...].astype(F32)
        grad = inv[at] * (
            scaled
            - jnp.mean(scaled, axis=-1, keepdims=True)
            - n * jnp.mean(scaled * n, axis=-1, keepdims=True)
        )
        first_o[at] = grad
        low = grad.astype(BF16)
        low_s[at] = low
        dctx_i[at] = mm_nt(low, wo_i[...]).astype(BF16)
        dctx_o[at] = mm_nt(low, wo_o[...]).astype(BF16)
        sums[0] += jnp.sum(grad_in * n, axis=0, keepdims=True)
        sums[1] += jnp.sum(grad_in, axis=0, keepdims=True)
        sums[2] += jnp.sum(grad, axis=0, keepdims=True)
    for i, value in enumerate(sums):
        vec_o[i : i + 1] = value
    low_t[...] = low_s[...].T
    quarter = dim // 4
    for rel in range(4):
        row = pl.multiple_of((pos_ref[0] ^ rel) * quarter, 16)
        block = low_t[pl.ds(row, quarter), :]
        (keep_i if rel < 2 else send_i)[rel % 2] = mm(block, ctx_i[...]).astype(BF16)
        (keep_o if rel < 2 else send_o)[rel % 2] = mm(block, ctx_o[...]).astype(BF16)


def attend_back_body(
    last, pos_ref, x, q, k, v, p_a, p_m, dctx, ctx, wq, wk, wv, *refs
):
    if last:
        (tot_in, first), refs = refs[:2], refs[2:]
    gk, gs, tot, keep, send, bq, bv, x_tmp, x_t, d3 = refs
    j = pl.program_id(0)
    rows = q.shape[0]
    total, dim = x.shape
    half = rows - SEG
    quarter = dim // 4

    @pl.when(j == 0)
    def _():
        x_tmp[...] = x[...].T
        for rel in range(4):
            row = pl.multiple_of((pos_ref[0] ^ rel) * quarter, 16)
            x_t[rel * quarter : (rel + 1) * quarter] = x_tmp[pl.ds(row, quarter), :]
        if last:
            tot[...] = tot_in[...]
            tot[:rows] += first[...]
        else:
            tot[...] = jnp.zeros_like(tot)
        d3[rows:, :PAIR] = jnp.zeros((total - rows, PAIR), BF16)

    @pl.when(j < 3)
    def _():
        lane = lax.broadcasted_iota(jnp.int32, (1, PAIR), 1) // HEAD_DIM
        zero = jnp.zeros((), BF16)
        delta_t = (dctx[...].astype(F32) * ctx[...].astype(F32)).T
        keys_t = k[...].astype(F32).T.astype(BF16)
        for first_row, count, key_first, p in ((0, SEG, 0, p_a), (SEG, half, SEG, p_m)):
            at = slice(first_row, first_row + count)
            ks = slice(key_first, key_first + SEG)
            values_grad = keys_grad = 0.0
            query_parts = []
            for h in range(2):
                grad_h = jnp.where(lane == h, dctx[at], zero)
                query_h = jnp.where(lane == h, q[at], zero)
                probs = p[h]
                delta = jnp.sum(
                    delta_t[h * HEAD_DIM : (h + 1) * HEAD_DIM, at], axis=0, keepdims=True
                )
                prob_grad = mm_nt(v[ks], grad_h)
                score_grad = (probs.astype(F32) * (prob_grad - delta)).astype(BF16)
                values_grad += mm(probs, grad_h)
                keys_grad += mm(score_grad, query_h)
                query_parts.append(
                    mm(keys_t[h * HEAD_DIM : (h + 1) * HEAD_DIM, ks], score_grad)
                )
            query_grad = jnp.concatenate(query_parts, axis=0).T * HEAD_DIM**-0.5
            d3[at, :PAIR] = query_grad.astype(BF16)
            d3[ks, PAIR : 2 * PAIR] = keys_grad.astype(BF16)
            d3[ks, 2 * PAIR :] = values_grad.astype(BF16)
        bq[...] = jnp.sum(d3[:rows, :PAIR].astype(F32), axis=0, keepdims=True)
        bv[...] = jnp.sum(d3[:, 2 * PAIR :].astype(F32), axis=0, keepdims=True)
        w = jnp.concatenate([wq[...], wk[...], wv[...]], axis=1)
        tot[...] += mm_nt(d3[...], w)
        for part in range(2):
            keep[part] = mm(x_t[part * quarter : (part + 1) * quarter], d3[...]).astype(BF16)
            send[part] = mm(x_t[(part + 2) * quarter : (part + 3) * quarter], d3[...]).astype(BF16)

    @pl.when(j == 3)
    def _():
        keep[...] = gk[...]
        send[...] = gs[...]


def attend_back(pos, x, saved, dctx, weights, sums, grads, last, name):
    q, k, v, ctx, p_a, p_m = saved
    rows, width = q.shape
    total, dim = x.shape
    half = rows - SEG
    pairs = width // PAIR
    column = lambda n: pl.BlockSpec((n, PAIR), lambda j, pos: (0, jnp.minimum(j, pairs - 1)))
    plane = lambda a, b, c: pl.BlockSpec(
        (a, b, c), lambda j, pos: (jnp.minimum(j, pairs - 1), 0, 0)
    )
    out = pl.BlockSpec((2, dim // 4, 3 * PAIR), lambda j, pos: (0, j, 0))
    return call(
        functools.partial(attend_back_body, last),
        (pairs + 1,),
        pos,
        [x, q, k, v, p_a, p_m, dctx, ctx, *weights, *sums, *grads],
        [
            whole(x),
            column(rows),
            column(total),
            column(total),
            plane(2, SEG, SEG),
            plane(2, SEG, half),
            column(rows),
            column(rows),
            *[column(dim)] * 3,
            *[whole(s) for s in sums],
            *[whole(g) for g in grads],
        ],
        [
            shape((total, dim), F32),
            shape((2, dim, 3 * PAIR), BF16),
            shape((2, dim, 3 * PAIR), BF16),
            shape((1, width), F32),
            shape((1, width), F32),
        ],
        [
            pl.BlockSpec((total, dim), lambda j, pos: (0, 0)),
            out,
            out,
            column(1),
            column(1),
        ],
        [
            pltpu.VMEM((dim, total), BF16),
            pltpu.VMEM((dim, total), BF16),
            pltpu.VMEM((total, 3 * PAIR), BF16),
        ],
        2 * total * dim * 3 * width * 2 + 16 * 2 * SEG * rows * width,
        name,
    )


class Copies:
    def __init__(self, send, recv, local):
        self.send, self.recv, self.local = send, recv, local
        self.remote_count = self.local_count = 0

    def to(self, src, dst, **device):
        n = self.remote_count
        self.remote_count += 1
        return pltpu.make_async_remote_copy(
            src_ref=src,
            dst_ref=dst,
            send_sem=self.send.at[n],
            recv_sem=self.recv.at[n],
            device_id=device,
            device_id_type=MESH_IDS,
        )

    def here(self, src, dst):
        n = self.local_count
        self.local_count += 1
        return pltpu.make_async_copy(src, dst, self.local.at[n])


def coords():
    return tuple(lax.axis_index(a) for a in ("z", "x", "c", "y"))


def greet(devices):
    barrier = pltpu.get_barrier_semaphore()
    for device in devices:
        pl.semaphore_signal(barrier, inc=1, device_id=device, device_id_type=MESH_IDS)
    pl.semaphore_wait(barrier, len(devices))


def gather_body(
    tokens, cot, wq, wk, wv, wo, wu, wd, bias, info,
    x_o, cot_o, wq_o, wk_o, wv_o, wo_o, wu_o, wd_o, bias_o, info_o,
    send, recv, local, crossed,
):
    z, x, c, y = coords()
    copies = Copies(send, recv, local)
    half = tokens.shape[0] - SEG
    full = pl.ds(pl.multiple_of(y * half, half), SEG)
    mid = pl.ds(pl.multiple_of((1 - y) * SEG, half), half)
    greet([{"y": 1 - y}, {"x": 1 - x}, {"c": 1 - c}, {"c": 1 - c, "y": 1 - y}])
    same = c == y
    own, sib = pl.ds(SEG, half), pl.ds(SEG + half, half)

    x_y = copies.to(tokens.at[mid], x_o.at[sib], y=1 - y)
    cot_d = pltpu.make_async_remote_copy(
        src_ref=cot.at[mid], dst_ref=cot_o.at[own], send_sem=crossed.at[0], recv_sem=crossed.at[1],
        device_id={"c": 1 - c, "y": 1 - y}, device_id_type=MESH_IDS,
    )
    x_own = copies.here(tokens.at[mid], x_o.at[own])
    cot_own = copies.here(cot.at[mid], cot_o.at[own])
    x_c1 = copies.to(x_o.at[own], x_o.at[sib], c=1 - c)
    x_c2 = copies.to(x_o.at[sib], x_o.at[own], c=1 - c)
    small = [copies.to(bias, bias_o, y=1 - y), copies.to(info, info_o, c=1 - c)]
    bulk = [copies.here(tokens.at[full], x_o.at[pl.ds(0, SEG)]), copies.here(cot.at[full], cot_o.at[pl.ds(0, SEG)])]

    @pl.when(same)
    def _():
        x_own.start()
        cot_own.start()

    @pl.when(jnp.logical_not(same))
    def _():
        x_y.start()

    for copy in small + bulk:
        copy.start()

    def piece(array, side, x_at):
        ref, by_columns, part, parts = array[side], *array[2:]
        n = ref.shape[1 if by_columns else 0] // 4
        at = pl.ds(pl.multiple_of((2 * c + x_at) * n, 128 if by_columns else 16), n)
        if by_columns:
            m = ref.shape[0] // parts
            return ref.at[pl.ds(part * m, m), at]
        at = pl.ds(pl.multiple_of((2 * c + x_at) * n + part * (n // parts), 16), n // parts)
        return ref.at[at]

    arrays = [
        (wq, wq_o, False, 0, 1), (wk, wk_o, False, 0, 1), (wv, wv_o, False, 0, 1), (wo, wo_o, False, 0, 1),
        (wu, wu_o, True, 0, 2), (wu, wu_o, True, 1, 2), (wd, wd_o, False, 0, 2), (wd, wd_o, False, 1, 2),
    ]
    over_y = []

    def next_y():
        if len(over_y) < len(arrays):
            array = arrays[len(over_y)]
            over_y.append(copies.to(piece(array, 0, x), piece(array, 1, x), y=1 - y))
            over_y[-1].start()

    for _ in range(3):
        next_y()

    @pl.when(jnp.logical_not(same))
    def _():
        cot_d.start()

    @pl.when(same)
    def _():
        x_own.wait()
        x_y.wait_recv()
        x_c1.start()
        x_c2.start()

    over_x, over_c = [], []

    def from_x(n):
        over_x[n].wait_recv()
        theirs = piece(arrays[n], 1, 1 - x)
        over_c.append(copies.to(theirs, theirs, c=1 - c))
        over_c[-1].start()

    for n, array in enumerate(arrays):
        over_y[n].wait_recv()
        next_y()
        mine = piece(array, 1, x)
        over_x.append(copies.to(mine, mine, x=1 - x))
        over_c.append(copies.to(mine, mine, c=1 - c))
        over_x[-1].start()
        over_c[-1].start()
        if n > 0:
            from_x(n - 1)
    from_x(len(arrays) - 1)

    @pl.when(same)
    def _():
        cot_own.wait()
        x_c1.wait_send()
        x_c2.wait_send()

    @pl.when(jnp.logical_not(same))
    def _():
        x_y.wait_send()
        cot_d.wait_send()
        cot_d.wait_recv()
        x_c1.wait_recv()
        x_c2.wait_recv()

    for copy in bulk + small + over_c:
        copy.wait()
    for copy in over_y + over_x:
        copy.wait_send()


def reduce_body(
    depth, s_fo, k_fo, s_fi, k_fi, s_ao, k_ao, s_ai, k_ai, vec, total, output,
    sums_o, vec_o, in_o, out_o,
    k_e, k_i, c_e, c_i, y_r, x_r, z_r, zx_r, vec_r, mid_f, mid_b, mid_r, send, recv, local, crossed,
):
    z, x, c, y = coords()
    copies = Copies(send, recv, local)
    steps = []
    while 2 ** len(steps) < depth:
        steps.append(2 ** len(steps))
    bits = [(z // s) % 2 for s in steps]
    z_partner = [z + s - 2 * s * b for s, b in zip(steps, bits)]
    near = [{"c": 1 - c}, {"y": 1 - y}, {"x": 1 - x}] + [{"z": p} for p in z_partner]
    greet(near + [{"c": 1 - c, "y": 1 - y}])
    same = c == y
    split = min(2, len(steps))
    ffn_rows = s_fo.shape[1]
    rows = ffn_rows + s_ao.shape[1]
    half = mid_b.shape[1]
    count = rows // CHUNK
    every = []

    def at(k):
        return pl.ds(k * CHUNK, CHUNK)

    def source(ffn, att, k):
        if k * CHUNK < ffn_rows:
            return ffn.at[:, at(k)]
        return att.at[:, pl.ds(k * CHUNK - ffn_rows, CHUNK)]

    def go(copy):
        copy.start()
        every.append(copy)
        return copy

    def add(n, out, *ins):
        def step(i, _):
            rows_at = pl.ds(pl.multiple_of(i * 32, 32), 32)
            value = ins[0][rows_at].astype(F32)
            for other in ins[1:]:
                value = value + other[rows_at].astype(F32)
            out[rows_at] = value.astype(out.dtype)
            return 0

        lax.fori_loop(0, n // 32, step, 0)

    def add2(n, out, *ins):
        for part in range(2):
            add(n, out.at[part], *[v.at[part] for v in ins])

    load_e, load_i, got_e, got_i = {}, {}, {}, {}
    got_y, got_x, got_z, back_z, put, got_bx = {}, {}, {}, {}, {}, {}
    load_mid = copies.here(total.at[pl.ds(SEG, 2 * half)], mid_f)
    load_mid.start()
    for k in range(count):
        load_e[k] = copies.here(source(k_fo, k_ao, k), k_e.at[:, at(k)])
        load_i[k] = copies.here(source(k_fi, k_ai, k), k_i.at[:, at(k)])

    def over_cores(k):
        got_e[k] = go(copies.to(source(s_fo, s_ao, k), c_e.at[:, at(k)], c=1 - c))
        load_e[k].start()
        got_i[k] = go(copies.to(source(s_fi, s_ai, k), c_i.at[:, at(k)], c=1 - c))
        load_i[k].start()

    over_cores(0)
    over_cores(1)

    out_d = pltpu.make_async_remote_copy(
        src_ref=output.at[pl.ds(SEG, half)], dst_ref=out_o, send_sem=crossed.at[0], recv_sem=crossed.at[1],
        device_id={"c": 1 - c, "y": 1 - y}, device_id_type=MESH_IDS,
    )
    out_here = copies.here(output.at[pl.ds(SEG, half)], out_o)
    in_d = pltpu.make_async_remote_copy(
        src_ref=mid_b.at[1], dst_ref=mid_r.at[1], send_sem=crossed.at[2], recv_sem=crossed.at[3],
        device_id={"c": 1 - c, "y": 1 - y}, device_id_type=MESH_IDS,
    )

    @pl.when(same)
    def _():
        out_here.start()

    load_mid.wait()
    add(half, mid_b.at[0], mid_f.at[pl.ds(half, half)])
    in_c = go(copies.to(mid_b.at[0], mid_r.at[0], c=1 - c))

    links = near
    vec_copies = {}

    def vec_start(n):
        source_ref = vec if n == 0 else vec_r.at[2 * n - 1]
        vec_copies[n] = go(copies.to(source_ref, vec_r.at[2 * n], **links[n]))

    def vec_next(n):
        vec_copies[n].wait_recv()
        last = n == len(links) - 1
        before = vec if n == 0 else vec_r.at[2 * n - 1]
        value = before[...] + vec_r[2 * n]
        if last:
            vec_o[...] = value
        else:
            vec_r[2 * n + 1] = value
            vec_start(n + 1)

    def middle():
        in_c.wait_recv()
        add(half, mid_f, mid_f, mid_r.at[0])
        add(half, mid_b.at[1], mid_f)

        @pl.when(jnp.logical_not(same))
        def _():
            out_d.start()
            in_d.start()

    def to_y(k):
        load_e[k].wait()
        got_e[k].wait_recv()
        add2(CHUNK, k_e.at[:, at(k)], k_e.at[:, at(k)], c_e.at[:, at(k)])
        got_y[k] = go(copies.to(k_e.at[:, at(k)], y_r.at[:, at(k)], y=1 - y))
        if k + 2 < count:
            over_cores(k + 2)

    def to_x(k):
        load_i[k].wait()
        got_i[k].wait_recv()
        got_y[k].wait_recv()
        add2(CHUNK, k_i.at[:, at(k)], k_i.at[:, at(k)], c_i.at[:, at(k)], y_r.at[:, at(k)])
        got_x[k] = go(copies.to(k_i.at[1, at(k)], x_r.at[at(k)], x=1 - x))

    def base(k, level):
        row, size = k * CHUNK, CHUNK
        for n in range(min(level, split)):
            size //= 2
            row = row + bits[n] * size
        return row, size

    def z_slot(k, level):
        first = sum(CHUNK // 2 ** (n + 1) for n in range(level))
        size = CHUNK // 2 ** (level + 1)
        return z_r.at[k, pl.ds(first, size)], size

    def to_z(k, level):
        row, size = base(k, level)
        mine = k_i.at[0, pl.ds(pl.multiple_of(row, 16), size)]
        if level == 0:
            got_x[k].wait_recv()
            add(size, mine, mine, x_r.at[at(k)])
        else:
            got_z[k, level - 1].wait_recv()
            came = z_slot(k, level - 1)[0] if level <= split else zx_r.at[k, level - 1 - split]
            add(size, mine, mine, came)
        if level < split:
            size //= 2
            out = k_i.at[0, pl.ds(pl.multiple_of(row + (1 - bits[level]) * size, 16), size)]
            got_z[k, level] = go(copies.to(out, z_slot(k, level)[0], z=z_partner[level]))
        elif level < len(steps):
            hold = zx_r.at[k, len(steps) - split + level - split]
            add(size, hold, mine)
            got_z[k, level] = go(copies.to(hold, zx_r.at[k, level - split], z=z_partner[level]))
        else:
            place = sums_o.at[0, pl.ds(pl.multiple_of(row, 16), size)]
            put[k] = copies.here(mine, place)
            put[k].start()
            if split:
                back_z[k, split - 1] = go(copies.to(mine, place, z=z_partner[split - 1]))

    def from_z(k, level):
        if level == split - 1:
            put[k].wait()
        if split:
            back_z[k, level].wait_recv()
        if level > 0:
            row, size = base(k, level)
            place = sums_o.at[0, pl.ds(pl.multiple_of(row, 16), size)]
            back_z[k, level - 1] = go(copies.to(place, place, z=z_partner[level - 1]))
        else:
            mine = sums_o.at[0, at(k)]
            got_bx[k] = go(copies.to(mine, sums_o.at[1, at(k)], x=1 - x))
            go(copies.to(mine, sums_o.at[2, at(k)], c=1 - c))

    def from_x(k):
        got_bx[k].wait_recv()
        go(copies.to(sums_o.at[1, at(k)], sums_o.at[3, at(k)], c=1 - c))

    tasks = []
    pace = 12.5
    for k in range(count):
        clock = 5.0 + pace * max(k - 1, 0)
        tasks.append((clock, to_y, (k,)))
        clock = 5.0 + pace * (k + 1) + 2.0
        tasks.append((clock, to_x, (k,)))
        clock += 8.0
        for level in range(len(steps) + 1):
            tasks.append((clock, to_z, (k, level)))
            clock += 5.0
        for level in range(max(split, 1) - 1, -1, -1):
            tasks.append((clock, from_z, (k, level)))
            clock += 5.0
        tasks.append((clock + 3.0, from_x, (k,)))
    tasks.append((10.0, middle, ()))
    tasks.append((6.0, vec_start, (0,)))
    for n in range(len(links)):
        tasks.append((20.0 + 12.0 * n, vec_next, (n,)))
    for _, task, arguments in sorted(tasks, key=lambda t: t[0]):
        task(*arguments)

    @pl.when(same)
    def _():
        out_here.wait()
        in_o[...] = mid_f[:half]

    @pl.when(jnp.logical_not(same))
    def _():
        out_d.wait()
        in_d.wait()
        in_o[...] = mid_r[1].astype(F32)

    waited = {id(v) for group in (got_e, got_i, got_y, got_x, got_z, back_z, got_bx, vec_copies) for v in group.values()}
    waited.add(id(in_c))
    for copy in every:
        copy.wait_send()
        if id(copy) not in waited:
            copy.wait_recv()


def final_body(pos_ref, sums, total, output, in_mid, out_mid, out_o, in_o, q_o, k_o, v_o, wo_o, up_o, down_o, tmp):
    j = pl.program_id(0)
    dim = up_o.shape[0]
    quarter, width = q_o.shape
    is_mid = jnp.where(pos_ref[2] == 0, j >= 2, j == 0)

    @pl.when(is_mid)
    def _():
        out_o[...] = out_mid[...]
        in_o[...] = in_mid[...]

    @pl.when(jnp.logical_not(is_mid))
    def _():
        out_o[...] = output[...]
        in_o[...] = total[...]

    up_o[...] = sums[0, :dim].astype(F32)
    down_o[...] = sums[0, dim : 2 * dim].astype(F32).T
    for pair in range(width // PAIR):
        at = 2 * dim + pair * quarter
        for part, ref in enumerate((q_o, k_o, v_o)):
            ref[:, pair * PAIR : (pair + 1) * PAIR] = sums[
                0, at : at + quarter, part * PAIR : (part + 1) * PAIR
            ].astype(F32)
    row = pl.multiple_of((pos_ref[0] ^ j) * quarter, 16)
    at = 2 * dim + (width // PAIR) * quarter
    tmp[pl.ds(row, quarter), :] = sums[0, at : at + quarter].astype(F32)

    @pl.when(j == pl.num_programs(0) - 1)
    def _():
        wo_o[...] = tmp[...].T


def shards(
    depth,
    tokens, lengths, buckets, w_query, b_query, w_key, w_value, b_value, w_out, b_out,
    norm1_gain, norm1_bias, w_up, b_up, w_down, b_down, norm2_gain, norm2_bias, cotangent,
):
    ix, ic, iy = (lax.axis_index(a) for a in ("x", "c", "y"))
    pos = jnp.stack([2 * ic + ix, ic, iy]).astype(jnp.int32)
    rows, dim = tokens.shape
    half = rows - SEG
    width = w_query.shape[1]
    units = w_up.shape[1]
    chunk = units // 4
    any_space = pl.BlockSpec(memory_space=pl.ANY)
    in_vmem = pl.BlockSpec(memory_space=pltpu.VMEM)

    table = jnp.concatenate([buckets[:, None], lengths], axis=1).astype(F32)
    info = jnp.stack([jnp.where(iy == 0, table[0], table[2]), table[1]])
    info = jnp.pad(info, ((0, 6), (0, 123)))
    bias = jnp.concatenate([b_query, b_value, b_up]).astype(F32).reshape(-1, width)
    bias = jnp.pad(bias, ((0, -bias.shape[0] % 8), (0, 0)))
    weights = (w_query, w_key, w_value, w_out, w_up, w_down)
    x, cot, wq_o, wk_o, wv_o, wo_o, wu_o, wd_o, bias_o, info_o = pl.pallas_call(
        gather_body,
        out_shape=[
            shape((rows + half, dim), BF16),
            shape((rows, dim), BF16),
            *[shape(w.shape, BF16) for w in weights],
            shape(bias.shape, F32),
            shape(info.shape, F32),
        ],
        in_specs=[any_space] * 8 + [in_vmem] * 2,
        out_specs=[in_vmem] * 2 + [any_space] * 6 + [in_vmem] * 2,
        scratch_shapes=[
            pltpu.SemaphoreType.DMA((40,)),
            pltpu.SemaphoreType.DMA((40,)),
            pltpu.SemaphoreType.DMA((4,)),
            pltpu.SemaphoreType.DMA((2,)),
        ],
        compiler_params=pltpu.CompilerParams(collective_id=1, has_side_effects=True),
        name="gather",
    )(tokens, cotangent, *weights, bias, info)
    info = jnp.where((jnp.arange(8) == 1)[:, None] & (ic != iy), info_o, info)
    bq_o = bias_o[0:1]
    bv_o = bias_o[1:2]
    bu_o = bias_o[2 : 2 + units // width].reshape(1, units)

    own = attend_forward(
        pos, x, (w_query, w_key, w_value), b_query[None], b_value[None], info, rows, "attend_fwd_own"
    )
    other = attend_forward(pos, x, (wq_o, wk_o, wv_o), bq_o, bv_o, info, rows, "attend_fwd_other")
    keep = own[6]
    ctx_i, ctx_o = own[3], other[3]
    row_vec = lambda v: v[None]
    const = lambda *dims: pl.BlockSpec(dims, lambda j, pos: (0,) * len(dims))
    cols = pl.BlockSpec((rows, chunk), lambda j, pos: (0, j))
    up_specs = [
        pl.BlockSpec((dim, chunk), lambda j, pos: (0, pos[0] ^ j)),
        pl.BlockSpec((1, chunk), lambda j, pos: (0, pos[0] ^ j)),
        pl.BlockSpec((chunk, dim), lambda j, pos: (pos[0] ^ j, 0)),
    ]
    b_out1, g1, s1 = row_vec(b_out), row_vec(norm1_gain), row_vec(norm1_bias)
    normed1, inverse1, hidden, act_i, slope_i, branch = call(
        up_body,
        (4,),
        pos,
        [x, ctx_i, ctx_o, w_out, wo_o, b_out1, g1, s1, w_up, b_up[None], w_down],
        [
            const(rows, dim),
            *[whole(v) for v in (ctx_i, ctx_o, w_out, wo_o, b_out1, g1, s1)],
            *up_specs,
        ],
        [
            shape((rows, dim), F32),
            shape((rows, 1), F32),
            shape((rows, dim), BF16),
            shape((rows, units), BF16),
            shape((rows, units), BF16),
            shape((rows, dim), F32),
        ],
        [const(rows, dim), const(rows, 1), const(rows, dim), cols, cols, const(rows, dim)],
        [],
        2 * rows * dim * (dim + 2 * units),
        "ffn_fwd_own",
    )
    b_down1, g2, s2 = row_vec(b_down), row_vec(norm2_gain), row_vec(norm2_bias)
    act_o, slope_o, output, second, low, vec2 = call(
        down_body,
        (4,),
        pos,
        [hidden, branch, wu_o, wd_o, bu_o, b_down1, g2, s2, cot, keep],
        [
            whole(hidden),
            whole(branch),
            up_specs[0],
            up_specs[2],
            up_specs[1],
            *[whole(v) for v in (b_down1, g2, s2, cot, keep)],
        ],
        [
            shape((rows, units), BF16),
            shape((rows, units), BF16),
            shape((rows, dim), BF16),
            shape((rows, dim), F32),
            shape((rows, dim), BF16),
            shape((3, dim), F32),
        ],
        [cols, cols, const(rows, dim), const(rows, dim), const(rows, dim), const(3, dim)],
        [pltpu.VMEM((rows, dim), F32)],
        4 * rows * dim * units,
        "ffn_fwd_other",
    )

    hg, send_o, keep_o, bup_o = ffn_back(
        pos, low, hidden, act_o, slope_o, (wu_o, wd_o), second, "ffn_back_other"
    )
    hg, send_i, keep_i, bup_i = ffn_back(
        pos, low, hidden, act_i, slope_i, (w_up, w_down), hg, "ffn_back_own"
    )
    quarter = dim // 4
    part = (2, quarter, width)
    first, dctx_i, dctx_o, ko_i, so_i, ko_o, so_o, vec1 = call(
        out_back_body,
        (1,),
        pos,
        [hg, normed1, inverse1, g1, w_out, wo_o, ctx_i, ctx_o],
        [whole(v) for v in (hg, normed1, inverse1, g1, w_out, wo_o, ctx_i, ctx_o)],
        [
            shape((rows, dim), F32),
            shape((rows, width), BF16),
            shape((rows, width), BF16),
            shape(part, BF16),
            shape(part, BF16),
            shape(part, BF16),
            shape(part, BF16),
            shape((3, dim), F32),
        ],
        [
            const(rows, dim),
            const(rows, width),
            const(rows, width),
            const(*part),
            const(*part),
            const(*part),
            const(*part),
            const(3, dim),
        ],
        [pltpu.VMEM((rows, dim), BF16), pltpu.VMEM((dim, rows), BF16)],
        4 * rows * dim * dim,
        "out_back",
    )
    total, ak_o, as_o, bq_o, bv_o = attend_back(
        pos, x, other[:6], dctx_o, (wq_o, wk_o, wv_o), (), (ko_o, so_o), False, "attend_back_other"
    )
    total, ak_i, as_i, bq_i, bv_i = attend_back(
        pos, x, own[:6], dctx_i, (w_query, w_key, w_value), (total, first), (ko_i, so_i), True, "attend_back_own"
    )

    mine = jnp.concatenate([bup_i.reshape(-1), bq_i[0], bv_i[0]])
    theirs = jnp.concatenate([bup_o.reshape(-1), bq_o[0], bv_o[0]])
    vec = jnp.concatenate([jnp.where(iy == 0, mine, theirs), jnp.where(iy == 0, theirs, mine)])
    vec = jnp.concatenate([vec.reshape(-1, dim), vec1, vec2])
    vec = jnp.pad(vec, ((0, -vec.shape[0] % 8), (0, 0)))

    levels = depth.bit_length() - 1
    more = max(levels - 2, 0)
    size = 2 * dim + dim
    parts = size // CHUNK
    whole_size = (2, size, width)
    sums, vec, in_mid, out_mid = pl.pallas_call(
        functools.partial(reduce_body, depth),
        out_shape=[
            shape((4, size, width), BF16),
            shape(vec.shape, F32),
            shape((half, dim), F32),
            shape((half, dim), BF16),
        ],
        in_specs=[any_space] * 8 + [in_vmem] + [any_space] * 2,
        out_specs=[any_space, in_vmem, in_vmem, in_vmem],
        scratch_shapes=[
            *[pltpu.VMEM(whole_size, BF16)] * 5,
            pltpu.VMEM((size, width), BF16),
            pltpu.VMEM((parts, CHUNK, width), BF16),
            pltpu.VMEM((parts, max(2 * more, 1), CHUNK // 4, width), BF16),
            pltpu.VMEM((2 * (levels + 3), *vec.shape), F32),
            pltpu.VMEM((2 * half, dim), F32),
            pltpu.VMEM((2, half, dim), BF16),
            pltpu.VMEM((2, half, dim), BF16),
            pltpu.SemaphoreType.DMA((16 + parts * (10 + levels),)),
            pltpu.SemaphoreType.DMA((16 + parts * (10 + levels),)),
            pltpu.SemaphoreType.DMA((4 + 3 * parts,)),
            pltpu.SemaphoreType.DMA((4,)),
        ],
        compiler_params=pltpu.CompilerParams(
            collective_id=2, has_side_effects=True, vmem_limit_bytes=VMEM_LIMIT
        ),
        name="reduce",
    )(send_o, keep_o, send_i, keep_i, as_o, ak_o, as_i, ak_i, vec, total, output)

    own_vec = lax.dynamic_slice_in_dim(vec[: 2 * (units + 2 * width) // dim].reshape(2, -1), iy, 1)[0]
    rest = vec[2 * (units + 2 * width) // dim :]
    full_block = lambda j, pos: (jnp.where(pos[2] == 0, jnp.minimum(j, 1), jnp.clip(j - 1, 0, 1)), 0)
    row_block = pl.BlockSpec((half, dim), lambda j, pos: (jnp.minimum(j, 2), 0))
    by_rows = lambda n, m: pl.BlockSpec((n, m), lambda j, pos: (pos[0] ^ j, 0))
    output, input_grad, w_query_grad, w_key_grad, w_value_grad, w_out_grad, w_up_grad, w_down_grad = call(
        final_body,
        (4,),
        pos,
        [sums, total, output, in_mid, out_mid],
        [
            pl.BlockSpec((1, size, width), lambda j, pos: (j, 0, 0)),
            pl.BlockSpec((half, dim), full_block),
            pl.BlockSpec((half, dim), full_block),
            whole(in_mid),
            whole(out_mid),
        ],
        [
            shape((rows, dim), BF16),
            shape((rows, dim), F32),
            *[shape((dim, width), F32)] * 3,
            shape((width, dim), F32),
            shape((dim, units), F32),
            shape((units, dim), F32),
        ],
        [
            row_block,
            row_block,
            *[by_rows(quarter, width)] * 3,
            const(width, dim),
            pl.BlockSpec((dim, chunk), lambda j, pos: (0, pos[0] ^ j)),
            by_rows(chunk, dim),
        ],
        [pltpu.VMEM((dim, width), F32)],
        0,
        "final",
    )
    return (
        output,
        input_grad,
        w_query_grad,
        own_vec[units : units + width],
        w_key_grad,
        w_value_grad,
        own_vec[units + width :],
        w_out_grad,
        rest[2],
        rest[0],
        rest[1],
        w_up_grad,
        own_vec[:units],
        w_down_grad,
        rest[5],
        rest[3],
        rest[4],
    )


def solution(mesh):
    depth = mesh.shape["dp"] // 4
    inner = Mesh(mesh.devices.reshape(depth, 2, 2, mesh.shape["mp"]), ("z", "x", "c", "y"))
    dp = ("z", "x", "c")
    every = (*dp, "y")
    placed = (
        P(every, None),
        P(dp, None),
        P(dp),
        P(None, "y"),
        P("y"),
        P(None, "y"),
        P(None, "y"),
        P("y"),
        P("y", None),
        P(),
        P(),
        P(),
        P(None, "y"),
        P("y"),
        P("y", None),
        P(),
        P(),
        P(),
        P(every, None),
    )
    return jax.shard_map(
        functools.partial(shards, depth),
        mesh=inner,
        in_specs=placed,
        out_specs=(
            P(every, None),
            P(every, None),
            P(None, "y"),
            P("y"),
            P(None, "y"),
            P(None, "y"),
            P("y"),
            P("y", None),
            P(),
            P(),
            P(),
            P(None, "y"),
            P("y"),
            P("y", None),
            P(),
            P(),
            P(),
        ),
        check_vma=False,
    )
```

```python
import functools

import jax
import jax.numpy as jnp
from jax import lax
from jax.experimental import pallas as pl
from jax.experimental.pallas import tpu as pltpu
from jax.sharding import Mesh, PartitionSpec as P

HEAD_DIM = 64
SEG = 512
PAIR = 2 * HEAD_DIM
NEG = -1e30
EPS = 1e-12
ROOT_HALF = 0.7071067811865476
INV_ROOT_TWO_PI = 0.3989422804014327
F32 = jnp.float32
BF16 = jnp.bfloat16
VMEM_LIMIT = 60 * 1024 * 1024
TILE = 256
CHUNK = 384
MESH_IDS = pl.DeviceIdType.MESH


def mm(left, right):
    return lax.dot_general(left, right, (((1,), (0,)), ((), ())), preferred_element_type=F32)


def mm_nt(left, right):
    return lax.dot_general(left, right, (((1,), (1,)), ((), ())), preferred_element_type=F32)


def mm_tn(left, right):
    return lax.dot_general(left, right, (((0,), (0,)), ((), ())), preferred_element_type=F32)


def call(body, grid, pos, inputs, in_specs, out_shape, out_specs, scratch, flops, name):
    moved = sum(v.size * v.dtype.itemsize for v in inputs) + sum(
        v.size * v.dtype.itemsize for v in out_shape
    )
    return pl.pallas_call(
        body,
        grid_spec=pltpu.PrefetchScalarGridSpec(
            num_scalar_prefetch=1,
            grid=grid,
            in_specs=in_specs,
            out_specs=out_specs,
            scratch_shapes=scratch,
        ),
        out_shape=out_shape,
        compiler_params=pltpu.CompilerParams(
            dimension_semantics=("arbitrary",) * len(grid), vmem_limit_bytes=VMEM_LIMIT
        ),
        cost_estimate=pl.CostEstimate(flops=flops, bytes_accessed=moved, transcendentals=0),
        name=name,
    )(pos, *inputs)


def whole(array):
    zeros = (0,) * array.ndim
    return pl.BlockSpec(array.shape, lambda j, pos: zeros)


def shape(dims, kind):
    return jax.ShapeDtypeStruct(dims, kind)


def gelu_parts(inner):
    erf = lax.erf(inner * ROOT_HALF)
    below = 0.5 + 0.5 * erf
    density = jnp.exp(inner * inner * -0.5) * INV_ROOT_TWO_PI
    return inner * below, below + inner * density


def row_ids(info, at, places):
    bucket = info[at : at + 1, 0:1]
    span = jnp.where(bucket < 0.5, 1.0 * SEG, jnp.where(bucket < 1.5, 0.5 * SEG, 0.25 * SEG))
    row = jnp.zeros_like(places)
    size = jnp.zeros_like(places) + info[at : at + 1, 1:2]
    for slot in range(1, 4):
        later = places >= span * slot
        row = jnp.where(later, 1.0 * slot, row)
        size = jnp.where(later, info[at : at + 1, slot + 1 : slot + 2], size)
    return row, places - row * span < size


def attend_forward_body(pos_ref, x_ref, wq, wk, wv, bq, bv, info, *refs):
    (q_o, k_o, v_o, ctx_o, pa_o, pm_o, keep_o, mask_a, mask_m) = refs
    j = pl.program_id(0)
    rows = q_o.shape[0]
    half = rows - SEG

    @pl.when(j == 0)
    def _():
        for at, count, mask in ((0, SEG, mask_a), (1, half, mask_m)):
            places = lax.broadcasted_iota(jnp.int32, (SEG, 1), 0)
            across = lax.broadcasted_iota(jnp.int32, (1, count), 1)
            if at == 1:
                places = (places + half * pos_ref[1]) % SEG
                across = across + half * pos_ref[1]
            key_row, valid = row_ids(info, at, places.astype(F32))
            query_row, _ = row_ids(info, at, across.astype(F32))
            allowed = jnp.where(valid, key_row, -1.0) == query_row
            mask[...] = jnp.where(allowed, 0.0, NEG)
            keep_o[at * SEG : at * SEG + count] = jnp.where(valid[:count], 1.0, 0.0)

    w3 = jnp.concatenate([wq[...], wk[...], wv[...]], axis=1)
    qkv = mm(x_ref[...], w3)
    query = ((qkv[:rows, :PAIR] + bq[...].astype(F32)) * HEAD_DIM**-0.5).astype(BF16)
    keys = qkv[:, PAIR : 2 * PAIR].astype(BF16)
    values = (qkv[:, 2 * PAIR :] + bv[...].astype(F32)).astype(BF16)
    q_o[...] = query
    k_o[...] = keys
    v_o[...] = values
    values_t = values.astype(F32).T.astype(BF16)
    lane = lax.broadcasted_iota(jnp.int32, (1, PAIR), 1) // HEAD_DIM
    for first, count, key_first, mask, p_o in (
        (0, SEG, 0, mask_a, pa_o),
        (SEG, half, SEG, mask_m, pm_o),
    ):
        parts = []
        for h in range(2):
            query_h = jnp.where(lane == h, query[first : first + count], jnp.zeros((), BF16))
            scores = mm_nt(keys[key_first : key_first + SEG], query_h) + mask[...]
            top = jnp.max(scores, axis=0, keepdims=True)
            grown = jnp.exp(scores - top)
            probs = (grown * (1.0 / jnp.sum(grown, axis=0, keepdims=True))).astype(BF16)
            p_o[h] = probs
            parts.append(
                mm(
                    values_t[h * HEAD_DIM : (h + 1) * HEAD_DIM, key_first : key_first + SEG],
                    probs,
                )
            )
        ctx_o[first : first + count] = jnp.concatenate(parts, axis=0).T.astype(BF16)


def attend_forward(pos, x, weights, bq, bv, info, rows, name):
    total = x.shape[0]
    dim = x.shape[1]
    width = bq.shape[1]
    pairs = width // PAIR
    half = rows - SEG
    column = lambda n: pl.BlockSpec((n, PAIR), lambda j, pos: (0, j))
    inputs = [x, *weights, bq, bv, info]
    return call(
        attend_forward_body,
        (pairs,),
        pos,
        inputs,
        [whole(x), *[column(dim)] * 3, column(1), column(1), whole(info)],
        [
            shape((rows, width), BF16),
            shape((total, width), BF16),
            shape((total, width), BF16),
            shape((rows, width), BF16),
            shape((2 * pairs, SEG, SEG), BF16),
            shape((2 * pairs, SEG, half), BF16),
            shape((rows, 1), F32),
        ],
        [
            column(rows),
            column(total),
            column(total),
            column(rows),
            pl.BlockSpec((2, SEG, SEG), lambda j, pos: (j, 0, 0)),
            pl.BlockSpec((2, SEG, half), lambda j, pos: (j, 0, 0)),
            pl.BlockSpec((rows, 1), lambda j, pos: (0, 0)),
        ],
        [pltpu.VMEM((SEG, SEG), F32), pltpu.VMEM((SEG, half), F32)],
        2 * total * dim * 3 * width + 8 * 2 * SEG * rows * width,
        name,
    )


def up_body(
    pos_ref, x, ctx_i, ctx_o, wo_i, wo_o, b_out, gain, bias, wu, bu, wd,
    normed_o, inv_o, hidden_o, active_o, slope_o, branch_o,
):
    j = pl.program_id(0)
    rows = x.shape[0]

    @pl.when(j == 0)
    def _():
        for r in range(0, rows, TILE):
            at = slice(r, r + TILE)
            first = (
                x[at].astype(F32)
                + (mm(ctx_i[at], wo_i[...]) + mm(ctx_o[at], wo_o[...]))
                + b_out[...].astype(F32)
            )
            centre = first - jnp.mean(first, axis=-1, keepdims=True)
            inverse = lax.rsqrt(jnp.mean(centre * centre, axis=-1, keepdims=True) + EPS)
            normed = centre * inverse
            normed_o[at] = normed.astype(BF16)
            inv_o[at] = inverse
            hidden_o[at] = (normed * gain[...].astype(F32) + bias[...].astype(F32)).astype(BF16)

    for r in range(0, rows, TILE):
        at = slice(r, r + TILE)
        inner = mm(hidden_o[at], wu[...]) + bu[...].astype(F32)
        active, slope = gelu_parts(inner)
        active = active.astype(BF16)
        active_o[at] = active
        slope_o[at] = slope.astype(BF16)
        add = mm(active, wd[...])

        @pl.when(j == 0)
        def _():
            branch_o[at] = add

        @pl.when(j > 0)
        def _():
            branch_o[at] += add


def down_body(
    pos_ref, hidden, branch, wu, wd, bu, b_down, gain, bias, cot, keep,
    active_o, slope_o, out_o, grad_o, low_o, vec_o, acc,
):
    j = pl.program_id(0)
    rows = hidden.shape[0]

    @pl.when(j == 0)
    def _():
        acc[...] = branch[...]

    for r in range(0, rows, TILE):
        at = slice(r, r + TILE)
        inner = mm(hidden[at], wu[...]) + bu[...].astype(F32)
        active, slope = gelu_parts(inner)
        active = active.astype(BF16)
        active_o[at] = active
        slope_o[at] = slope.astype(BF16)
        acc[at] += mm(active, wd[...])

    @pl.when(j == pl.num_programs(0) - 1)
    def _():
        sums = [0.0, 0.0, 0.0]
        for r in range(0, rows, TILE):
            at = slice(r, r + TILE)
            second = hidden[at].astype(F32) + acc[at] + b_down[...].astype(F32)
            centre = second - jnp.mean(second, axis=-1, keepdims=True)
            inverse = lax.rsqrt(jnp.mean(centre * centre, axis=-1, keepdims=True) + EPS)
            normed = centre * inverse
            g = gain[...].astype(F32)
            out_o[at] = ((normed * g + bias[...].astype(F32)) * keep[at]).astype(BF16)
            upstream = cot[at].astype(F32) * keep[at]
            scaled = upstream * g
            grad = inverse * (
                scaled
                - jnp.mean(scaled, axis=-1, keepdims=True)
                - normed * jnp.mean(scaled * normed, axis=-1, keepdims=True)
            )
            grad_o[at] = grad
            low_o[at] = grad.astype(BF16)
            sums[0] += jnp.sum(upstream * normed, axis=0, keepdims=True)
            sums[1] += jnp.sum(upstream, axis=0, keepdims=True)
            sums[2] += jnp.sum(grad, axis=0, keepdims=True)
        for i, value in enumerate(sums):
            vec_o[i : i + 1] = value


class Copies:
    def __init__(self, send, recv, local):
        self.send, self.recv, self.local = send, recv, local
        self.remote_count = self.local_count = 0

    def to(self, src, dst, **device):
        n = self.remote_count
        self.remote_count += 1
        return pltpu.make_async_remote_copy(
            src_ref=src,
            dst_ref=dst,
            send_sem=self.send.at[n],
            recv_sem=self.recv.at[n],
            device_id=device,
            device_id_type=MESH_IDS,
        )

    def here(self, src, dst):
        n = self.local_count
        self.local_count += 1
        return pltpu.make_async_copy(src, dst, self.local.at[n])


def coords():
    return tuple(lax.axis_index(a) for a in ("z", "x", "c", "y"))


def greet(devices):
    barrier = pltpu.get_barrier_semaphore()
    for device in devices:
        pl.semaphore_signal(barrier, inc=1, device_id=device, device_id_type=MESH_IDS)
    pl.semaphore_wait(barrier, len(devices))


def gather_body(
    tokens, cot, wq, wk, wv, wo, wu, wd, bias, info,
    x_o, cot_o, wq_o, wk_o, wv_o, wo_o, wu_o, wd_o, bias_o, info_o,
    send, recv, local, crossed,
):
    z, x, c, y = coords()
    copies = Copies(send, recv, local)
    half = tokens.shape[0] - SEG
    full = pl.ds(pl.multiple_of(y * half, half), SEG)
    mid = pl.ds(pl.multiple_of((1 - y) * SEG, half), half)
    greet([{"y": 1 - y}, {"x": 1 - x}, {"c": 1 - c}, {"c": 1 - c, "y": 1 - y}])
    same = c == y
    own, sib = pl.ds(SEG, half), pl.ds(SEG + half, half)

    x_y = copies.to(tokens.at[mid], x_o.at[sib], y=1 - y)
    cot_d = pltpu.make_async_remote_copy(
        src_ref=cot.at[mid], dst_ref=cot_o.at[own], send_sem=crossed.at[0], recv_sem=crossed.at[1],
        device_id={"c": 1 - c, "y": 1 - y}, device_id_type=MESH_IDS,
    )
    x_own = copies.here(tokens.at[mid], x_o.at[own])
    cot_own = copies.here(cot.at[mid], cot_o.at[own])
    x_c1 = copies.to(x_o.at[own], x_o.at[sib], c=1 - c)
    x_c2 = copies.to(x_o.at[sib], x_o.at[own], c=1 - c)
    small = [copies.to(bias, bias_o, y=1 - y), copies.to(info, info_o, c=1 - c)]
    bulk = [copies.here(tokens.at[full], x_o.at[pl.ds(0, SEG)]), copies.here(cot.at[full], cot_o.at[pl.ds(0, SEG)])]

    @pl.when(same)
    def _():
        x_own.start()
        cot_own.start()

    @pl.when(jnp.logical_not(same))
    def _():
        x_y.start()

    for copy in small + bulk:
        copy.start()

    def piece(array, side, x_at):
        ref, by_columns, part, parts = array[side], *array[2:]
        n = ref.shape[1 if by_columns else 0] // 4
        at = pl.ds(pl.multiple_of((2 * c + x_at) * n, 128 if by_columns else 16), n)
        if by_columns:
            m = ref.shape[0] // parts
            return ref.at[pl.ds(part * m, m), at]
        at = pl.ds(pl.multiple_of((2 * c + x_at) * n + part * (n // parts), 16), n // parts)
        return ref.at[at]

    arrays = [
        (wq, wq_o, False, 0, 1), (wk, wk_o, False, 0, 1), (wv, wv_o, False, 0, 1), (wo, wo_o, False, 0, 1),
        (wu, wu_o, True, 0, 2), (wu, wu_o, True, 1, 2), (wd, wd_o, False, 0, 2), (wd, wd_o, False, 1, 2),
    ]
    over_y = []

    def next_y():
        if len(over_y) < len(arrays):
            array = arrays[len(over_y)]
            over_y.append(copies.to(piece(array, 0, x), piece(array, 1, x), y=1 - y))
            over_y[-1].start()

    for _ in range(3):
        next_y()

    @pl.when(jnp.logical_not(same))
    def _():
        cot_d.start()

    @pl.when(same)
    def _():
        x_own.wait()
        x_y.wait_recv()
        x_c1.start()
        x_c2.start()

    over_x, over_c = [], []

    def from_x(n):
        over_x[n].wait_recv()
        theirs = piece(arrays[n], 1, 1 - x)
        over_c.append(copies.to(theirs, theirs, c=1 - c))
        over_c[-1].start()

    for n, array in enumerate(arrays):
        over_y[n].wait_recv()
        next_y()
        mine = piece(array, 1, x)
        over_x.append(copies.to(mine, mine, x=1 - x))
        over_c.append(copies.to(mine, mine, c=1 - c))
        over_x[-1].start()
        over_c[-1].start()
        if n > 0:
            from_x(n - 1)
    from_x(len(arrays) - 1)

    @pl.when(same)
    def _():
        cot_own.wait()
        x_c1.wait_send()
        x_c2.wait_send()

    @pl.when(jnp.logical_not(same))
    def _():
        x_y.wait_send()
        cot_d.wait_send()
        cot_d.wait_recv()
        x_c1.wait_recv()
        x_c2.wait_recv()

    for copy in bulk + small + over_c:
        copy.wait()
    for copy in over_y + over_x:
        copy.wait_send()


def plan(parts, levels, split, ready_e, ready_i):
    free = {"y": 0.0, "x": 0.0, "z": 0.0}
    order = []
    waiting = [(ready_e[k], n, k, ("y",)) for n, k in enumerate(parts)]
    done_y = {}

    def send(link, now, us):
        start = max(now, free[link])
        free[link] = start + us
        return start + us + 2.0

    while waiting:
        waiting.sort()
        now, n, k, stage = waiting.pop(0)
        us = parts[k] * 12.4 / CHUNK
        name = stage[0]
        link = {"y": "y", "x": "x", "fx": None}.get(name, "z")
        if name == "fz" and stage[1] == 0:
            link = "x"
        if link and free[link] > now + 2.5:
            waiting.append((free[link] - 2.0, n, k, stage))
            continue
        order.append((now, stage, k))
        if name == "y":
            waiting.append((max(send("y", now, us), ready_i[k]), n, k, ("x",)))
        elif name == "x":
            waiting.append((send("x", now, us / 2), n, k, ("z", 0)))
        elif name == "z":
            level = stage[1]
            if level < levels:
                waiting.append((send("z", now, us / 4), n, k, ("z", level + 1)))
            elif split:
                waiting.append((send("z", now, us / 4), n, k, ("fz", split - 1)))
            else:
                waiting.append((now, n, k, ("fz", 0)))
        elif name == "fz":
            if stage[1] > 0:
                waiting.append((send("z", now, us / 4), n, k, ("fz", stage[1] - 1)))
            else:
                waiting.append((send("x", now, us / 2), n, k, ("fx",)))
    return order


def backward_body(
    depth,
    low_h, hidden_h, act_i, act_o, slope_i, slope_o, wu_i, wu_o, wd_i, wd_o, second_h, normed_h, inv_h,
    wo_i, wo_o, ctx_h, x_h, q_h, k_h, v_h, pa_h, pm_h, wq_i, wk_i, wv_i, wq_o, wk_o, wv_o, output_h, gain, vec2,
    sums_o, top_o, vec_o, in_o, out_o,
    low, hidden, slots, total, b_e, b_i, c_e, c_i, y_r, x_r, z_a, z_b, zx_r, normed, inv, wo, ctx, dctx, x_s,
    p_a, p_m, d3, vecs, vec_r, mid_b, mid_r, send, recv, local, crossed,
):
    z, x, c, y = coords()
    copies = Copies(send, recv, local)
    steps = []
    while 2 ** len(steps) < depth:
        steps.append(2 ** len(steps))
    levels = len(steps)
    split = min(2, levels)
    bits = [(z // s) % 2 for s in steps]
    z_partner = [z + s - 2 * s * b for s, b in zip(steps, bits)]
    near = [{"c": 1 - c}, {"y": 1 - y}, {"x": 1 - x}] + [{"z": p} for p in z_partner]
    same = c == y
    rows, dim = low.shape
    half = rows - SEG
    width = b_e.shape[2]
    quarter = dim // 4
    ffn_rows = 2 * dim
    first_row, parts = {}, {}
    att_at = ffn_rows // CHUNK
    for n in range(att_at):
        first_row[n], parts[n] = n * CHUNK, CHUNK
    for n in range(4):
        first_row[att_at + n], parts[att_at + n] = ffn_rows + n * quarter, quarter
    every, waited = [], set()

    def at(k):
        return pl.ds(first_row[k], parts[k])

    def go(copy):
        copy.start()
        every.append(copy)
        return copy

    def arrived(copy):
        copy.wait_recv()
        waited.add(id(copy))

    loads = {}

    def load(name, *pairs):
        loads[name] = [copies.here(src, dst) for src, dst in pairs]
        for copy in loads[name]:
            copy.start()

    def loaded(name):
        for copy in loads.pop(name, ()):
            copy.wait()

    chunks = [(False, 1 - c), (False, c), (True, 1 - c), (True, c)]

    def load_ffn(n):
        own, h = chunks[n]
        s = n % 2
        cut = pl.ds(pl.multiple_of(h * dim, 128), dim)
        load(
            ("ffn", n),
            ((wd_i if own else wd_o).at[cut], slots.at[2 + s]),
            ((slope_i if own else slope_o).at[:, cut], slots.at[6 + s]),
            ((wu_i if own else wu_o).at[:, cut], slots.at[s]),
            ((act_i if own else act_o).at[:, cut], slots.at[4 + s]),
        )

    load("low", (low_h, low))
    load_ffn(0)
    load("second", (second_h, total.at[pl.ds(0, rows)]), (hidden_h, hidden))
    load_ffn(1)
    greet(near + [{"c": 1 - c, "y": 1 - y}])

    out_d = pltpu.make_async_remote_copy(
        src_ref=output_h.at[pl.ds(SEG, half)], dst_ref=out_o, send_sem=crossed.at[0], recv_sem=crossed.at[1],
        device_id={"c": 1 - c, "y": 1 - y}, device_id_type=MESH_IDS,
    )
    in_d = pltpu.make_async_remote_copy(
        src_ref=mid_b.at[1], dst_ref=mid_r.at[1], send_sem=crossed.at[2], recv_sem=crossed.at[3],
        device_id={"c": 1 - c, "y": 1 - y}, device_id_type=MESH_IDS,
    )
    out_here = copies.here(output_h.at[pl.ds(SEG, half)], out_o)

    @pl.when(same)
    def _():
        out_here.start()

    @pl.when(jnp.logical_not(same))
    def _():
        out_d.start()

    load("mid", (wo_i, wo.at[pl.ds(0, width)]), (wo_o, wo.at[pl.ds(width, width)]), (ctx_h, ctx), (normed_h, normed), (inv_h, inv), (x_h, x_s))

    def add(n, out, *ins):
        def step(i, _):
            rows_at = pl.ds(pl.multiple_of(i * 48, 16), 48)
            value = ins[0][rows_at].astype(F32)
            for other in ins[1:]:
                value = value + other[rows_at].astype(F32)
            out[rows_at] = value.astype(out.dtype)
            return 0

        lax.fori_loop(0, n // 48, step, 0)

    def add2(n, out, *ins):
        for part in range(2):
            add(n, out.at[part], *[v.at[part] for v in ins])

    got_e, got_i, got_y, got_x, got_z, back_z, put, got_bx = {}, {}, {}, {}, {}, {}, {}, {}

    def cores(own, k):
        buf, there, got = (b_i, c_i, got_i) if own else (b_e, c_e, got_e)
        got[k] = go(copies.to(buf.at[pl.ds(2, 2), at(k)], there.at[:, at(k)], c=1 - c))

    def to_y(k):
        arrived(got_e[k])
        mine = b_e.at[pl.ds(0, 2), at(k)]
        add2(parts[k], mine, mine, c_e.at[:, at(k)])
        got_y[k] = go(copies.to(mine, y_r.at[:, at(k)], y=1 - y))

    def to_x(k):
        arrived(got_i[k])
        arrived(got_y[k])
        mine = b_i.at[pl.ds(0, 2), at(k)]
        add2(parts[k], mine, mine, c_i.at[:, at(k)], y_r.at[:, at(k)])
        got_x[k] = go(copies.to(b_i.at[1, at(k)], x_r.at[at(k)], x=1 - x))

    def base(k, level):
        row, size = first_row[k], parts[k]
        for n in range(min(level, split)):
            size //= 2
            row = row + bits[n] * size
        return row, size

    def slot(k, level):
        cut = 2 ** (level + 1)
        return (z_a, z_b)[level].at[pl.ds(first_row[k] // cut, parts[k] // cut)]

    def extra(k, n):
        return zx_r.at[n, pl.ds(first_row[k] // 4, parts[k] // 4)]

    def to_z(k, level):
        row, size = base(k, level)
        mine = b_i.at[0, pl.ds(pl.multiple_of(row, 16), size)]
        if level == 0:
            arrived(got_x[k])
            add(size, mine, mine, x_r.at[at(k)])
        else:
            if level > split:
                got_z[k, level - 1].wait()
            else:
                arrived(got_z[k, level - 1])
            add(size, mine, mine, slot(k, level - 1) if level <= split else extra(k, level - 1 - split))
        if level < split:
            size //= 2
            out = b_i.at[0, pl.ds(pl.multiple_of(row + (1 - bits[level]) * size, 16), size)]
            got_z[k, level] = go(copies.to(out, slot(k, level), z=z_partner[level]))
        elif level < levels:
            got_z[k, level] = copies.to(mine, extra(k, level - split), z=z_partner[level])
            got_z[k, level].start()
        else:
            place = sums_o.at[0, pl.ds(pl.multiple_of(row, 16), size)]
            put[k] = copies.here(mine, place)
            put[k].start()
            if split:
                back_z[k, split - 1] = go(copies.to(mine, place, z=z_partner[split - 1]))

    def from_z(k, level):
        if level == max(split, 1) - 1:
            put[k].wait()
        if split:
            arrived(back_z[k, level])
        if level > 0:
            row, size = base(k, level)
            place = sums_o.at[0, pl.ds(pl.multiple_of(row, 16), size)]
            back_z[k, level - 1] = go(copies.to(place, place, z=z_partner[level - 1]))
        else:
            mine = sums_o.at[0, at(k)]
            got_bx[k] = go(copies.to(mine, sums_o.at[1, at(k)], x=1 - x))
            go(copies.to(mine, sums_o.at[2, at(k)], c=1 - c))

    def from_x(k):
        arrived(got_bx[k])
        go(copies.to(sums_o.at[1, at(k)], sums_o.at[3, at(k)], c=1 - c))

    vec_copies = {}

    def vec_start(n):
        source = vecs if n == 0 else vec_r.at[2 * n - 1]
        vec_copies[n] = go(copies.to(source, vec_r.at[2 * n], **near[n]))

    def vec_next(n):
        arrived(vec_copies[n])
        value = (vecs if n == 0 else vec_r.at[2 * n - 1])[...] + vec_r[2 * n]
        if n == len(near) - 1:
            vec_o[...] = value
        else:
            vec_r[2 * n + 1] = value
            vec_start(n + 1)

    work = []

    def step(us, body, *arguments):
        work.append((us, body, arguments))

    def put_columns(buf, row, grads, keep):
        for part in range(2):
            rel = (0 if keep else 2) + (part + x) % 2
            buf[rel, row : row + dim] = grads[:, part * width : (part + 1) * width]

    def put_rows(buf, group, grads):
        for p in range(4):
            rel = 2 * ((p // 2 + c) % 2) + (p % 2 + x) % 2
            buf[rel, ffn_rows + group * quarter : ffn_rows + (group + 1) * quarter] = grads[
                p * quarter : (p + 1) * quarter
            ]

    def inner_grad(n):
        own, h = chunks[n]
        if n == 0:
            loaded("low")
        loaded(("ffn", n))
        s = n % 2
        grad = (mm_nt(low[...], slots[2 + s]) * slots[6 + s].astype(F32)).astype(BF16)
        d3[:rows, :dim] = grad
        bias = jnp.sum(grad.astype(F32), axis=0, keepdims=True)
        for part in range(2):
            row = 4 * (y if own else 1 - y) + 2 * h + part
            vecs[pl.ds(row, 1)] = bias[:, part * width : (part + 1) * width]

    def hidden_grad(n):
        if n == 0:
            loaded("second")
        total[:rows] += mm_nt(d3[:rows, :dim], slots[n % 2])

    def up_grad(n):
        own = chunks[n][0]
        put_columns(b_i if own else b_e, 0, mm_tn(hidden[...], d3[:rows, :dim]).astype(BF16), n % 2 == 1)
        if n % 2 == 0:
            cores(own, 0)
            cores(own, 1)

    def down_grad(n):
        own = chunks[n][0]
        put_columns(b_i if own else b_e, dim, mm_tn(low[...], slots[4 + n % 2]).astype(BF16), n % 2 == 1)
        if n % 2 == 0:
            cores(own, 2)
            cores(own, 3)
        if n < 2:
            load_ffn(n + 2)
        elif n == 2:
            load(
                "att0",
                (q_h, slots.at[0]),
                (k_h.at[pl.ds(0, SEG)], slots.at[2, pl.ds(0, SEG)]),
                (k_h.at[pl.ds(SEG, SEG)], slots.at[4, pl.ds(0, SEG)]),
                (v_h.at[pl.ds(0, SEG)], slots.at[6, pl.ds(0, SEG)]),
            )
            load_probs(0)
            load_probs(1)
        else:
            left, right = pl.ds(0, width), pl.ds(width, width)
            load(
                "att1",
                (v_h.at[pl.ds(SEG, SEG)], slots.at[1, pl.ds(0, SEG)]),
                (wq_i, slots.at[3, :, left]),
                (wk_i, slots.at[3, :, right]),
                (wv_i, slots.at[5, :, left]),
                (wv_o, slots.at[5, :, right]),
                (wq_o, slots.at[7, :, left]),
                (wk_o, slots.at[7, :, right]),
            )

    pairs = width // PAIR
    pair_order = [pairs + n for n in range(pairs)] + list(range(pairs))

    def load_probs(n):
        pair = pair_order[n]
        load(
            ("p", n),
            (pa_h.at[pl.ds(2 * pair, 2)], p_a.at[n % 2]),
            (pm_h.at[pl.ds(2 * pair, 2)], p_m.at[n % 2]),
        )

    def out_back():
        loaded("mid")
        sums = [0.0, 0.0, 0.0]
        for r in range(0, rows, TILE):
            tile = slice(r, r + TILE)
            grad_in = total[tile]
            n = normed[tile].astype(F32)
            scaled = grad_in * gain[...].astype(F32)
            grad = inv[tile] * (
                scaled
                - jnp.mean(scaled, axis=-1, keepdims=True)
                - n * jnp.mean(scaled * n, axis=-1, keepdims=True)
            )
            sums[0] += jnp.sum(grad_in * n, axis=0, keepdims=True)
            sums[1] += jnp.sum(grad_in, axis=0, keepdims=True)
            sums[2] += jnp.sum(grad, axis=0, keepdims=True)
            total[tile] = grad
            low[tile] = grad.astype(BF16)
        for i, value in enumerate(sums):
            for part in range(2):
                cut = slice(part * width, (part + 1) * width)
                vecs[12 + 2 * i + part : 13 + 2 * i + part] = value[:, cut]
                vecs[18 + 2 * i + part : 19 + 2 * i + part] = vec2[i : i + 1, cut]
        total[rows:] = jnp.zeros((half, dim), F32)
        d3[rows:, :width] = jnp.zeros((half, width), BF16)

    def out_grads():
        grads = mm_tn(low[...], ctx[...]).astype(BF16)
        put_rows(b_i, 3, grads[:, :width])
        put_rows(b_e, 3, grads[:, width:])
        cores(False, att_at + 3)
        cores(True, att_at + 3)

    def context_grad():
        dctx[...] = mm_nt(low[...], wo[...]).astype(BF16)

    def attend(n):
        pair = pair_order[n]
        cols = slice(pair * PAIR, (pair + 1) * PAIR)
        local_at = (pair % pairs) * PAIR
        if n == 0:
            loaded("att0")
            loaded("att1")
        loaded(("p", n))
        lane = lax.broadcasted_iota(jnp.int32, (1, PAIR), 1) // HEAD_DIM
        zero = jnp.zeros((), BF16)
        for first, count, key_first, k_slot, v_slot, probs_ref in (
            (0, SEG, 0, 2, 6, p_a),
            (SEG, half, SEG, 4, 1, p_m),
        ):
            q_at = slice(first, first + count)
            ks = slice(key_first, key_first + SEG)
            grad2, query2 = dctx[q_at, cols], slots[0, q_at, cols]
            keys, values = slots[k_slot, :SEG, cols], slots[v_slot, :SEG, cols]
            delta_t = (grad2.astype(F32) * ctx[q_at, cols].astype(F32)).T
            values_grad = keys_grad = query_grad = 0.0
            for h in range(2):
                grad_h = jnp.where(lane == h, grad2, zero)
                query_h = jnp.where(lane == h, query2, zero)
                keys_h = jnp.where(lane == h, keys, zero)
                probs = probs_ref[n % 2, h]
                delta = jnp.sum(delta_t[h * HEAD_DIM : (h + 1) * HEAD_DIM], axis=0, keepdims=True)
                prob_grad = mm_nt(values, grad_h)
                score_grad = (probs.astype(F32) * (prob_grad - delta)).astype(BF16)
                values_grad += mm(probs, grad_h)
                keys_grad += mm(score_grad, query_h)
                query_grad += mm_tn(score_grad, keys_h)
            for part, value, out_at in (
                (0, query_grad * HEAD_DIM**-0.5, q_at),
                (1, keys_grad, ks),
                (2, values_grad, ks),
            ):
                d3[out_at, part * width + local_at : part * width + local_at + PAIR] = value.astype(BF16)
        if n + 2 < 2 * pairs:
            load_probs(n + 2)

    def input_part(own):
        main = 3 if own else 7
        last = slice(0, width) if own else slice(width, 2 * width)
        total[...] += mm_nt(d3[:, : 2 * width], slots[main]) + mm_nt(
            d3[:, 2 * width :], slots[5, :, last]
        )

    def weight_part(own):
        buf = b_i if own else b_e
        grads = mm_tn(x_s[...], d3[...]).astype(BF16)
        for group in range(3):
            put_rows(buf, group, grads[:, group * width : (group + 1) * width])
            cores(own, att_at + group)
        row = y if own else 1 - y
        vecs[pl.ds(8 + row, 1)] = jnp.sum(d3[:rows, :width].astype(F32), axis=0, keepdims=True)
        vecs[pl.ds(10 + row, 1)] = jnp.sum(d3[:, 2 * width :].astype(F32), axis=0, keepdims=True)

    done = []

    def finish():
        top = copies.here(total.at[pl.ds(0, SEG)], top_o)
        top.start()
        done.append(top)
        mid_b[0] = total[rows:].astype(BF16)
        done.append(go(copies.to(mid_b.at[0], mid_r.at[0], c=1 - c)))
        vec_start(0)

    def middle():
        arrived(done[1])
        total[SEG:rows] += mid_r[0].astype(F32)
        mid_b[1] = total[SEG:rows].astype(BF16)

        @pl.when(jnp.logical_not(same))
        def _():
            in_d.start()

    ready_e, ready_i = {}, {}
    clock = 3.0
    for n in range(4):
        step(1.4, inner_grad, n)
        step(1.3, hidden_grad, n)
        step(1.3, up_grad, n)
        step(1.3, down_grad, n)
    step(1.6, out_back)
    step(1.4, out_grads)
    step(1.2, context_grad)
    for n in range(2 * pairs):
        step(2.1, attend, n)
        if n % pairs == pairs - 1:
            own = n > pairs
            if own:
                step(2.8, input_part, own)
                step(3.0, weight_part, own)
            else:
                step(3.0, weight_part, own)
                step(2.8, input_part, own)
    step(0.7, finish)
    when = {}
    for us, body, arguments in work:
        clock += us
        when[(body, *arguments)] = clock
    for k in range(att_at):
        ready = (up_grad, down_grad)[k * CHUNK // dim]
        ready_e[k] = when[ready, 1]
        ready_i[k] = when[ready, 3]
    for n in range(4):
        for ready, own in ((ready_e, False), (ready_i, True)):
            ready[att_at + n] = when[(out_grads,) if n == 3 else (weight_part, own)] + 1.0
    stages = {"y": to_y, "x": to_x, "z": to_z, "fz": from_z, "fx": from_x}
    chunk_order = {k: parts[k] for k in [*range(att_at), att_at + 3, att_at, att_at + 1, att_at + 2]}
    tasks = [
        (time, stages[stage[0]], (k, *stage[1:]))
        for time, stage, k in plan(chunk_order, levels, split, ready_e, ready_i)
    ]
    end = when[(finish,)]
    tasks.append((end + 4.0, middle, ()))
    for n in range(len(near)):
        tasks.append((end + 5.0 + 5.0 * n, vec_next, (n,)))
    tasks.sort(key=lambda t: t[0])
    clock = 3.0
    for us, body, arguments in work:
        while tasks and tasks[0][0] <= clock:
            _, task, its = tasks.pop(0)
            task(*its)
        body(*arguments)
        clock += us
    for _, task, its in tasks:
        task(*its)

    @pl.when(same)
    def _():
        out_here.wait()
        in_o[...] = total[SEG:rows]

    @pl.when(jnp.logical_not(same))
    def _():
        out_d.wait()
        in_d.wait()
        in_o[...] = mid_r[1].astype(F32)

    done[0].wait()
    for copy in every:
        copy.wait_send()
        if id(copy) not in waited:
            copy.wait_recv()


def final_body(pos_ref, sums, top, output, in_mid, out_mid, out_o, in_o, q_o, k_o, v_o, wo_o, up_o, down_o, tmp):
    j = pl.program_id(0)
    dim = up_o.shape[0]
    quarter, width = q_o.shape
    is_mid = jnp.where(pos_ref[2] == 0, j >= 2, j == 0)

    @pl.when(is_mid)
    def _():
        out_o[...] = out_mid[...]
        in_o[...] = in_mid[...]

    @pl.when(jnp.logical_not(is_mid))
    def _():
        out_o[...] = output[...]
        in_o[...] = top[...]

    up_o[...] = sums[0, :dim].astype(F32)
    down_o[...] = sums[0, dim : 2 * dim].astype(F32).T
    for part, ref in enumerate((q_o, k_o, v_o)):
        at = 2 * dim + part * quarter
        ref[...] = sums[0, at : at + quarter].astype(F32)
    row = pl.multiple_of((pos_ref[0] ^ j) * quarter, 16)
    at = 2 * dim + 3 * quarter
    tmp[pl.ds(row, quarter), :] = sums[0, at : at + quarter].astype(F32)

    @pl.when(j == pl.num_programs(0) - 1)
    def _():
        wo_o[...] = tmp[...].T


def shards(
    depth,
    tokens, lengths, buckets, w_query, b_query, w_key, w_value, b_value, w_out, b_out,
    norm1_gain, norm1_bias, w_up, b_up, w_down, b_down, norm2_gain, norm2_bias, cotangent,
):
    ix, ic, iy = (lax.axis_index(a) for a in ("x", "c", "y"))
    pos = jnp.stack([2 * ic + ix, ic, iy]).astype(jnp.int32)
    rows, dim = tokens.shape
    half = rows - SEG
    width = w_query.shape[1]
    units = w_up.shape[1]
    chunk = units // 4
    any_space = pl.BlockSpec(memory_space=pl.ANY)
    in_vmem = pl.BlockSpec(memory_space=pltpu.VMEM)

    table = jnp.concatenate([buckets[:, None], lengths], axis=1).astype(F32)
    info = jnp.stack([jnp.where(iy == 0, table[0], table[2]), table[1]])
    info = jnp.pad(info, ((0, 6), (0, 123)))
    bias = jnp.concatenate([b_query, b_value, b_up]).astype(F32).reshape(-1, width)
    bias = jnp.pad(bias, ((0, -bias.shape[0] % 8), (0, 0)))
    weights = (w_query, w_key, w_value, w_out, w_up, w_down)
    x, cot, wq_o, wk_o, wv_o, wo_o, wu_o, wd_o, bias_o, info_o = pl.pallas_call(
        gather_body,
        out_shape=[
            shape((rows + half, dim), BF16),
            shape((rows, dim), BF16),
            *[shape(w.shape, BF16) for w in weights],
            shape(bias.shape, F32),
            shape(info.shape, F32),
        ],
        in_specs=[any_space] * 8 + [in_vmem] * 2,
        out_specs=[in_vmem] * 2 + [any_space] * 6 + [in_vmem] * 2,
        scratch_shapes=[
            pltpu.SemaphoreType.DMA((40,)),
            pltpu.SemaphoreType.DMA((40,)),
            pltpu.SemaphoreType.DMA((4,)),
            pltpu.SemaphoreType.DMA((2,)),
        ],
        compiler_params=pltpu.CompilerParams(collective_id=1, has_side_effects=True),
        name="gather",
    )(tokens, cotangent, *weights, bias, info)
    info = jnp.where((jnp.arange(8) == 1)[:, None] & (ic != iy), info_o, info)
    bq_o = bias_o[0:1]
    bv_o = bias_o[1:2]
    bu_o = bias_o[2 : 2 + units // width].reshape(1, units)

    own = attend_forward(
        pos, x, (w_query, w_key, w_value), b_query[None], b_value[None], info, rows, "attend_fwd_own"
    )
    other = attend_forward(pos, x, (wq_o, wk_o, wv_o), bq_o, bv_o, info, rows, "attend_fwd_other")
    keep = own[6]
    ctx_i, ctx_o = own[3], other[3]
    row_vec = lambda v: v[None]
    const = lambda *dims: pl.BlockSpec(dims, lambda j, pos: (0,) * len(dims))
    cols = pl.BlockSpec((rows, chunk), lambda j, pos: (0, pos[0] ^ j))
    up_specs = [
        pl.BlockSpec((dim, chunk), lambda j, pos: (0, pos[0] ^ j)),
        pl.BlockSpec((1, chunk), lambda j, pos: (0, pos[0] ^ j)),
        pl.BlockSpec((chunk, dim), lambda j, pos: (pos[0] ^ j, 0)),
    ]
    b_out1, g1, s1 = row_vec(b_out), row_vec(norm1_gain), row_vec(norm1_bias)
    normed1, inverse1, hidden, act_i, slope_i, branch = call(
        up_body,
        (4,),
        pos,
        [x, ctx_i, ctx_o, w_out, wo_o, b_out1, g1, s1, w_up, b_up[None], w_down],
        [
            const(rows, dim),
            *[whole(v) for v in (ctx_i, ctx_o, w_out, wo_o, b_out1, g1, s1)],
            *up_specs,
        ],
        [
            shape((rows, dim), BF16),
            shape((rows, 1), F32),
            shape((rows, dim), BF16),
            shape((rows, units), BF16),
            shape((rows, units), BF16),
            shape((rows, dim), F32),
        ],
        [const(rows, dim), const(rows, 1), const(rows, dim), cols, cols, const(rows, dim)],
        [],
        2 * rows * dim * (dim + 2 * units),
        "ffn_fwd_own",
    )
    b_down1, g2, s2 = row_vec(b_down), row_vec(norm2_gain), row_vec(norm2_bias)
    act_o, slope_o, output, second, low, vec2 = call(
        down_body,
        (4,),
        pos,
        [hidden, branch, wu_o, wd_o, bu_o, b_down1, g2, s2, cot, keep],
        [
            whole(hidden),
            whole(branch),
            up_specs[0],
            up_specs[2],
            up_specs[1],
            *[whole(v) for v in (b_down1, g2, s2, cot, keep)],
        ],
        [
            shape((rows, units), BF16),
            shape((rows, units), BF16),
            shape((rows, dim), BF16),
            shape((rows, dim), F32),
            shape((rows, dim), BF16),
            shape((3, dim), F32),
        ],
        [cols, cols, const(rows, dim), const(rows, dim), const(rows, dim), const(3, dim)],
        [pltpu.VMEM((rows, dim), F32)],
        4 * rows * dim * units,
        "ffn_fwd_other",
    )

    side = lambda n: jnp.concatenate([own[n], other[n]], axis=1)
    probs = [jnp.concatenate([own[n], other[n]]) for n in (4, 5)]
    ctx = jnp.concatenate([ctx_i, ctx_o], axis=1)
    levels = depth.bit_length() - 1
    more = max(levels - 2, 0)
    size = 3 * dim
    links = levels + 3
    remote = 8 * (levels + 10) + links + 2
    sums, top, vec, in_mid, out_mid = pl.pallas_call(
        functools.partial(backward_body, depth),
        out_shape=[
            shape((4, size, width), BF16),
            shape((SEG, dim), F32),
            shape((24, width), F32),
            shape((half, dim), F32),
            shape((half, dim), BF16),
        ],
        in_specs=[any_space] * 29 + [in_vmem] * 2,
        out_specs=[any_space] * 2 + [in_vmem] * 3,
        scratch_shapes=[
            *[pltpu.VMEM((rows, dim), BF16)] * 2,
            pltpu.VMEM((8, rows, dim), BF16),
            pltpu.VMEM((rows + half, dim), F32),
            *[pltpu.VMEM((4, size, width), BF16)] * 2,
            *[pltpu.VMEM((2, size, width), BF16)] * 3,
            pltpu.VMEM((size, width), BF16),
            pltpu.VMEM((size // 2, width), BF16),
            pltpu.VMEM((size // 4, width), BF16),
            pltpu.VMEM((max(more, 1), size // 4 if more else 16, width), BF16),
            pltpu.VMEM((rows, dim), BF16),
            pltpu.VMEM((rows, 1), F32),
            *[pltpu.VMEM((rows, dim), BF16)] * 3,
            pltpu.VMEM((rows + half, dim), BF16),
            pltpu.VMEM((2, 2, SEG, SEG), BF16),
            pltpu.VMEM((2, 2, SEG, half), BF16),
            pltpu.VMEM((rows + half, 3 * width), BF16),
            pltpu.VMEM((24, width), F32),
            pltpu.VMEM((2 * links, 24, width), F32),
            pltpu.VMEM((2, half, dim), BF16),
            pltpu.VMEM((2, half, dim), BF16),
            pltpu.SemaphoreType.DMA((remote,)),
            pltpu.SemaphoreType.DMA((remote,)),
            pltpu.SemaphoreType.DMA((64,)),
            pltpu.SemaphoreType.DMA((4,)),
        ],
        compiler_params=pltpu.CompilerParams(
            collective_id=2, has_side_effects=True, vmem_limit_bytes=VMEM_LIMIT
        ),
        name="backward",
    )(
        low, hidden, act_i, act_o, slope_i, slope_o, w_up, wu_o, w_down, wd_o, second, normed1, inverse1,
        w_out, wo_o, ctx, x, side(0), side(1), side(2), *probs, w_query, w_key, w_value, wq_o, wk_o, wv_o,
        output, g1, vec2,
    )
    quarter = dim // 4
    b_up_grad = lax.dynamic_slice_in_dim(vec, 4 * iy, 4).reshape(units)
    b_query_grad = lax.dynamic_slice_in_dim(vec, 8 + iy, 1)[0]
    b_value_grad = lax.dynamic_slice_in_dim(vec, 10 + iy, 1)[0]
    rest = vec[12:].reshape(6, dim)
    full_block = lambda j, pos: (jnp.where(pos[2] == 0, jnp.minimum(j, 1), jnp.clip(j - 1, 0, 1)), 0)
    row_block = pl.BlockSpec((half, dim), lambda j, pos: (jnp.minimum(j, 2), 0))
    by_rows = lambda n, m: pl.BlockSpec((n, m), lambda j, pos: (pos[0] ^ j, 0))
    output, input_grad, w_query_grad, w_key_grad, w_value_grad, w_out_grad, w_up_grad, w_down_grad = call(
        final_body,
        (4,),
        pos,
        [sums, top, output, in_mid, out_mid],
        [
            pl.BlockSpec((1, size, width), lambda j, pos: (j, 0, 0)),
            pl.BlockSpec((half, dim), full_block),
            pl.BlockSpec((half, dim), full_block),
            whole(in_mid),
            whole(out_mid),
        ],
        [
            shape((rows, dim), BF16),
            shape((rows, dim), F32),
            *[shape((dim, width), F32)] * 3,
            shape((width, dim), F32),
            shape((dim, units), F32),
            shape((units, dim), F32),
        ],
        [
            row_block,
            row_block,
            *[by_rows(quarter, width)] * 3,
            const(width, dim),
            pl.BlockSpec((dim, chunk), lambda j, pos: (0, pos[0] ^ j)),
            by_rows(chunk, dim),
        ],
        [pltpu.VMEM((dim, width), F32)],
        0,
        "final",
    )
    return (
        output,
        input_grad,
        w_query_grad,
        b_query_grad,
        w_key_grad,
        w_value_grad,
        b_value_grad,
        w_out_grad,
        rest[2],
        rest[0],
        rest[1],
        w_up_grad,
        b_up_grad,
        w_down_grad,
        rest[5],
        rest[3],
        rest[4],
    )


def solution(mesh):
    depth = mesh.shape["dp"] // 4
    inner = Mesh(mesh.devices.reshape(depth, 2, 2, mesh.shape["mp"]), ("z", "x", "c", "y"))
    dp = ("z", "x", "c")
    every = (*dp, "y")
    placed = (
        P(every, None),
        P(dp, None),
        P(dp),
        P(None, "y"),
        P("y"),
        P(None, "y"),
        P(None, "y"),
        P("y"),
        P("y", None),
        P(),
        P(),
        P(),
        P(None, "y"),
        P("y"),
        P("y", None),
        P(),
        P(),
        P(),
        P(every, None),
    )
    return jax.shard_map(
        functools.partial(shards, depth),
        mesh=inner,
        in_specs=placed,
        out_specs=(
            P(every, None),
            P(every, None),
            P(None, "y"),
            P("y"),
            P(None, "y"),
            P(None, "y"),
            P("y"),
            P("y", None),
            P(),
            P(),
            P(),
            P(None, "y"),
            P("y"),
            P("y", None),
            P(),
            P(),
            P(),
        ),
        check_vma=False,
    )
```

```python
import functools

import jax
import jax.numpy as jnp
from jax import lax
from jax.experimental import pallas as pl
from jax.experimental.pallas import tpu as pltpu
from jax.sharding import Mesh, PartitionSpec as P

HEAD_DIM = 64
SEG = 512
PAIR = 2 * HEAD_DIM
NEG = -1e30
EPS = 1e-12
ROOT_HALF = 0.7071067811865476
INV_ROOT_TWO_PI = 0.3989422804014327
F32 = jnp.float32
BF16 = jnp.bfloat16
VMEM_LIMIT = 60 * 1024 * 1024
TILE = 256
CHUNK = 384
MESH_IDS = pl.DeviceIdType.MESH


def mm(left, right):
    return lax.dot_general(left, right, (((1,), (0,)), ((), ())), preferred_element_type=F32)


def mm_nt(left, right):
    return lax.dot_general(left, right, (((1,), (1,)), ((), ())), preferred_element_type=F32)


def mm_tn(left, right):
    return lax.dot_general(left, right, (((0,), (0,)), ((), ())), preferred_element_type=F32)


def call(body, grid, pos, inputs, in_specs, out_shape, out_specs, scratch, flops, name):
    moved = sum(v.size * v.dtype.itemsize for v in inputs) + sum(
        v.size * v.dtype.itemsize for v in out_shape
    )
    return pl.pallas_call(
        body,
        grid_spec=pltpu.PrefetchScalarGridSpec(
            num_scalar_prefetch=1,
            grid=grid,
            in_specs=in_specs,
            out_specs=out_specs,
            scratch_shapes=scratch,
        ),
        out_shape=out_shape,
        compiler_params=pltpu.CompilerParams(
            dimension_semantics=("arbitrary",) * len(grid), vmem_limit_bytes=VMEM_LIMIT
        ),
        cost_estimate=pl.CostEstimate(flops=flops, bytes_accessed=moved, transcendentals=0),
        name=name,
    )(pos, *inputs)


def whole(array):
    zeros = (0,) * array.ndim
    return pl.BlockSpec(array.shape, lambda j, pos: zeros)


def shape(dims, kind):
    return jax.ShapeDtypeStruct(dims, kind)


def gelu_parts(inner):
    erf = lax.erf(inner * ROOT_HALF)
    below = 0.5 + 0.5 * erf
    density = jnp.exp(inner * inner * -0.5) * INV_ROOT_TWO_PI
    return inner * below, below + inner * density


def row_ids(info, at, places):
    bucket = info[at : at + 1, 0:1]
    span = jnp.where(bucket < 0.5, 1.0 * SEG, jnp.where(bucket < 1.5, 0.5 * SEG, 0.25 * SEG))
    row = jnp.zeros_like(places)
    size = jnp.zeros_like(places) + info[at : at + 1, 1:2]
    for slot in range(1, 4):
        later = places >= span * slot
        row = jnp.where(later, 1.0 * slot, row)
        size = jnp.where(later, info[at : at + 1, slot + 1 : slot + 2], size)
    return row, places - row * span < size


class Copies:
    def __init__(self, send, recv, local):
        self.send, self.recv, self.local = send, recv, local
        self.remote_count = self.local_count = 0

    def to(self, src, dst, **device):
        n = self.remote_count
        self.remote_count += 1
        return pltpu.make_async_remote_copy(
            src_ref=src,
            dst_ref=dst,
            send_sem=self.send.at[n],
            recv_sem=self.recv.at[n],
            device_id=device,
            device_id_type=MESH_IDS,
        )

    def here(self, src, dst):
        n = self.local_count
        self.local_count += 1
        return pltpu.make_async_copy(src, dst, self.local.at[n])


def coords():
    return tuple(lax.axis_index(a) for a in ("z", "x", "c", "y"))


def greet(devices):
    barrier = pltpu.get_barrier_semaphore()
    for device in devices:
        pl.semaphore_signal(barrier, inc=1, device_id=device, device_id_type=MESH_IDS)
    pl.semaphore_wait(barrier, len(devices))


def forward_body(
    tokens, cot_h, wq, wk, wv, wo, wu, wd, bias, info, consts,
    x_o, wq_o, wk_o, wv_o, wo_o, wu_o, wd_o, q_o, k_o, v_o, pa_o, pm_o, ctx_o, normed_o, inv_o, hidden_o,
    act_io, act_oo, slope_io, slope_oo, second_o, low_o, out_o, vec_o,
    x_s, cot, w3, wo_s, wu_s, wd_s, q_s, k_s, v_s, p_a, p_m, ctx, normed, inv, hidden, acc, act, slope, low, out_s,
    keep, mask_a, mask_m, bias_r, info_r, info_s, send, recv, local, crossed,
):
    z, x, c, y = coords()
    copies = Copies(send, recv, local)
    rows, dim = cot.shape
    half = rows - SEG
    width = wq.shape[1]
    pairs = width // PAIR
    same = c == y
    full = pl.ds(pl.multiple_of(y * half, half), SEG)
    mid = pl.ds(pl.multiple_of((1 - y) * SEG, half), half)
    own_at, sib_at = pl.ds(SEG, half), pl.ds(SEG + half, half)
    loads, stores = {}, []

    def load(name, *moves):
        loads[name] = [copies.here(src, dst) for src, dst in moves]
        for copy in loads[name]:
            copy.start()

    def loaded(name):
        for copy in loads.pop(name, ()):
            copy.wait()

    def store(src, dst):
        copy = copies.here(src, dst)
        copy.start()
        stores.append(copy)
        return copy

    load(
        "qkv",
        (tokens.at[full], x_s.at[pl.ds(0, SEG)]),
        *[(w, w3.at[0, :, pl.ds(n * width, width)]) for n, w in enumerate((wq, wk, wv))],
    )
    x_own = copies.here(tokens.at[mid], x_s.at[own_at])
    cot_own = copies.here(cot_h.at[mid], cot.at[own_at])

    @pl.when(same)
    def _():
        x_own.start()
        cot_own.start()

    greet([{"y": 1 - y}, {"x": 1 - x}, {"c": 1 - c}, {"c": 1 - c, "y": 1 - y}])

    x_y = copies.to(tokens.at[mid], x_s.at[sib_at], y=1 - y)
    x_c1 = copies.to(x_s.at[own_at], x_s.at[sib_at], c=1 - c)
    x_c2 = copies.to(x_s.at[sib_at], x_s.at[own_at], c=1 - c)
    cot_d = pltpu.make_async_remote_copy(
        src_ref=cot_h.at[mid], dst_ref=cot.at[own_at], send_sem=crossed.at[0], recv_sem=crossed.at[1],
        device_id={"c": 1 - c, "y": 1 - y}, device_id_type=MESH_IDS,
    )
    info_copy = copies.to(info, info_r, c=1 - c)
    bias_copy = copies.to(bias, bias_r, y=1 - y)

    @pl.when(jnp.logical_not(same))
    def _():
        x_y.start()

    info_copy.start()
    bias_copy.start()

    def row_piece(ref, x_at, part, parts, offset=0, columns=None):
        n = (ref.shape[0] if offset == 0 else ref.shape[0] - offset) // 4
        at = pl.ds(pl.multiple_of(offset + (2 * c + x_at) * n + part * (n // parts), 16), n // parts)
        return ref.at[at] if columns is None else ref.at[at, columns]

    def column_piece(ref, x_at, part, parts):
        n, m = ref.shape[1] // 4, ref.shape[0] // parts
        return ref.at[pl.ds(part * m, m), pl.ds(pl.multiple_of((2 * c + x_at) * n, 128), n)]

    arrays = []
    for n, w in enumerate((wq, wk, wv)):
        cut = pl.ds(n * width, width)
        arrays.append((
            "qkv", 3.1,
            lambda x_at, w=w: row_piece(w, x_at, 0, 1),
            lambda x_at, cut=cut: row_piece(w3.at[1], x_at, 0, 1, 0, cut),
        ))
    arrays.append(("wo", 3.1, lambda x_at: row_piece(wo, x_at, 0, 1), lambda x_at: row_piece(wo_s, x_at, 0, 1, width)))
    for part in range(2):
        arrays.append((
            "wu", 6.2,
            lambda x_at, part=part: column_piece(wu, x_at, part, 2),
            lambda x_at, part=part: column_piece(wu_s.at[1], x_at, part, 2),
        ))
    for part in range(3):
        arrays.append((
            "wd", 4.1,
            lambda x_at, part=part: row_piece(wd, x_at, part, 3),
            lambda x_at, part=part: row_piece(wd_s.at[1], x_at, part, 3),
        ))
    over_y, over_x, over_c = [], {}, {}

    def next_y():
        n = len(over_y)
        if n < len(arrays):
            over_y.append(copies.to(arrays[n][2](x), arrays[n][3](x), y=1 - y))
            over_y[n].start()
        elif n == len(arrays):
            over_y.append(None)

            @pl.when(jnp.logical_not(same))
            def _():
                cot_d.start()

    def pass_on(n, x_at):
        there = arrays[n][3](x_at)
        over_c[n, x_at is x] = copies.to(there, there, c=1 - c)
        over_c[n, x_at is x].start()

    def from_y(n):
        over_y[n].wait_recv()
        next_y()
        there = arrays[n][3](x)
        over_x[n] = copies.to(there, there, x=1 - x)
        over_x[n].start()
        pass_on(n, x)

    def from_x(n):
        over_x[n].wait_recv()
        pass_on(n, 1 - x)

    def mid_rows():
        @pl.when(same)
        def _():
            x_own.wait()
            x_y.wait_recv()
            x_c1.start()
            x_c2.start()

    tasks = [(7.0, mid_rows, ())]
    clock = 2.0 + 4.1
    x_free = 0.0
    for n, array in enumerate(arrays):
        clock += array[1]
        tasks.append((clock + 2.0, from_y, (n,)))
        x_free = max(x_free, clock + 2.0) + array[1]
        tasks.append((x_free + 2.0, from_x, (n,)))
    tasks.sort(key=lambda t: t[0])
    come = set()

    def run_until(time):
        while tasks and tasks[0][0] <= time:
            _, task, its = tasks.pop(0)
            task(*its)

    def need(name):
        if name in come:
            return
        come.add(name)
        while any(task in (from_y, from_x) and arrays[its[0]][0] == name for _, task, its in tasks):
            _, task, its = tasks.pop(0)
            task(*its)
        for n, array in enumerate(arrays):
            if array[0] == name:
                over_c[n, True].wait_recv()
                over_c[n, False].wait_recv()

    for _ in range(3):
        next_y()
    load("wo", (wo, wo_s.at[pl.ds(0, width)]))
    load("wu", (wu, wu_s.at[0]))
    load("wd", (wd, wd_s.at[0]))
    load("cot", (cot_h.at[full], cot.at[pl.ds(0, SEG)]))

    work = []

    def step(us, body, *arguments):
        work.append((us, body, arguments))

    def mask_of(mask, at, count):
        places = lax.broadcasted_iota(jnp.int32, (SEG, 1), 0)
        across = lax.broadcasted_iota(jnp.int32, (1, count), 1)
        if at == 1:
            places = (places + half * c) % SEG
            across = across + half * c
        key_row, valid = row_ids(info_s, at, places.astype(F32))
        query_row, _ = row_ids(info_s, at, across.astype(F32))
        allowed = jnp.where(valid, key_row, -1.0) == query_row
        mask[...] = jnp.where(allowed, 0.0, NEG)
        keep[at * SEG : at * SEG + count] = jnp.where(valid[:count], 1.0, 0.0)

    def project(other, first, count):
        if not other and first == 0:
            loaded("qkv")
            info_s[...] = info[...]
            mask_of(mask_a, 0, SEG)
        if not other and first == SEG:
            info_copy.wait_recv()
            info_s[...] = jnp.where(same, info[...], info_r[...])
            mask_of(mask_m, 1, half)

            @pl.when(jnp.logical_not(same))
            def _():
                x_c1.wait_recv()
                x_c2.wait_recv()

            store(x_s, x_o)
        if other:
            bias_copy.wait_recv()
            need("qkv")
            for n, w in enumerate((wq_o, wk_o, wv_o)):
                store(w3.at[1, :, pl.ds(n * width, width)], w)
        vector = bias_r if other else bias
        at = slice(first, first + count)
        mine = slice(first, min(first + count, rows))
        size = mine.stop - first
        cols = slice(width, 2 * width) if other else slice(0, width)
        qkv = mm(x_s[at], w3[1 if other else 0])
        q_s[mine, cols] = ((qkv[:size, :width] + vector[0:1]) * HEAD_DIM**-0.5).astype(BF16)
        k_s[at, cols] = qkv[:, width : 2 * width].astype(BF16)
        v_s[at, cols] = (qkv[:, 2 * width :] + vector[1:2]).astype(BF16)

    used = {}

    def attend(pair, middle):
        first, count, mask, probs, out = (SEG, half, mask_m, p_m, pm_o) if middle else (0, SEG, mask_a, p_a, pa_o)
        at = slice(first, first + count)
        ks = slice(first, first + SEG)
        cols = slice(pair * PAIR, (pair + 1) * PAIR)
        s = pair % 3
        if (middle, s) in used:
            used[middle, s].wait()
        lane = lax.broadcasted_iota(jnp.int32, (1, PAIR), 1) // HEAD_DIM
        query, keys = q_s[at, cols], k_s[ks, cols]
        values_t = v_s[ks, cols].astype(F32).T.astype(BF16)
        parts = []
        for h in range(2):
            query_h = jnp.where(lane == h, query, jnp.zeros((), BF16))
            scores = mm_nt(keys, query_h) + mask[...]
            top = jnp.max(scores, axis=0, keepdims=True)
            grown = jnp.exp(scores - top)
            prob = (grown * (1.0 / jnp.sum(grown, axis=0, keepdims=True))).astype(BF16)
            probs[s, h] = prob
            parts.append(mm(values_t[h * HEAD_DIM : (h + 1) * HEAD_DIM], prob))
        ctx[at, cols] = jnp.concatenate(parts, axis=0).T.astype(BF16)
        used[middle, s] = copies.here(probs.at[s], out.at[pl.ds(2 * pair, 2)])
        used[middle, s].start()

    def stored_qkv():
        for src, dst in ((q_s, q_o), (k_s, k_o), (v_s, v_o), (ctx, ctx_o)):
            store(src, dst)

    def normalize(value):
        centre = value - jnp.mean(value, axis=-1, keepdims=True)
        inverse = lax.rsqrt(jnp.mean(centre * centre, axis=-1, keepdims=True) + EPS)
        return centre * inverse, inverse

    def first_norm():
        loaded("wo")
        need("wo")
        store(wo_s.at[pl.ds(width, width)], wo_o)
        acc[...] = mm(ctx[...], wo_s[...])
        for r in range(0, rows, TILE):
            at = slice(r, r + TILE)
            normal, inverse = normalize(x_s[at].astype(F32) + acc[at] + consts[0:1])
            normed[at] = normal.astype(BF16)
            inv[at] = inverse
            hidden[at] = (normal * consts[1:2] + consts[2:3]).astype(BF16)
        store(normed, normed_o)
        store(inv, inv_o)
        store(hidden, hidden_o)

    def up(other, h):
        if h == 0:
            if other:
                need("wu")
                store(wu_s.at[1], wu_o)
            else:
                loaded("wu")
        s = 1 if other else 0
        vector = bias_r if other else bias
        cols = slice(h * dim, (h + 1) * dim)
        shift = jnp.concatenate([vector[2 + 2 * h : 3 + 2 * h], vector[3 + 2 * h : 4 + 2 * h]], axis=1)
        active, steep = gelu_parts(mm(hidden[...], wu_s[s, :, cols]) + shift)
        act[s, :, cols] = active.astype(BF16)
        slope[s, :, cols] = steep.astype(BF16)
        if h == 1:
            store(act.at[s], act_oo if other else act_io)
            store(slope.at[s], slope_oo if other else slope_io)

    def down(other):
        if other:
            need("wd")
            store(wd_s.at[1], wd_o)
            acc[...] += mm(act[1], wd_s[1])
        else:
            loaded("wd")
            acc[...] = mm(act[0], wd_s[0])

    def second_norm():
        loaded("cot")

        @pl.when(same)
        def _():
            cot_own.wait()

        @pl.when(jnp.logical_not(same))
        def _():
            cot_d.wait_recv()

        sums = [0.0, 0.0, 0.0]
        for r in range(0, rows, TILE):
            at = slice(r, r + TILE)
            normal, inverse = normalize(hidden[at].astype(F32) + acc[at] + consts[3:4])
            g = consts[4:5]
            out_s[at] = ((normal * g + consts[5:6]) * keep[at]).astype(BF16)
            upstream = cot[at].astype(F32) * keep[at]
            scaled = upstream * g
            grad = inverse * (
                scaled
                - jnp.mean(scaled, axis=-1, keepdims=True)
                - normal * jnp.mean(scaled * normal, axis=-1, keepdims=True)
            )
            acc[at] = grad
            low[at] = grad.astype(BF16)
            sums[0] += jnp.sum(upstream * normal, axis=0, keepdims=True)
            sums[1] += jnp.sum(upstream, axis=0, keepdims=True)
            sums[2] += jnp.sum(grad, axis=0, keepdims=True)
        for i, value in enumerate(sums):
            vec_o[i : i + 1] = value
        for src, dst in ((acc, second_o), (low, low_o), (out_s, out_o)):
            store(src, dst)

    step(1.5, project, False, 0, SEG)
    for pair in range(pairs):
        step(1.4, attend, pair, False)
    step(1.8, project, False, SEG, SEG)
    for pair in range(pairs):
        step(0.7, attend, pair, True)
    step(2.4, project, True, 0, rows + half)
    for pair in range(pairs, 2 * pairs):
        step(1.4, attend, pair, False)
        step(0.7, attend, pair, True)
    step(0.2, stored_qkv)
    step(2.5, first_norm)
    step(2.2, up, False, 0)
    step(2.2, up, False, 1)
    step(2.2, down, False)
    step(2.2, up, True, 0)
    step(2.2, up, True, 1)
    step(2.2, down, True)
    step(2.0, second_norm)
    starts = {(project, False, SEG, SEG): 10.5, (project, True, 0, rows + half): 23.5, (up, True, 0): 41.0, (down, True): 51.0}
    clock = 2.0
    for us, body, arguments in work:
        clock = max(clock, starts.get((body, *arguments), 0.0))
        run_until(clock)
        body(*arguments)
        clock += us
    run_until(1e9)

    @pl.when(same)
    def _():
        x_c1.wait_send()
        x_c2.wait_send()

    @pl.when(jnp.logical_not(same))
    def _():
        x_y.wait_send()
        cot_d.wait_send()

    info_copy.wait_send()
    bias_copy.wait_send()
    for copy in [v for v in over_y if v is not None] + list(over_x.values()) + list(over_c.values()):
        copy.wait_send()
    for copy in stores + list(used.values()):
        copy.wait()


def plan(parts, levels, split, ready_e, ready_i):
    free = {"y": 0.0, "x": 0.0, "z": 0.0}
    order = []
    waiting = [(ready_e[k], n, k, ("y",)) for n, k in enumerate(parts)]
    done_y = {}

    def send(link, now, us):
        start = max(now, free[link])
        free[link] = start + us
        return start + us + 2.0

    while waiting:
        waiting.sort()
        now, n, k, stage = waiting.pop(0)
        us = parts[k] * 12.4 / CHUNK
        name = stage[0]
        link = {"y": "y", "x": "x", "fx": None}.get(name, "z")
        if name == "fz" and stage[1] == 0:
            link = "x"
        if link and free[link] > now + 2.5:
            waiting.append((free[link] - 2.0, n, k, stage))
            continue
        order.append((now, stage, k))
        if name == "y":
            waiting.append((max(send("y", now, us), ready_i[k]), n, k, ("x",)))
        elif name == "x":
            waiting.append((send("x", now, us / 2), n, k, ("z", 0)))
        elif name == "z":
            level = stage[1]
            if level < levels:
                waiting.append((send("z", now, us / 4), n, k, ("z", level + 1)))
            elif split:
                waiting.append((send("z", now, us / 4), n, k, ("fz", split - 1)))
            else:
                waiting.append((now, n, k, ("fz", 0)))
        elif name == "fz":
            if stage[1] > 0:
                waiting.append((send("z", now, us / 4), n, k, ("fz", stage[1] - 1)))
            else:
                waiting.append((send("x", now, us / 2), n, k, ("fx",)))
    return order


def backward_body(
    depth,
    low_h, hidden_h, act_i, act_o, slope_i, slope_o, wu_i, wu_o, wd_i, wd_o, second_h, normed_h, inv_h,
    wo_i, wo_o, ctx_h, x_h, q_h, k_h, v_h, pa_h, pm_h, wq_i, wk_i, wv_i, wq_o, wk_o, wv_o, output_h, consts, vec2,
    sums_o, top_o, vec_o, in_o, out_o,
    low, hidden, slots, total, b_e, b_i, c_e, c_i, y_r, x_r, z_a, z_b, zx_r, normed, inv, wo, ctx, dctx, x_s,
    p_a, p_m, d3, vecs, vec_r, mid_b, mid_r, send, recv, local, crossed,
):
    z, x, c, y = coords()
    copies = Copies(send, recv, local)
    steps = []
    while 2 ** len(steps) < depth:
        steps.append(2 ** len(steps))
    levels = len(steps)
    split = min(2, levels)
    bits = [(z // s) % 2 for s in steps]
    z_partner = [z + s - 2 * s * b for s, b in zip(steps, bits)]
    near = [{"c": 1 - c}, {"y": 1 - y}, {"x": 1 - x}] + [{"z": p} for p in z_partner]
    same = c == y
    rows, dim = low.shape
    half = rows - SEG
    width = b_e.shape[2]
    quarter = dim // 4
    ffn_rows = 2 * dim
    first_row, parts = {}, {}
    att_at = ffn_rows // CHUNK
    for n in range(att_at):
        first_row[n], parts[n] = n * CHUNK, CHUNK
    for n in range(4):
        first_row[att_at + n], parts[att_at + n] = ffn_rows + n * quarter, quarter
    every, waited = [], set()

    def at(k):
        return pl.ds(first_row[k], parts[k])

    def go(copy):
        copy.start()
        every.append(copy)
        return copy

    def arrived(copy):
        copy.wait_recv()
        waited.add(id(copy))

    loads = {}

    def load(name, *pairs):
        loads[name] = [copies.here(src, dst) for src, dst in pairs]
        for copy in loads[name]:
            copy.start()

    def loaded(name):
        for copy in loads.pop(name, ()):
            copy.wait()

    chunks = [(False, 1 - c), (False, c), (True, 1 - c), (True, c)]

    def load_ffn(n):
        own, h = chunks[n]
        s = n % 2
        cut = pl.ds(pl.multiple_of(h * dim, 128), dim)
        load(
            ("ffn", n),
            ((wd_i if own else wd_o).at[cut], slots.at[2 + s]),
            ((slope_i if own else slope_o).at[:, cut], slots.at[6 + s]),
            ((wu_i if own else wu_o).at[:, cut], slots.at[s]),
            ((act_i if own else act_o).at[:, cut], slots.at[4 + s]),
        )

    load("low", (low_h, low))
    load_ffn(0)
    load("second", (second_h, total.at[pl.ds(0, rows)]), (hidden_h, hidden))
    load_ffn(1)
    greet(near + [{"c": 1 - c, "y": 1 - y}])

    out_d = pltpu.make_async_remote_copy(
        src_ref=output_h.at[pl.ds(SEG, half)], dst_ref=out_o, send_sem=crossed.at[0], recv_sem=crossed.at[1],
        device_id={"c": 1 - c, "y": 1 - y}, device_id_type=MESH_IDS,
    )
    in_d = pltpu.make_async_remote_copy(
        src_ref=mid_b.at[1], dst_ref=mid_r.at[1], send_sem=crossed.at[2], recv_sem=crossed.at[3],
        device_id={"c": 1 - c, "y": 1 - y}, device_id_type=MESH_IDS,
    )
    out_here = copies.here(output_h.at[pl.ds(SEG, half)], out_o)

    @pl.when(same)
    def _():
        out_here.start()

    @pl.when(jnp.logical_not(same))
    def _():
        out_d.start()

    load("mid", (wo_i, wo.at[pl.ds(0, width)]), (wo_o, wo.at[pl.ds(width, width)]), (ctx_h, ctx), (normed_h, normed), (inv_h, inv), (x_h, x_s))

    def add(n, out, *ins):
        def step(i, _):
            rows_at = pl.ds(pl.multiple_of(i * 48, 16), 48)
            value = ins[0][rows_at].astype(F32)
            for other in ins[1:]:
                value = value + other[rows_at].astype(F32)
            out[rows_at] = value.astype(out.dtype)
            return 0

        lax.fori_loop(0, n // 48, step, 0)

    def add2(n, out, *ins):
        for part in range(2):
            add(n, out.at[part], *[v.at[part] for v in ins])

    got_e, got_i, got_y, got_x, got_z, back_z, put, got_bx = {}, {}, {}, {}, {}, {}, {}, {}

    def cores(own, k):
        buf, there, got = (b_i, c_i, got_i) if own else (b_e, c_e, got_e)
        got[k] = go(copies.to(buf.at[pl.ds(2, 2), at(k)], there.at[:, at(k)], c=1 - c))

    def to_y(k):
        arrived(got_e[k])
        mine = b_e.at[pl.ds(0, 2), at(k)]
        add2(parts[k], mine, mine, c_e.at[:, at(k)])
        got_y[k] = go(copies.to(mine, y_r.at[:, at(k)], y=1 - y))

    def to_x(k):
        arrived(got_i[k])
        arrived(got_y[k])
        mine = b_i.at[pl.ds(0, 2), at(k)]
        add2(parts[k], mine, mine, c_i.at[:, at(k)], y_r.at[:, at(k)])
        got_x[k] = go(copies.to(b_i.at[1, at(k)], x_r.at[at(k)], x=1 - x))

    def base(k, level):
        row, size = first_row[k], parts[k]
        for n in range(min(level, split)):
            size //= 2
            row = row + bits[n] * size
        return row, size

    def slot(k, level):
        cut = 2 ** (level + 1)
        return (z_a, z_b)[level].at[pl.ds(first_row[k] // cut, parts[k] // cut)]

    def extra(k, n):
        return zx_r.at[n, pl.ds(first_row[k] // 4, parts[k] // 4)]

    def to_z(k, level):
        row, size = base(k, level)
        mine = b_i.at[0, pl.ds(pl.multiple_of(row, 16), size)]
        if level == 0:
            arrived(got_x[k])
            add(size, mine, mine, x_r.at[at(k)])
        else:
            if level > split:
                got_z[k, level - 1].wait()
            else:
                arrived(got_z[k, level - 1])
            add(size, mine, mine, slot(k, level - 1) if level <= split else extra(k, level - 1 - split))
        if level < split:
            size //= 2
            out = b_i.at[0, pl.ds(pl.multiple_of(row + (1 - bits[level]) * size, 16), size)]
            got_z[k, level] = go(copies.to(out, slot(k, level), z=z_partner[level]))
        elif level < levels:
            got_z[k, level] = copies.to(mine, extra(k, level - split), z=z_partner[level])
            got_z[k, level].start()
        else:
            place = sums_o.at[0, pl.ds(pl.multiple_of(row, 16), size)]
            put[k] = copies.here(mine, place)
            put[k].start()
            if split:
                back_z[k, split - 1] = go(copies.to(mine, place, z=z_partner[split - 1]))

    def from_z(k, level):
        if level == max(split, 1) - 1:
            put[k].wait()
        if split:
            arrived(back_z[k, level])
        if level > 0:
            row, size = base(k, level)
            place = sums_o.at[0, pl.ds(pl.multiple_of(row, 16), size)]
            back_z[k, level - 1] = go(copies.to(place, place, z=z_partner[level - 1]))
        else:
            mine = sums_o.at[0, at(k)]
            got_bx[k] = go(copies.to(mine, sums_o.at[1, at(k)], x=1 - x))
            go(copies.to(mine, sums_o.at[2, at(k)], c=1 - c))

    def from_x(k):
        arrived(got_bx[k])
        go(copies.to(sums_o.at[1, at(k)], sums_o.at[3, at(k)], c=1 - c))

    vec_copies = {}

    def vec_start(n):
        source = vecs if n == 0 else vec_r.at[2 * n - 1]
        vec_copies[n] = go(copies.to(source, vec_r.at[2 * n], **near[n]))

    def vec_next(n):
        arrived(vec_copies[n])
        value = (vecs if n == 0 else vec_r.at[2 * n - 1])[...] + vec_r[2 * n]
        if n == len(near) - 1:
            vec_o[...] = value
        else:
            vec_r[2 * n + 1] = value
            vec_start(n + 1)

    work = []

    def step(us, body, *arguments):
        work.append((us, body, arguments))

    def put_columns(buf, row, grads, keep):
        for part in range(2):
            rel = (0 if keep else 2) + (part + x) % 2
            buf[rel, row : row + dim] = grads[:, part * width : (part + 1) * width]

    def put_rows(buf, group, grads):
        for p in range(4):
            rel = 2 * ((p // 2 + c) % 2) + (p % 2 + x) % 2
            buf[rel, ffn_rows + group * quarter : ffn_rows + (group + 1) * quarter] = grads[
                p * quarter : (p + 1) * quarter
            ]

    def inner_grad(n):
        own, h = chunks[n]
        if n == 0:
            loaded("low")
        loaded(("ffn", n))
        s = n % 2
        grad = (mm_nt(low[...], slots[2 + s]) * slots[6 + s].astype(F32)).astype(BF16)
        d3[:rows, :dim] = grad
        bias = jnp.sum(grad.astype(F32), axis=0, keepdims=True)
        for part in range(2):
            row = 4 * (y if own else 1 - y) + 2 * h + part
            vecs[pl.ds(row, 1)] = bias[:, part * width : (part + 1) * width]

    def hidden_grad(n):
        if n == 0:
            loaded("second")
        total[:rows] += mm_nt(d3[:rows, :dim], slots[n % 2])

    def up_grad(n):
        own = chunks[n][0]
        put_columns(b_i if own else b_e, 0, mm_tn(hidden[...], d3[:rows, :dim]).astype(BF16), n % 2 == 1)
        if n % 2 == 0:
            cores(own, 0)
            cores(own, 1)

    def down_grad(n):
        own = chunks[n][0]
        put_columns(b_i if own else b_e, dim, mm_tn(low[...], slots[4 + n % 2]).astype(BF16), n % 2 == 1)
        if n % 2 == 0:
            cores(own, 2)
            cores(own, 3)
        if n < 2:
            load_ffn(n + 2)
        elif n == 2:
            load(
                "att0",
                (q_h, slots.at[0]),
                (k_h.at[pl.ds(0, SEG)], slots.at[2, pl.ds(0, SEG)]),
                (k_h.at[pl.ds(SEG, SEG)], slots.at[4, pl.ds(0, SEG)]),
                (v_h.at[pl.ds(0, SEG)], slots.at[6, pl.ds(0, SEG)]),
            )
            load_probs(0)
            load_probs(1)
        else:
            left, right = pl.ds(0, width), pl.ds(width, width)
            load(
                "att1",
                (v_h.at[pl.ds(SEG, SEG)], slots.at[1, pl.ds(0, SEG)]),
                (wq_i, slots.at[3, :, left]),
                (wk_i, slots.at[3, :, right]),
                (wv_i, slots.at[5, :, left]),
                (wv_o, slots.at[5, :, right]),
                (wq_o, slots.at[7, :, left]),
                (wk_o, slots.at[7, :, right]),
            )

    pairs = width // PAIR
    pair_order = [pairs + n for n in range(pairs)] + list(range(pairs))

    def load_probs(n):
        pair = pair_order[n]
        load(
            ("p", n),
            (pa_h.at[pl.ds(2 * pair, 2)], p_a.at[n % 2]),
            (pm_h.at[pl.ds(2 * pair, 2)], p_m.at[n % 2]),
        )

    def out_back():
        loaded("mid")
        sums = [0.0, 0.0, 0.0]
        for r in range(0, rows, TILE):
            tile = slice(r, r + TILE)
            grad_in = total[tile]
            n = normed[tile].astype(F32)
            scaled = grad_in * consts[1:2]
            grad = inv[tile] * (
                scaled
                - jnp.mean(scaled, axis=-1, keepdims=True)
                - n * jnp.mean(scaled * n, axis=-1, keepdims=True)
            )
            sums[0] += jnp.sum(grad_in * n, axis=0, keepdims=True)
            sums[1] += jnp.sum(grad_in, axis=0, keepdims=True)
            sums[2] += jnp.sum(grad, axis=0, keepdims=True)
            total[tile] = grad
            low[tile] = grad.astype(BF16)
        for i, value in enumerate(sums):
            for part in range(2):
                cut = slice(part * width, (part + 1) * width)
                vecs[12 + 2 * i + part : 13 + 2 * i + part] = value[:, cut]
                vecs[18 + 2 * i + part : 19 + 2 * i + part] = vec2[i : i + 1, cut]
        total[rows:] = jnp.zeros((half, dim), F32)
        d3[rows:, :width] = jnp.zeros((half, width), BF16)

    def out_grads():
        grads = mm_tn(low[...], ctx[...]).astype(BF16)
        put_rows(b_i, 3, grads[:, :width])
        put_rows(b_e, 3, grads[:, width:])
        cores(False, att_at + 3)
        cores(True, att_at + 3)

    def context_grad():
        dctx[...] = mm_nt(low[...], wo[...]).astype(BF16)

    def attend(n):
        pair = pair_order[n]
        cols = slice(pair * PAIR, (pair + 1) * PAIR)
        local_at = (pair % pairs) * PAIR
        if n == 0:
            loaded("att0")
            loaded("att1")
        loaded(("p", n))
        lane = lax.broadcasted_iota(jnp.int32, (1, PAIR), 1) // HEAD_DIM
        zero = jnp.zeros((), BF16)
        for first, count, key_first, k_slot, v_slot, probs_ref in (
            (0, SEG, 0, 2, 6, p_a),
            (SEG, half, SEG, 4, 1, p_m),
        ):
            q_at = slice(first, first + count)
            ks = slice(key_first, key_first + SEG)
            grad2, query2 = dctx[q_at, cols], slots[0, q_at, cols]
            keys, values = slots[k_slot, :SEG, cols], slots[v_slot, :SEG, cols]
            delta_t = (grad2.astype(F32) * ctx[q_at, cols].astype(F32)).T
            values_grad = keys_grad = query_grad = 0.0
            for h in range(2):
                grad_h = jnp.where(lane == h, grad2, zero)
                query_h = jnp.where(lane == h, query2, zero)
                keys_h = jnp.where(lane == h, keys, zero)
                probs = probs_ref[n % 2, h]
                delta = jnp.sum(delta_t[h * HEAD_DIM : (h + 1) * HEAD_DIM], axis=0, keepdims=True)
                prob_grad = mm_nt(values, grad_h)
                score_grad = (probs.astype(F32) * (prob_grad - delta)).astype(BF16)
                values_grad += mm(probs, grad_h)
                keys_grad += mm(score_grad, query_h)
                query_grad += mm_tn(score_grad, keys_h)
            for part, value, out_at in (
                (0, query_grad * HEAD_DIM**-0.5, q_at),
                (1, keys_grad, ks),
                (2, values_grad, ks),
            ):
                d3[out_at, part * width + local_at : part * width + local_at + PAIR] = value.astype(BF16)
        if n + 2 < 2 * pairs:
            load_probs(n + 2)

    def input_part(own):
        main = 3 if own else 7
        last = slice(0, width) if own else slice(width, 2 * width)
        total[...] += mm_nt(d3[:, : 2 * width], slots[main]) + mm_nt(
            d3[:, 2 * width :], slots[5, :, last]
        )

    def weight_part(own):
        buf = b_i if own else b_e
        grads = mm_tn(x_s[...], d3[...]).astype(BF16)
        for group in range(3):
            put_rows(buf, group, grads[:, group * width : (group + 1) * width])
            cores(own, att_at + group)
        row = y if own else 1 - y
        vecs[pl.ds(8 + row, 1)] = jnp.sum(d3[:rows, :width].astype(F32), axis=0, keepdims=True)
        vecs[pl.ds(10 + row, 1)] = jnp.sum(d3[:, 2 * width :].astype(F32), axis=0, keepdims=True)

    done = []

    def finish():
        top = copies.here(total.at[pl.ds(0, SEG)], top_o)
        top.start()
        done.append(top)
        mid_b[0] = total[rows:].astype(BF16)
        done.append(go(copies.to(mid_b.at[0], mid_r.at[0], c=1 - c)))
        vec_start(0)

    def middle():
        arrived(done[1])
        total[SEG:rows] += mid_r[0].astype(F32)
        mid_b[1] = total[SEG:rows].astype(BF16)

        @pl.when(jnp.logical_not(same))
        def _():
            in_d.start()

    ready_e, ready_i = {}, {}
    clock = 3.0
    for n in range(4):
        step(1.4, inner_grad, n)
        step(1.3, hidden_grad, n)
        step(1.3, up_grad, n)
        step(1.3, down_grad, n)
    step(1.6, out_back)
    step(1.4, out_grads)
    step(1.2, context_grad)
    for n in range(2 * pairs):
        step(2.1, attend, n)
        if n % pairs == pairs - 1:
            own = n > pairs
            if own:
                step(2.8, input_part, own)
                step(3.0, weight_part, own)
            else:
                step(3.0, weight_part, own)
                step(2.8, input_part, own)
    step(0.7, finish)
    when = {}
    for us, body, arguments in work:
        clock += us
        when[(body, *arguments)] = clock
    for k in range(att_at):
        ready = (up_grad, down_grad)[k * CHUNK // dim]
        ready_e[k] = when[ready, 1]
        ready_i[k] = when[ready, 3]
    for n in range(4):
        for ready, own in ((ready_e, False), (ready_i, True)):
            ready[att_at + n] = when[(out_grads,) if n == 3 else (weight_part, own)] + 1.0
    stages = {"y": to_y, "x": to_x, "z": to_z, "fz": from_z, "fx": from_x}
    chunk_order = {k: parts[k] for k in [*range(att_at), att_at + 3, att_at, att_at + 1, att_at + 2]}
    tasks = [
        (time, stages[stage[0]], (k, *stage[1:]))
        for time, stage, k in plan(chunk_order, levels, split, ready_e, ready_i)
    ]
    end = when[(finish,)]
    tasks.append((end + 4.0, middle, ()))
    for n in range(len(near)):
        tasks.append((end + 5.0 + 5.0 * n, vec_next, (n,)))
    tasks.sort(key=lambda t: t[0])
    clock = 3.0
    for us, body, arguments in work:
        while tasks and tasks[0][0] <= clock:
            _, task, its = tasks.pop(0)
            task(*its)
        body(*arguments)
        clock += us
    for _, task, its in tasks:
        task(*its)

    @pl.when(same)
    def _():
        out_here.wait()
        in_o[...] = total[SEG:rows]

    @pl.when(jnp.logical_not(same))
    def _():
        out_d.wait()
        in_d.wait()
        in_o[...] = mid_r[1].astype(F32)

    done[0].wait()
    for copy in every:
        copy.wait_send()
        if id(copy) not in waited:
            copy.wait_recv()


def final_body(pos_ref, sums, top, output, in_mid, out_mid, out_o, in_o, q_o, k_o, v_o, wo_o, up_o, down_o, tmp):
    j = pl.program_id(0)
    dim = up_o.shape[0]
    quarter, width = q_o.shape
    is_mid = jnp.where(pos_ref[2] == 0, j >= 2, j == 0)

    @pl.when(is_mid)
    def _():
        out_o[...] = out_mid[...]
        in_o[...] = in_mid[...]

    @pl.when(jnp.logical_not(is_mid))
    def _():
        out_o[...] = output[...]
        in_o[...] = top[...]

    up_o[...] = sums[0, :dim].astype(F32)
    down_o[...] = sums[0, dim : 2 * dim].astype(F32).T
    for part, ref in enumerate((q_o, k_o, v_o)):
        at = 2 * dim + part * quarter
        ref[...] = sums[0, at : at + quarter].astype(F32)
    row = pl.multiple_of((pos_ref[0] ^ j) * quarter, 16)
    at = 2 * dim + 3 * quarter
    tmp[pl.ds(row, quarter), :] = sums[0, at : at + quarter].astype(F32)

    @pl.when(j == pl.num_programs(0) - 1)
    def _():
        wo_o[...] = tmp[...].T


def shards(
    depth,
    tokens, lengths, buckets, w_query, b_query, w_key, w_value, b_value, w_out, b_out,
    norm1_gain, norm1_bias, w_up, b_up, w_down, b_down, norm2_gain, norm2_bias, cotangent,
):
    ix, ic, iy = (lax.axis_index(a) for a in ("x", "c", "y"))
    pos = jnp.stack([2 * ic + ix, ic, iy]).astype(jnp.int32)
    rows, dim = tokens.shape
    half = rows - SEG
    width = w_query.shape[1]
    units = w_up.shape[1]
    chunk = units // 4
    any_space = pl.BlockSpec(memory_space=pl.ANY)
    in_vmem = pl.BlockSpec(memory_space=pltpu.VMEM)

    table = jnp.concatenate([buckets[:, None], lengths], axis=1).astype(F32)
    info = jnp.stack([jnp.where(iy == 0, table[0], table[2]), table[1]])
    info = jnp.pad(info, ((0, 6), (0, 123)))
    bias = jnp.concatenate([b_query, b_value, b_up]).astype(F32).reshape(-1, width)
    bias = jnp.pad(bias, ((0, -bias.shape[0] % 8), (0, 0)))
    consts = jnp.stack([b_out, norm1_gain, norm1_bias, b_down, norm2_gain, norm2_bias]).astype(F32)
    consts = jnp.pad(consts, ((0, 2), (0, 0)))
    weights = (w_query, w_key, w_value, w_out, w_up, w_down)
    total = rows + half
    square = (rows, dim)
    wide = (rows, units)
    pairs = width // PAIR
    made = [
        shape((total, dim), BF16),
        *[shape(w.shape, BF16) for w in weights],
        shape(square, BF16),
        shape((total, dim), BF16),
        shape((total, dim), BF16),
        shape((4 * pairs, SEG, SEG), BF16),
        shape((4 * pairs, SEG, half), BF16),
        shape(square, BF16),
        shape(square, BF16),
        shape((rows, 1), F32),
        shape(square, BF16),
        *[shape(wide, BF16)] * 4,
        shape(square, F32),
        shape(square, BF16),
        shape(square, BF16),
        shape((3, dim), F32),
    ]
    (
        x, wq_o, wk_o, wv_o, wo_o, wu_o, wd_o, query, keys, values, probs_a, probs_m, ctx, normed1, inverse1, hidden,
        act_i, act_o, slope_i, slope_o, second, low, output, vec2,
    ) = pl.pallas_call(
        forward_body,
        out_shape=made,
        in_specs=[any_space] * 8 + [in_vmem] * 3,
        out_specs=[any_space] * (len(made) - 1) + [in_vmem],
        scratch_shapes=[
            pltpu.VMEM((total, dim), BF16),
            pltpu.VMEM(square, BF16),
            pltpu.VMEM((2, dim, 3 * width), BF16),
            pltpu.VMEM((2 * width, dim), BF16),
            pltpu.VMEM((2, dim, units), BF16),
            pltpu.VMEM((2, units, dim), BF16),
            pltpu.VMEM(square, BF16),
            *[pltpu.VMEM((total, dim), BF16)] * 2,
            pltpu.VMEM((3, 2, SEG, SEG), BF16),
            pltpu.VMEM((3, 2, SEG, half), BF16),
            *[pltpu.VMEM(square, BF16)] * 2,
            pltpu.VMEM((rows, 1), F32),
            pltpu.VMEM(square, BF16),
            pltpu.VMEM(square, F32),
            *[pltpu.VMEM((2, *wide), BF16)] * 2,
            *[pltpu.VMEM(square, BF16)] * 2,
            pltpu.VMEM((rows, 1), F32),
            pltpu.VMEM((SEG, SEG), F32),
            pltpu.VMEM((SEG, half), F32),
            pltpu.VMEM(bias.shape, F32),
            *[pltpu.VMEM(info.shape, F32)] * 2,
            pltpu.SemaphoreType.DMA((48,)),
            pltpu.SemaphoreType.DMA((48,)),
            pltpu.SemaphoreType.DMA((64,)),
            pltpu.SemaphoreType.DMA((2,)),
        ],
        compiler_params=pltpu.CompilerParams(
            collective_id=1, has_side_effects=True, vmem_limit_bytes=VMEM_LIMIT
        ),
        name="forward",
    )(tokens, cotangent, *weights, bias, info, consts)

    levels = depth.bit_length() - 1
    more = max(levels - 2, 0)
    size = 3 * dim
    links = levels + 3
    remote = 8 * (levels + 10) + links + 2
    sums, top, vec, in_mid, out_mid = pl.pallas_call(
        functools.partial(backward_body, depth),
        out_shape=[
            shape((4, size, width), BF16),
            shape((SEG, dim), F32),
            shape((24, width), F32),
            shape((half, dim), F32),
            shape((half, dim), BF16),
        ],
        in_specs=[any_space] * 29 + [in_vmem] * 2,
        out_specs=[any_space] * 2 + [in_vmem] * 3,
        scratch_shapes=[
            *[pltpu.VMEM((rows, dim), BF16)] * 2,
            pltpu.VMEM((8, rows, dim), BF16),
            pltpu.VMEM((rows + half, dim), F32),
            *[pltpu.VMEM((4, size, width), BF16)] * 2,
            *[pltpu.VMEM((2, size, width), BF16)] * 3,
            pltpu.VMEM((size, width), BF16),
            pltpu.VMEM((size // 2, width), BF16),
            pltpu.VMEM((size // 4, width), BF16),
            pltpu.VMEM((max(more, 1), size // 4 if more else 16, width), BF16),
            pltpu.VMEM((rows, dim), BF16),
            pltpu.VMEM((rows, 1), F32),
            *[pltpu.VMEM((rows, dim), BF16)] * 3,
            pltpu.VMEM((rows + half, dim), BF16),
            pltpu.VMEM((2, 2, SEG, SEG), BF16),
            pltpu.VMEM((2, 2, SEG, half), BF16),
            pltpu.VMEM((rows + half, 3 * width), BF16),
            pltpu.VMEM((24, width), F32),
            pltpu.VMEM((2 * links, 24, width), F32),
            pltpu.VMEM((2, half, dim), BF16),
            pltpu.VMEM((2, half, dim), BF16),
            pltpu.SemaphoreType.DMA((remote,)),
            pltpu.SemaphoreType.DMA((remote,)),
            pltpu.SemaphoreType.DMA((64,)),
            pltpu.SemaphoreType.DMA((4,)),
        ],
        compiler_params=pltpu.CompilerParams(
            collective_id=2, has_side_effects=True, vmem_limit_bytes=VMEM_LIMIT
        ),
        name="backward",
    )(
        low, hidden, act_i, act_o, slope_i, slope_o, w_up, wu_o, w_down, wd_o, second, normed1, inverse1,
        w_out, wo_o, ctx, x, query, keys, values, probs_a, probs_m, w_query, w_key, w_value, wq_o, wk_o, wv_o,
        output, consts, vec2,
    )
    quarter = dim // 4
    b_up_grad = lax.dynamic_slice_in_dim(vec, 4 * iy, 4).reshape(units)
    b_query_grad = lax.dynamic_slice_in_dim(vec, 8 + iy, 1)[0]
    b_value_grad = lax.dynamic_slice_in_dim(vec, 10 + iy, 1)[0]
    rest = vec[12:].reshape(6, dim)
    const = lambda *dims: pl.BlockSpec(dims, lambda j, pos: (0,) * len(dims))
    full_block = lambda j, pos: (jnp.where(pos[2] == 0, jnp.minimum(j, 1), jnp.clip(j - 1, 0, 1)), 0)
    row_block = pl.BlockSpec((half, dim), lambda j, pos: (jnp.minimum(j, 2), 0))
    by_rows = lambda n, m: pl.BlockSpec((n, m), lambda j, pos: (pos[0] ^ j, 0))
    output, input_grad, w_query_grad, w_key_grad, w_value_grad, w_out_grad, w_up_grad, w_down_grad = call(
        final_body,
        (4,),
        pos,
        [sums, top, output, in_mid, out_mid],
        [
            pl.BlockSpec((1, size, width), lambda j, pos: (j, 0, 0)),
            pl.BlockSpec((half, dim), full_block),
            pl.BlockSpec((half, dim), full_block),
            whole(in_mid),
            whole(out_mid),
        ],
        [
            shape((rows, dim), BF16),
            shape((rows, dim), F32),
            *[shape((dim, width), F32)] * 3,
            shape((width, dim), F32),
            shape((dim, units), F32),
            shape((units, dim), F32),
        ],
        [
            row_block,
            row_block,
            *[by_rows(quarter, width)] * 3,
            const(width, dim),
            pl.BlockSpec((dim, chunk), lambda j, pos: (0, pos[0] ^ j)),
            by_rows(chunk, dim),
        ],
        [pltpu.VMEM((dim, width), F32)],
        0,
        "final",
    )
    return (
        output,
        input_grad,
        w_query_grad,
        b_query_grad,
        w_key_grad,
        w_value_grad,
        b_value_grad,
        w_out_grad,
        rest[2],
        rest[0],
        rest[1],
        w_up_grad,
        b_up_grad,
        w_down_grad,
        rest[5],
        rest[3],
        rest[4],
    )


def solution(mesh):
    depth = mesh.shape["dp"] // 4
    inner = Mesh(mesh.devices.reshape(depth, 2, 2, mesh.shape["mp"]), ("z", "x", "c", "y"))
    dp = ("z", "x", "c")
    every = (*dp, "y")
    placed = (
        P(every, None),
        P(dp, None),
        P(dp),
        P(None, "y"),
        P("y"),
        P(None, "y"),
        P(None, "y"),
        P("y"),
        P("y", None),
        P(),
        P(),
        P(),
        P(None, "y"),
        P("y"),
        P("y", None),
        P(),
        P(),
        P(),
        P(every, None),
    )
    return jax.shard_map(
        functools.partial(shards, depth),
        mesh=inner,
        in_specs=placed,
        out_specs=(
            P(every, None),
            P(every, None),
            P(None, "y"),
            P("y"),
            P(None, "y"),
            P(None, "y"),
            P("y"),
            P("y", None),
            P(),
            P(),
            P(),
            P(None, "y"),
            P("y"),
            P("y", None),
            P(),
            P(),
            P(),
        ),
        check_vma=False,
    )
```

```python
import functools

import jax
import jax.numpy as jnp
from jax import lax
from jax.experimental import pallas as pl
from jax.experimental.pallas import tpu as pltpu
from jax.sharding import Mesh, PartitionSpec as P

HEAD_DIM = 64
SEG = 512
PAIR = 2 * HEAD_DIM
NEG = -1e30
EPS = 1e-12
ROOT_HALF = 0.7071067811865476
INV_ROOT_TWO_PI = 0.3989422804014327
F32 = jnp.float32
BF16 = jnp.bfloat16
VMEM_LIMIT = 60 * 1024 * 1024
TILE = 256
CHUNK = 192
MESH_IDS = pl.DeviceIdType.MESH


def mm(left, right):
    return lax.dot_general(left, right, (((1,), (0,)), ((), ())), preferred_element_type=F32)


def mm_nt(left, right):
    return lax.dot_general(left, right, (((1,), (1,)), ((), ())), preferred_element_type=F32)


def mm_tn(left, right):
    return lax.dot_general(left, right, (((0,), (0,)), ((), ())), preferred_element_type=F32)


def call(body, grid, pos, inputs, in_specs, out_shape, out_specs, scratch, flops, name):
    moved = sum(v.size * v.dtype.itemsize for v in inputs) + sum(
        v.size * v.dtype.itemsize for v in out_shape
    )
    return pl.pallas_call(
        body,
        grid_spec=pltpu.PrefetchScalarGridSpec(
            num_scalar_prefetch=1,
            grid=grid,
            in_specs=in_specs,
            out_specs=out_specs,
            scratch_shapes=scratch,
        ),
        out_shape=out_shape,
        compiler_params=pltpu.CompilerParams(
            dimension_semantics=("arbitrary",) * len(grid), vmem_limit_bytes=VMEM_LIMIT
        ),
        cost_estimate=pl.CostEstimate(flops=flops, bytes_accessed=moved, transcendentals=0),
        name=name,
    )(pos, *inputs)


def whole(array):
    zeros = (0,) * array.ndim
    return pl.BlockSpec(array.shape, lambda j, pos: zeros)


def shape(dims, kind):
    return jax.ShapeDtypeStruct(dims, kind)


def gelu_parts(inner):
    erf = lax.erf(inner * ROOT_HALF)
    below = 0.5 + 0.5 * erf
    density = jnp.exp(inner * inner * -0.5) * INV_ROOT_TWO_PI
    return inner * below, below + inner * density


def row_ids(info, at, places):
    bucket = info[at : at + 1, 0:1]
    span = jnp.where(bucket < 0.5, 1.0 * SEG, jnp.where(bucket < 1.5, 0.5 * SEG, 0.25 * SEG))
    row = jnp.zeros_like(places)
    size = jnp.zeros_like(places) + info[at : at + 1, 1:2]
    for slot in range(1, 4):
        later = places >= span * slot
        row = jnp.where(later, 1.0 * slot, row)
        size = jnp.where(later, info[at : at + 1, slot + 1 : slot + 2], size)
    return row, places - row * span < size


def wide_row(ref, row):
    return jnp.concatenate([ref[row : row + 1], ref[row + 1 : row + 2]], axis=1)


class Copies:
    def __init__(self, send, recv, local):
        self.send, self.recv, self.local = send, recv, local
        self.remote_count = self.local_count = 0

    def to(self, src, dst, **device):
        n = self.remote_count
        self.remote_count += 1
        return pltpu.make_async_remote_copy(
            src_ref=src,
            dst_ref=dst,
            send_sem=self.send.at[n],
            recv_sem=self.recv.at[n],
            device_id=device,
            device_id_type=MESH_IDS,
        )

    def here(self, src, dst):
        n = self.local_count
        self.local_count += 1
        return pltpu.make_async_copy(src, dst, self.local.at[n])


def coords():
    return tuple(lax.axis_index(a) for a in ("z", "x", "c", "y"))


def greet(devices):
    barrier = pltpu.get_barrier_semaphore()
    for device in devices:
        pl.semaphore_signal(barrier, inc=1, device_id=device, device_id_type=MESH_IDS)
    pl.semaphore_wait(barrier, len(devices))


def forward_body(
    tokens, cot_h, wq, wk, wv, wo, wu, wd, b_q, b_v, b_u, b_o, gain1, bias1, b_d, gain2, bias2, buckets, lengths,
    x_o, wq_o, wk_o, wv_o, wo_o, wu_o, wd_o, q_o, k_o, v_o, pa_o, pm_o, ctx_o, normed_o, inv_o, hidden_o,
    act_io, act_oo, slope_io, slope_oo, second_o, low_o, out_o, vec_o,
    x_s, cot, w3, wo_s, wu_s, wd_s, q_s, k_s, v_s, p_a, p_m, ctx, normed, inv, hidden, acc, act, slope, low, out_s,
    keep, mask_a, mask_m, bias, info, bias_r, info_r, info_s, send, recv, local, crossed,
):
    z, x, c, y = coords()
    copies = Copies(send, recv, local)
    rows, dim = cot.shape
    shared = 2 + wu.shape[1] // wq.shape[1]

    def const(n):
        return wide_row(bias, shared + 2 * n)

    half = rows - SEG
    width = wq.shape[1]
    pairs = width // PAIR
    same = c == y
    full = pl.ds(pl.multiple_of(y * half, half), SEG)
    mid = pl.ds(pl.multiple_of((1 - y) * SEG, half), half)
    own_at, sib_at = pl.ds(SEG, half), pl.ds(SEG + half, half)
    loads, stores = {}, []

    def load(name, *moves):
        loads[name] = [copies.here(src, dst) for src, dst in moves]
        for copy in loads[name]:
            copy.start()

    def loaded(name):
        for copy in loads.pop(name, ()):
            copy.wait()

    def store(src, dst):
        copy = copies.here(src, dst)
        copy.start()
        stores.append(copy)
        return copy

    load(
        "qkv",
        (tokens.at[full], x_s.at[pl.ds(0, SEG)]),
        *[(w, w3.at[0, :, pl.ds(n * width, width)]) for n, w in enumerate((wq, wk, wv))],
    )
    x_own = copies.here(tokens.at[mid], x_s.at[own_at])
    cot_own = copies.here(cot_h.at[mid], cot.at[own_at])

    @pl.when(same)
    def _():
        x_own.start()
        cot_own.start()

    row = 0
    for ref in (b_q, b_v, b_u, b_o, gain1, bias1, b_d, gain2, bias2):
        for n in range(ref.shape[0] // width):
            bias[row : row + 1] = ref[n * width : (n + 1) * width].astype(F32).reshape(1, width)
            row += 1
    bias[row:] = jnp.zeros((bias.shape[0] - row, width), F32)
    lane = lax.broadcasted_iota(jnp.int32, (1, info.shape[1]), 1)
    info[...] = jnp.zeros_like(info)
    for n, block in enumerate((2 * y, 1)):
        value = jnp.where(lane == 0, buckets[block], 0)
        for slot in range(4):
            value = jnp.where(lane == slot + 1, lengths[block, slot], value)
        info[n : n + 1] = value.astype(F32)
    greet([{"y": 1 - y}, {"x": 1 - x}, {"c": 1 - c}, {"z": z + 1 - 2 * (z % 2)}, {"c": 1 - c, "y": 1 - y}])

    x_y = copies.to(tokens.at[mid], x_s.at[sib_at], y=1 - y)
    x_c1 = copies.to(x_s.at[own_at], x_s.at[sib_at], c=1 - c)
    x_c2 = copies.to(x_s.at[sib_at], x_s.at[own_at], c=1 - c)
    cot_d = pltpu.make_async_remote_copy(
        src_ref=cot_h.at[mid], dst_ref=cot.at[own_at], send_sem=crossed.at[0], recv_sem=crossed.at[1],
        device_id={"c": 1 - c, "y": 1 - y}, device_id_type=MESH_IDS,
    )
    info_copy = copies.to(info, info_r, c=1 - c)
    bias_copy = copies.to(bias, bias_r, y=1 - y)

    @pl.when(jnp.logical_not(same))
    def _():
        x_y.start()

    info_copy.start()
    bias_copy.start()

    z_next = z + 1 - 2 * (z % 2)
    zb = z % 2

    def rows_of(ref, first, count, part, columns=None):
        def cut(x_at, z_at, sub=0, subs=1):
            n = count // 2 // subs
            row = first + (2 * c + x_at) * part + z_at * (count // 2) + sub * n
            at = pl.ds(pl.multiple_of(row, 16), n)
            return ref.at[at] if columns is None else ref.at[at, columns]

        return cut

    def columns_of(ref, first, count):
        def cut(x_at, z_at, sub=0, subs=1):
            n, m = ref.shape[1] // 4, count // 2 // subs
            row = pl.multiple_of(first + z_at * (count // 2) + sub * m, 16)
            return ref.at[pl.ds(row, m), pl.ds(pl.multiple_of((2 * c + x_at) * n, 128), n)]

        return cut

    arrays = []
    part = dim // 4
    for n, w in enumerate((wq, wk, wv)):
        cols = pl.ds(n * width, width)
        arrays.append(("qkv", 1.6, rows_of(w, 0, part, part), rows_of(w3.at[1], 0, part, part, cols)))
    part = width // 4
    arrays.append(("wo", 1.6, rows_of(wo, 0, part, part), rows_of(wo_s, width, part, part)))
    for n in range(2):
        arrays.append(("wu", 3.1, columns_of(wu, n * dim // 2, dim // 2), columns_of(wu_s.at[1], n * dim // 2, dim // 2)))
    part = wd.shape[0] // 4
    for n in range(2):
        first = n * part // 2
        arrays.append(("wd", 3.1, rows_of(wd, first, part // 2, part), rows_of(wd_s.at[1], first, part // 2, part)))
    over = {}

    def pass_on(n, hop, cut, **device):
        over[n, hop] = copies.to(cut, cut, **device)
        over[n, hop].start()

    def from_y(n):
        over[n, "y"].wait_recv()
        cut = arrays[n][3](x, zb)
        pass_on(n, "x", cut, x=1 - x)
        pass_on(n, "z", cut, z=z_next)
        pass_on(n, "cy", cut, c=1 - c)

    def halves(n):
        return 1 if arrays[n][0] == "wo" else 2

    def from_x(n):
        over[n, "x"].wait_recv()
        if halves(n) == 2:
            pass_on(n, "xz", arrays[n][3](1 - x, zb, 1, 2), z=z_next)
        pass_on(n, "cx", arrays[n][3](1 - x, zb), c=1 - c)

    def from_z(n):
        over[n, "z"].wait_recv()
        pass_on(n, "zx", arrays[n][3](x, 1 - zb, 0, halves(n)), x=1 - x)
        pass_on(n, "cz", arrays[n][3](x, 1 - zb), c=1 - c)

    def from_both(n):
        over[n, "zx"].wait_recv()
        if halves(n) == 2:
            over[n, "xz"].wait_recv()
        pass_on(n, "cb", arrays[n][3](1 - x, 1 - zb), c=1 - c)

    def mid_rows():
        @pl.when(same)
        def _():
            x_own.wait()
            x_y.wait_recv()
            x_c1.start()
            x_c2.start()

    tasks = [(8.0, mid_rows, ())]
    clock = 2.0 + 4.1
    hop = 0.0
    for n, array in enumerate(arrays):
        clock += array[1]
        first = clock + 2.0
        hop = max(hop, first) + array[1] * 1.5
        tasks.append((first, from_y, (n,)))
        tasks.append((hop - array[1] * 0.5 + 2.0, from_x, (n,)))
        tasks.append((hop - array[1] * 0.5 + 2.0, from_z, (n,)))
        tasks.append((hop + 4.0, from_both, (n,)))
        over[n, "y"] = copies.to(array[2](x, zb), array[3](x, zb), y=1 - y)
        over[n, "y"].start()
    tasks.sort(key=lambda t: t[0])

    @pl.when(jnp.logical_not(same))
    def _():
        cot_d.start()

    come = set()

    def run_until(time):
        while tasks and tasks[0][0] <= time:
            _, task, its = tasks.pop(0)
            task(*its)

    def need(name):
        if name in come:
            return
        come.add(name)
        while any(its and arrays[its[0]][0] == name for _, task, its in tasks):
            _, task, its = tasks.pop(0)
            task(*its)
        for n, array in enumerate(arrays):
            if array[0] == name:
                for hop in ("cy", "cx", "cz", "cb"):
                    over[n, hop].wait_recv()

    load("wo", (wo, wo_s.at[pl.ds(0, width)]))
    load("wu", (wu, wu_s.at[0]))
    load("wd", (wd, wd_s.at[0]))
    load("cot", (cot_h.at[full], cot.at[pl.ds(0, SEG)]))

    work = []

    def step(us, body, *arguments):
        work.append((us, body, arguments))

    now = [2.0]

    def poll(us):
        now[0] += us
        run_until(now[0])

    def mask_of(mask, at, count):
        places = lax.broadcasted_iota(jnp.int32, (SEG, 1), 0)
        across = lax.broadcasted_iota(jnp.int32, (1, count), 1)
        if at == 1:
            places = (places + half * c) % SEG
            across = across + half * c
        key_row, valid = row_ids(info_s, at, places.astype(F32))
        query_row, _ = row_ids(info_s, at, across.astype(F32))
        allowed = jnp.where(valid, key_row, -1.0) == query_row
        mask[...] = jnp.where(allowed, 0.0, NEG)
        keep[at * SEG : at * SEG + count] = jnp.where(valid[:count], 1.0, 0.0)

    def project(other, first, count):
        if not other and first == 0:
            loaded("qkv")
            info_s[...] = info[...]
            mask_of(mask_a, 0, SEG)
        if not other and first == SEG:
            info_copy.wait_recv()
            info_s[...] = jnp.where(same, info[...], info_r[...])
            mask_of(mask_m, 1, half)

            @pl.when(jnp.logical_not(same))
            def _():
                x_c1.wait_recv()
                x_c2.wait_recv()

            store(x_s, x_o)
        if other:
            bias_copy.wait_recv()
            need("qkv")
            for n, w in enumerate((wq_o, wk_o, wv_o)):
                store(w3.at[1, :, pl.ds(n * width, width)], w)
        vector = bias_r if other else bias
        cols = slice(width, 2 * width) if other else slice(0, width)
        for r in range(first, first + count, TILE):
            at = slice(r, r + TILE)
            qkv = mm(x_s[at], w3[1 if other else 0])
            if r < rows:
                q_s[at, cols] = ((qkv[:, :width] + vector[0:1]) * HEAD_DIM**-0.5).astype(BF16)
            k_s[at, cols] = qkv[:, width : 2 * width].astype(BF16)
            v_s[at, cols] = (qkv[:, 2 * width :] + vector[1:2]).astype(BF16)
            poll(0.6)

    used = {}

    def attend(pair, middle):
        first, count, mask, probs, out = (SEG, half, mask_m, p_m, pm_o) if middle else (0, SEG, mask_a, p_a, pa_o)
        at = slice(first, first + count)
        ks = slice(first, first + SEG)
        cols = slice(pair * PAIR, (pair + 1) * PAIR)
        s = pair % 3
        if (middle, s) in used:
            used[middle, s].wait()
        lane = lax.broadcasted_iota(jnp.int32, (1, PAIR), 1) // HEAD_DIM
        query, keys = q_s[at, cols], k_s[ks, cols]
        values_t = v_s[ks, cols].astype(F32).T.astype(BF16)
        parts = []
        for h in range(2):
            query_h = jnp.where(lane == h, query, jnp.zeros((), BF16))
            scores = mm_nt(keys, query_h) + mask[...]
            top = jnp.max(scores, axis=0, keepdims=True)
            grown = jnp.exp(scores - top)
            prob = (grown * (1.0 / jnp.sum(grown, axis=0, keepdims=True))).astype(BF16)
            probs[s, h] = prob
            parts.append(mm(values_t[h * HEAD_DIM : (h + 1) * HEAD_DIM], prob))
            if h == 0:
                poll(0.4 if middle else 0.75)
        ctx[at, cols] = jnp.concatenate(parts, axis=0).T.astype(BF16)
        used[middle, s] = copies.here(probs.at[s], out.at[pl.ds(2 * pair, 2)])
        used[middle, s].start()

    def stored_qkv():
        for src, dst in ((q_s, q_o), (k_s, k_o), (v_s, v_o), (ctx, ctx_o)):
            store(src, dst)

    def normalize(value):
        centre = value - jnp.mean(value, axis=-1, keepdims=True)
        inverse = lax.rsqrt(jnp.mean(centre * centre, axis=-1, keepdims=True) + EPS)
        return centre * inverse, inverse

    def first_norm():
        loaded("wo")
        need("wo")
        store(wo_s.at[pl.ds(width, width)], wo_o)
        for r in range(0, rows, TILE):
            at = slice(r, r + TILE)
            poll(0.8)
            normal, inverse = normalize(x_s[at].astype(F32) + mm(ctx[at], wo_s[...]) + const(0))
            normed[at] = normal.astype(BF16)
            inv[at] = inverse
            hidden[at] = (normal * const(1) + const(2)).astype(BF16)
        store(normed, normed_o)
        store(inv, inv_o)
        store(hidden, hidden_o)

    def up(other, h):
        if h == 0:
            if other:
                need("wu")
                store(wu_s.at[1], wu_o)
            else:
                loaded("wu")
        s = 1 if other else 0
        vector = bias_r if other else bias
        cols = slice(h * dim, (h + 1) * dim)
        shift = wide_row(vector, 2 + 2 * h)
        for r in range(0, rows, TILE):
            at = slice(r, r + TILE)
            active, steep = gelu_parts(mm(hidden[at], wu_s[s, :, cols]) + shift)
            act[s, at, cols] = active.astype(BF16)
            slope[s, at, cols] = steep.astype(BF16)
            poll(0.75)
        if h == 1:
            store(act.at[s], act_oo if other else act_io)
            store(slope.at[s], slope_oo if other else slope_io)

    def down(other):
        if other:
            need("wd")
            store(wd_s.at[1], wd_o)
        else:
            loaded("wd")
        for r in range(0, rows, TILE):
            at = slice(r, r + TILE)
            if other:
                acc[at] += mm(act[1, at], wd_s[1])
            else:
                acc[at] = mm(act[0, at], wd_s[0])
            poll(0.75)

    def second_norm():
        loaded("cot")

        @pl.when(same)
        def _():
            cot_own.wait()

        @pl.when(jnp.logical_not(same))
        def _():
            cot_d.wait_recv()

        sums = [0.0, 0.0, 0.0]
        for r in range(0, rows, TILE):
            at = slice(r, r + TILE)
            normal, inverse = normalize(hidden[at].astype(F32) + acc[at] + const(3))
            g = const(4)
            out_s[at] = ((normal * g + const(5)) * keep[at]).astype(BF16)
            upstream = cot[at].astype(F32) * keep[at]
            scaled = upstream * g
            grad = inverse * (
                scaled
                - jnp.mean(scaled, axis=-1, keepdims=True)
                - normal * jnp.mean(scaled * normal, axis=-1, keepdims=True)
            )
            acc[at] = grad
            low[at] = grad.astype(BF16)
            sums[0] += jnp.sum(upstream * normal, axis=0, keepdims=True)
            sums[1] += jnp.sum(upstream, axis=0, keepdims=True)
            sums[2] += jnp.sum(grad, axis=0, keepdims=True)
        for i, value in enumerate(sums):
            vec_o[i : i + 1] = value
        for src, dst in ((acc, second_o), (low, low_o), (out_s, out_o)):
            store(src, dst)

    step(1.5, project, False, 0, SEG)
    for pair in range(pairs):
        step(1.4, attend, pair, False)
    step(1.8, project, False, SEG, SEG)
    for pair in range(pairs):
        step(0.7, attend, pair, True)
    step(2.4, project, True, 0, rows + half)
    for pair in range(pairs, 2 * pairs):
        step(1.4, attend, pair, False)
        step(0.7, attend, pair, True)
    step(0.2, stored_qkv)
    step(2.5, first_norm)
    step(2.2, up, False, 0)
    step(2.2, up, False, 1)
    step(2.2, down, False)
    step(2.2, up, True, 0)
    step(2.2, up, True, 1)
    step(2.2, down, True)
    step(2.0, second_norm)
    starts = {(project, False, SEG, SEG): 10.5, (project, True, 0, rows + half): 19.0, (up, True, 0): 31.0, (down, True): 38.0}
    clock = 2.0
    for us, body, arguments in work:
        clock = max(clock, starts.get((body, *arguments), 0.0))
        run_until(clock)
        now[0] = clock
        body(*arguments)
        clock += us
    run_until(1e9)

    @pl.when(same)
    def _():
        x_c1.wait_send()
        x_c2.wait_send()

    @pl.when(jnp.logical_not(same))
    def _():
        x_y.wait_send()
        cot_d.wait_send()

    info_copy.wait_send()
    bias_copy.wait_send()
    for copy in over.values():
        copy.wait_send()
    for copy in stores + list(used.values()):
        copy.wait()


LINK_US = 6.2 / 384


def plan(parts, levels, split, ready_e, ready_i):
    free = {"y": 0.0, "x": 0.0, "z": 0.0, "far": 0.0}
    after = ["x"] + [("z", n) for n in range(levels)] + [("fz", n) for n in range(split - 1, -1, -1)] + ["fx"]
    link_of = {"y": "y", "x": "x", "fx": "x"}
    for n in range(levels):
        link_of["z", n] = link_of["fz", n] = "z" if n == 0 else "far"
    order = []
    ready = [(ready_e[k], "y", n, k) for n, k in enumerate(parts)]
    while ready:

        def key(item):
            back = item[1] == "fx" or item[1][0] == "fz"
            return max(item[0], free[link_of[item[1]]]), back, item[2]

        item = min(ready, key=key)
        ready.remove(item)
        time, stage, n, k = item
        start = key(item)[0]
        us = parts[k] * LINK_US * {"y": 2.0, "x": 1.0, "fx": 1.0}.get(stage, 0.5)
        free[link_of[stage]] = start + us
        order.append((start, stage, k))
        come = start + us + 2.0
        if stage == "y":
            ready.append((max(come, ready_i[k]), after[0], n, k))
        elif stage != "fx":
            ready.append((come, after[after.index(stage) + 1], n, k))
        else:
            order.append((come, "end", k))
    return sorted(order, key=lambda v: v[0])


def backward_body(
    depth,
    low_h, hidden_h, act_i, act_o, slope_i, slope_o, wu_i, wu_o, wd_i, wd_o, second_h, normed_h, inv_h,
    wo_i, wo_o, ctx_h, x_h, q_h, k_h, v_h, pa_h, pm_h, wq_i, wk_i, wv_i, wq_o, wk_o, wv_o, output_h, gain, vec2,
    sums_o, top_o, vec_o, in_o, out_o,
    low, hidden, slots, total, b_e, b_i, c_e, c_i, y_r, x_r, z_a, z_b, zx_r, normed, inv, wo, ctx, dctx, x_s,
    p_a, p_m, d3, vecs, vec_r, mid_r, send, recv, local, crossed,
):
    z, x, c, y = coords()
    copies = Copies(send, recv, local)
    steps = []
    while 2 ** len(steps) < depth:
        steps.append(2 ** len(steps))
    levels = len(steps)
    split = min(2, levels)
    bits = [(z // s) % 2 for s in steps]
    z_partner = [z + s - 2 * s * b for s, b in zip(steps, bits)]
    near = [{"c": 1 - c}, {"y": 1 - y}, {"x": 1 - x}] + [{"z": p} for p in z_partner]
    same = c == y
    rows, dim = low.shape
    half = rows - SEG
    width = b_e.shape[2]
    quarter = dim // 4
    ffn_rows = 2 * dim
    first_row, parts = {}, {}
    ffn_chunks = ffn_rows // CHUNK
    for n in range(ffn_chunks):
        first_row[n], parts[n] = n * CHUNK, CHUNK
    qkv_chunks, out_chunks = [], []
    row = ffn_rows
    while row < ffn_rows + 4 * quarter:
        end = ffn_rows + (3 if row < ffn_rows + 3 * quarter else 4) * quarter
        n = len(parts)
        first_row[n], parts[n] = row, min(128, end - row)
        (qkv_chunks if row < ffn_rows + 3 * quarter else out_chunks).append(n)
        row += parts[n]
    every, waited = [], set()

    def at(k):
        return pl.ds(first_row[k], parts[k])

    def go(copy):
        copy.start()
        every.append(copy)
        return copy

    def arrived(copy):
        copy.wait_recv()
        waited.add(id(copy))

    loads = {}

    def load(name, *pairs):
        loads[name] = [copies.here(src, dst) for src, dst in pairs]
        for copy in loads[name]:
            copy.start()

    def loaded(name):
        for copy in loads.pop(name, ()):
            copy.wait()

    chunks = [(False, 1 - c), (False, c), (True, 1 - c), (True, c)]

    def load_ffn(n, kind):
        own, h = chunks[n]
        cut = pl.ds(pl.multiple_of(h * dim, 128), dim)
        refs = {"wu": (wu_i, wu_o), "wd": (wd_i, wd_o), "act": (act_i, act_o), "slope": (slope_i, slope_o)}
        ref = refs[kind][0 if own else 1]
        slot_at = 2 * ("wu", "wd", "act", "slope").index(kind) + n % 2
        load((kind, n), (ref.at[cut] if kind == "wd" else ref.at[:, cut], slots.at[slot_at]))

    load("low", (low_h, low))
    load_ffn(0, "act")
    load_ffn(1, "act")
    load_ffn(0, "wd")
    load_ffn(0, "slope")
    load("hidden", (hidden_h, hidden))
    load_ffn(1, "wd")
    load_ffn(1, "slope")
    load("second", (second_h, total.at[pl.ds(0, rows)]))
    load_ffn(0, "wu")
    load_ffn(1, "wu")
    greet(near + [{"c": 1 - c, "y": 1 - y}])

    out_d = pltpu.make_async_remote_copy(
        src_ref=output_h.at[pl.ds(SEG, half)], dst_ref=out_o, send_sem=crossed.at[0], recv_sem=crossed.at[1],
        device_id={"c": 1 - c, "y": 1 - y}, device_id_type=MESH_IDS,
    )
    mid_b = [slots.at[0, pl.ds(n * half, half)] for n in range(2)]
    in_d = pltpu.make_async_remote_copy(
        src_ref=mid_b[1], dst_ref=in_o, send_sem=crossed.at[2], recv_sem=crossed.at[3],
        device_id={"c": 1 - c, "y": 1 - y}, device_id_type=MESH_IDS,
    )

    load("mid", (wo_i, wo.at[pl.ds(0, width)]), (wo_o, wo.at[pl.ds(width, width)]), (ctx_h, ctx), (normed_h, normed), (inv_h, inv), (x_h, x_s))

    def add(n, out, *ins):
        tile = next(t for t in (48, 32, 16) if n % t == 0)

        def step(i, _):
            rows_at = pl.ds(pl.multiple_of(i * tile, 16), tile)
            value = ins[0][rows_at].astype(F32)
            for other in ins[1:]:
                value = value + other[rows_at].astype(F32)
            out[rows_at] = value.astype(out.dtype)
            return 0

        lax.fori_loop(0, n // tile, step, 0)

    def add2(n, out, *ins):
        for part in range(2):
            add(n, out.at[part], *[v.at[part] for v in ins])

    got_e, got_i, got_y, got_x, got_z, back_z, put, got_bx = {}, {}, {}, {}, {}, {}, {}, {}

    def cores(own, k):
        buf, there, got = (b_i, c_i, got_i) if own else (b_e, c_e, got_e)
        got[k] = go(copies.to(buf.at[pl.ds(2, 2), at(k)], there.at[:, at(k)], c=1 - c))

    def to_y(k):
        arrived(got_e[k])
        mine = b_e.at[pl.ds(0, 2), at(k)]
        add2(parts[k], mine, mine, c_e.at[:, at(k)])
        got_y[k] = go(copies.to(mine, y_r.at[:, at(k)], y=1 - y))

    def to_x(k):
        arrived(got_i[k])
        arrived(got_y[k])
        mine = b_i.at[pl.ds(0, 2), at(k)]
        add2(parts[k], mine, mine, c_i.at[:, at(k)], y_r.at[:, at(k)])
        got_x[k] = go(copies.to(b_i.at[1, at(k)], x_r.at[at(k)], x=1 - x))

    def base(k, level):
        row, size = first_row[k], parts[k]
        for n in range(min(level, split)):
            size //= 2
            row = row + bits[n] * size
        return row, size

    def slot(k, level):
        cut = 2 ** (level + 1)
        return (z_a, z_b)[level].at[pl.ds(first_row[k] // cut, parts[k] // cut)]

    def extra(k, n):
        return zx_r.at[n, pl.ds(first_row[k] // 4, parts[k] // 4)]

    def to_z(k, level):
        row, size = base(k, level)
        mine = b_i.at[0, pl.ds(pl.multiple_of(row, 16), size)]
        if level == 0:
            arrived(got_x[k])
            add(size, mine, mine, x_r.at[at(k)])
        else:
            if level > split:
                got_z[k, level - 1].wait()
            else:
                arrived(got_z[k, level - 1])
            add(size, mine, mine, slot(k, level - 1) if level <= split else extra(k, level - 1 - split))
        if level < split:
            size //= 2
            out = b_i.at[0, pl.ds(pl.multiple_of(row + (1 - bits[level]) * size, 16), size)]
            got_z[k, level] = go(copies.to(out, slot(k, level), z=z_partner[level]))
        elif level < levels:
            got_z[k, level] = copies.to(mine, extra(k, level - split), z=z_partner[level])
            got_z[k, level].start()
        else:
            place = sums_o.at[0, pl.ds(pl.multiple_of(row, 16), size)]
            put[k] = copies.here(mine, place)
            put[k].start()
            if split:
                back_z[k, split - 1] = go(copies.to(mine, place, z=z_partner[split - 1]))

    def from_z(k, level):
        if level == max(split, 1) - 1:
            put[k].wait()
        if split:
            arrived(back_z[k, level])
        if level > 0:
            row, size = base(k, level)
            place = sums_o.at[0, pl.ds(pl.multiple_of(row, 16), size)]
            back_z[k, level - 1] = go(copies.to(place, place, z=z_partner[level - 1]))
        else:
            mine = sums_o.at[0, at(k)]
            got_bx[k] = go(copies.to(mine, sums_o.at[1, at(k)], x=1 - x))
            go(copies.to(mine, sums_o.at[2, at(k)], c=1 - c))

    def from_x(k):
        arrived(got_bx[k])
        go(copies.to(sums_o.at[1, at(k)], sums_o.at[3, at(k)], c=1 - c))

    vec_copies = {}

    def vec_start(n):
        source = vecs if n == 0 else vec_r.at[2 * n - 1]
        vec_copies[n] = go(copies.to(source, vec_r.at[2 * n], **near[n]))

    def vec_next(n):
        arrived(vec_copies[n])
        value = (vecs if n == 0 else vec_r.at[2 * n - 1])[...] + vec_r[2 * n]
        if n == len(near) - 1:
            vec_o[...] = value
        else:
            vec_r[2 * n + 1] = value
            vec_start(n + 1)

    work = []

    def step(us, body, *arguments):
        work.append((us, body, arguments))

    now = [3.0]

    def run_until(time):
        while tasks and tasks[0][0] <= time:
            _, task, its = tasks.pop(0)
            task(*its)

    def poll(us):
        now[0] += us
        run_until(now[0])

    def put_columns(buf, row, left, right, keep):
        for r in range(0, dim, TILE):
            grads = mm_tn(left[:, r : r + TILE], right[...]).astype(BF16)
            for part in range(2):
                rel = (0 if keep else 2) + (part + x) % 2
                buf[rel, row + r : row + r + TILE] = grads[:, part * width : (part + 1) * width]
            poll(0.45)

    def put_rows(buf, group, p, grads):
        rel = 2 * ((p // 2 + c) % 2) + (p % 2 + x) % 2
        buf[rel, ffn_rows + group * quarter : ffn_rows + (group + 1) * quarter] = grads

    inner_at = (d3.at[pl.ds(0, rows), pl.ds(0, dim)], dctx)

    def inner_grad(n):
        own, h = chunks[n]
        loaded(("wd", n))
        loaded(("slope", n))
        s = n % 2
        bias = 0.0
        for r in range(0, rows, TILE):
            at = slice(r, r + TILE)
            grad = (mm_nt(low[at], slots[2 + s]) * slots[6 + s, at].astype(F32)).astype(BF16)
            inner_at[s][at] = grad
            bias += jnp.sum(grad.astype(F32), axis=0, keepdims=True)
            poll(0.5)
        for part in range(2):
            row = 4 * (y if own else 1 - y) + 2 * h + part
            vecs[pl.ds(row, 1)] = bias[:, part * width : (part + 1) * width]
        if n < 2:
            load_ffn(n + 2, "wd")
            load_ffn(n + 2, "slope")

    def hidden_grad(n):
        loaded("second")
        loaded(("wu", n))
        for r in range(0, rows, TILE):
            at = slice(r, r + TILE)
            total[at] += mm_nt(inner_at[n % 2][at], slots[n % 2])
            poll(0.45)
        if n < 2:
            load_ffn(n + 2, "wu")
        if n == 3:
            load_attention()

    def up_grad(n):
        own = chunks[n][0]
        loaded("hidden")
        put_columns(b_i if own else b_e, 0, hidden, inner_at[n % 2], n % 2 == 1)
        if n % 2 == 0:
            for k in range(ffn_chunks // 2):
                cores(own, k)

    def down_grad(n):
        own = chunks[n][0]
        loaded("low")
        loaded(("act", n))
        put_columns(b_i if own else b_e, dim, low, slots.at[4 + n % 2], n % 2 == 1)
        if n % 2 == 0:
            for k in range(ffn_chunks // 2, ffn_chunks):
                cores(own, k)
        if n < 2:
            load_ffn(n + 2, "act")

    def load_attention():
        left, right = pl.ds(0, width), pl.ds(width, width)
        load(
            "att",
            (q_h, slots.at[0]),
            (k_h.at[pl.ds(0, SEG)], slots.at[2, pl.ds(0, SEG)]),
            (k_h.at[pl.ds(SEG, SEG)], slots.at[4, pl.ds(0, SEG)]),
            (v_h.at[pl.ds(0, SEG)], slots.at[6, pl.ds(0, SEG)]),
            (v_h.at[pl.ds(SEG, SEG)], slots.at[1, pl.ds(0, SEG)]),
        )
        load(
            "att_w",
            (wq_i, slots.at[3, :, left]),
            (wk_i, slots.at[3, :, right]),
            (wv_i, slots.at[5, :, left]),
            (wv_o, slots.at[5, :, right]),
            (wq_o, slots.at[7, :, left]),
            (wk_o, slots.at[7, :, right]),
        )
        load_probs(0)
        load_probs(1)

    pairs = width // PAIR
    pair_order = [pairs + n for n in range(pairs)] + list(range(pairs))

    def load_probs(n):
        pair = pair_order[n]
        load(
            ("p", n),
            (pa_h.at[pl.ds(2 * pair, 2)], p_a.at[n % 2]),
            (pm_h.at[pl.ds(2 * pair, 2)], p_m.at[n % 2]),
        )

    def out_back():
        loaded("mid")
        sums = [0.0, 0.0, 0.0]
        gain_row = gain[...].astype(F32).reshape(1, dim)
        for r in range(0, rows, TILE):
            tile = slice(r, r + TILE)
            grad_in = total[tile]
            n = normed[tile].astype(F32)
            scaled = grad_in * gain_row
            grad = inv[tile] * (
                scaled
                - jnp.mean(scaled, axis=-1, keepdims=True)
                - n * jnp.mean(scaled * n, axis=-1, keepdims=True)
            )
            sums[0] += jnp.sum(grad_in * n, axis=0, keepdims=True)
            sums[1] += jnp.sum(grad_in, axis=0, keepdims=True)
            sums[2] += jnp.sum(grad, axis=0, keepdims=True)
            total[tile] = grad
            low[tile] = grad.astype(BF16)
        for i, value in enumerate(sums):
            for part in range(2):
                cut = slice(part * width, (part + 1) * width)
                vecs[12 + 2 * i + part : 13 + 2 * i + part] = value[:, cut]
                vecs[18 + 2 * i + part : 19 + 2 * i + part] = vec2[i : i + 1, cut]
        total[rows:] = jnp.zeros((half, dim), F32)
        d3[rows:, :width] = jnp.zeros((half, width), BF16)

    def out_grads():
        for pair in range(2):
            grads = mm_tn(low[:, 2 * pair * quarter : 2 * (pair + 1) * quarter], ctx[...]).astype(BF16)
            for n in range(2):
                at = slice(n * quarter, (n + 1) * quarter)
                put_rows(b_i, 3, 2 * pair + n, grads[at, :width])
                put_rows(b_e, 3, 2 * pair + n, grads[at, width:])
            poll(0.7)
        for k in out_chunks:
            cores(False, k)
            cores(True, k)

    def context_grad():
        for r in range(0, rows, TILE):
            at = slice(r, r + TILE)
            dctx[at] = mm_nt(low[at], wo[...]).astype(BF16)
            poll(0.4)

    def attend(n):
        pair = pair_order[n]
        cols = slice(pair * PAIR, (pair + 1) * PAIR)
        local_at = (pair % pairs) * PAIR
        if n == 0:
            loaded("att")
        loaded(("p", n))
        lane = lax.broadcasted_iota(jnp.int32, (1, PAIR), 1) // HEAD_DIM
        zero = jnp.zeros((), BF16)
        for first, count, key_first, k_slot, v_slot, probs_ref in (
            (0, SEG, 0, 2, 6, p_a),
            (SEG, half, SEG, 4, 1, p_m),
        ):
            q_at = slice(first, first + count)
            ks = slice(key_first, key_first + SEG)
            grad2, query2 = dctx[q_at, cols], slots[0, q_at, cols]
            keys, values = slots[k_slot, :SEG, cols], slots[v_slot, :SEG, cols]
            delta_t = (grad2.astype(F32) * ctx[q_at, cols].astype(F32)).T
            values_grad = keys_grad = query_grad = 0.0
            for h in range(2):
                grad_h = jnp.where(lane == h, grad2, zero)
                query_h = jnp.where(lane == h, query2, zero)
                keys_h = jnp.where(lane == h, keys, zero)
                probs = probs_ref[n % 2, h]
                delta = jnp.sum(delta_t[h * HEAD_DIM : (h + 1) * HEAD_DIM], axis=0, keepdims=True)
                prob_grad = mm_nt(values, grad_h)
                score_grad = (probs.astype(F32) * (prob_grad - delta)).astype(BF16)
                values_grad += mm(probs, grad_h)
                keys_grad += mm(score_grad, query_h)
                query_grad += mm_tn(score_grad, keys_h)
                poll(0.7 if first == 0 else 0.35)
            for part, value, out_at in (
                (0, query_grad * HEAD_DIM**-0.5, q_at),
                (1, keys_grad, ks),
                (2, values_grad, ks),
            ):
                d3[out_at, part * width + local_at : part * width + local_at + PAIR] = value.astype(BF16)
        if n + 2 < 2 * pairs:
            load_probs(n + 2)

    def input_part(own):
        loaded("att_w")
        main = 3 if own else 7
        last = slice(0, width) if own else slice(width, 2 * width)
        for r in range(0, rows + half, TILE):
            at = slice(r, r + TILE)
            total[at] += mm_nt(d3[at, : 2 * width], slots[main]) + mm_nt(
                d3[at, 2 * width :], slots[5, :, last]
            )
            poll(0.7)

    def weight_part(own):
        buf = b_i if own else b_e
        for pair in range(2):
            grads = mm_tn(x_s[:, 2 * pair * quarter : 2 * (pair + 1) * quarter], d3[...]).astype(BF16)
            for n in range(2):
                at = slice(n * quarter, (n + 1) * quarter)
                for group in range(3):
                    put_rows(buf, group, 2 * pair + n, grads[at, group * width : (group + 1) * width])
            poll(1.4)
        for k in qkv_chunks:
            cores(own, k)
        row = y if own else 1 - y
        vecs[pl.ds(8 + row, 1)] = jnp.sum(d3[:rows, :width].astype(F32), axis=0, keepdims=True)
        vecs[pl.ds(10 + row, 1)] = jnp.sum(d3[:, 2 * width :].astype(F32), axis=0, keepdims=True)

    done = []

    def leave(first, count):
        copy = copies.here(total.at[pl.ds(first, count)], top_o.at[pl.ds(first, count)])
        copy.start()
        done.append(copy)

    def finish():
        mid_b[0][...] = total[rows:].astype(BF16)
        done.append(go(copies.to(mid_b[0], mid_r, c=1 - c)))
        leave(0, SEG)
        vec_start(0)

    def middle():
        arrived(done[0])
        value = total[SEG:rows] + mid_r[...].astype(F32)
        total[SEG:rows] = value
        mid_b[1][...] = value.astype(BF16)
        leave(SEG, half)

        @pl.when(jnp.logical_not(same))
        def _():
            in_d.start()
            out_d.start()

    ready_e, ready_i = {}, {}
    clock = 3.0
    for n in (0, 2):
        step(1.4, down_grad, n)
        step(1.4, down_grad, n + 1)
        step(1.5, inner_grad, n)
        step(1.4, up_grad, n)
        step(1.5, inner_grad, n + 1)
        step(1.4, up_grad, n + 1)
        step(1.3, hidden_grad, n)
        step(1.3, hidden_grad, n + 1)
    step(1.6, out_back)
    step(1.4, out_grads)
    step(1.2, context_grad)
    for n in range(2 * pairs):
        step(2.1, attend, n)
        if n % pairs == pairs - 1:
            own = n > pairs
            if own:
                step(2.8, input_part, own)
                step(3.0, weight_part, own)
            else:
                step(3.0, weight_part, own)
                step(2.8, input_part, own)
    step(0.7, finish)
    when = {}
    for us, body, arguments in work:
        clock += us
        when[(body, *arguments)] = clock
    for k in parts:
        if k < ffn_chunks:
            ready = (up_grad, down_grad)[2 * k // ffn_chunks]
            ready_e[k], ready_i[k] = when[ready, 1], when[ready, 3]
        elif k in out_chunks:
            ready_e[k] = ready_i[k] = when[(out_grads,)] + 1.5
        else:
            ready_e[k], ready_i[k] = when[weight_part, False] + 1.5, when[weight_part, True] + 1.5
    chunk_order = {
        k: parts[k] for k in [*range(ffn_chunks // 2, ffn_chunks), *range(ffn_chunks // 2), *out_chunks, *qkv_chunks]
    }
    tasks = []
    for time, stage, k in plan(chunk_order, levels, split, ready_e, ready_i):
        if stage == "y":
            tasks.append((time, to_y, (k,)))
        elif stage == "x":
            tasks.append((time, to_x, (k,)))
        elif stage == "end":
            tasks.append((time, from_x, (k,)))
        elif stage == "fx":
            if not split:
                tasks.append((time, to_z, (k, levels)))
            tasks.append((time, from_z, (k, 0)))
        elif stage[0] == "z":
            tasks.append((time, to_z, (k, stage[1])))
        elif stage[1] == split - 1:
            tasks.append((time, to_z, (k, levels)))
        else:
            tasks.append((time, from_z, (k, stage[1] + 1)))
    end = when[(finish,)]
    last_y = max(time for time, task, _ in tasks if task is to_y)
    tasks.append((max(end + 4.0, last_y + 0.1), middle, ()))
    for n in range(len(near)):
        tasks.append((end + 5.0 + 5.0 * n, vec_next, (n,)))
    tasks.sort(key=lambda t: t[0])
    clock = 3.0
    for us, body, arguments in work:
        run_until(clock)
        now[0] = clock
        body(*arguments)
        clock += us
    run_until(1e9)

    @pl.when(jnp.logical_not(same))
    def _():
        out_d.wait()
        in_d.wait()

    for copy in done[1:]:
        copy.wait()
    for copy in every:
        copy.wait_send()
        if id(copy) not in waited:
            copy.wait_recv()


def final_body(
    pos_ref, sums, top, output, top_mid, output_mid, in_mid, out_mid, vec,
    out_o, in_o, q_o, k_o, v_o, wo_o, up_o, down_o, bq_o, bv_o, bu_o, n1g_o, n1b_o, bo_o, n2g_o, n2b_o, bd_o, tmp,
):
    j = pl.program_id(0)
    dim = up_o.shape[0]
    quarter, width = q_o.shape
    same = pos_ref[1] == pos_ref[2]
    is_mid = jnp.where(pos_ref[2] == 0, j >= 2, j == 0)

    @pl.when(is_mid & same)
    def _():
        out_o[...] = output_mid[...]
        in_o[...] = top_mid[...]

    @pl.when(is_mid & jnp.logical_not(same))
    def _():
        out_o[...] = out_mid[...]
        in_o[...] = in_mid[...].astype(F32)

    @pl.when(jnp.logical_not(is_mid))
    def _():
        out_o[...] = output[...]
        in_o[...] = top[...]

    @pl.when(j == 0)
    def _():
        bq_o[...] = vec[pl.ds(8 + pos_ref[2], 1)].reshape(width)
        bv_o[...] = vec[pl.ds(10 + pos_ref[2], 1)].reshape(width)
        parts = [vec[pl.ds(4 * pos_ref[2] + n, 1)] for n in range(4)]
        bu_o[...] = jnp.concatenate(parts, axis=1).reshape(4 * width)
        for n, ref in enumerate((n1g_o, n1b_o, bo_o, n2g_o, n2b_o, bd_o)):
            ref[...] = wide_row(vec, 12 + 2 * n).reshape(dim)

    up_o[...] = sums[0, :dim].astype(F32)
    down_o[...] = sums[0, dim : 2 * dim].astype(F32).T
    for part, ref in enumerate((q_o, k_o, v_o)):
        at = 2 * dim + part * quarter
        ref[...] = sums[0, at : at + quarter].astype(F32)
    row = pl.multiple_of((pos_ref[0] ^ j) * quarter, 16)
    at = 2 * dim + 3 * quarter
    tmp[pl.ds(row, quarter), :] = sums[0, at : at + quarter].astype(F32)

    @pl.when(j == pl.num_programs(0) - 1)
    def _():
        wo_o[...] = tmp[...].T


def shards(
    depth,
    tokens, lengths, buckets, w_query, b_query, w_key, w_value, b_value, w_out, b_out,
    norm1_gain, norm1_bias, w_up, b_up, w_down, b_down, norm2_gain, norm2_bias, cotangent,
):
    ix, ic, iy = (lax.axis_index(a) for a in ("x", "c", "y"))
    pos = jnp.stack([2 * ic + ix, ic, iy]).astype(jnp.int32)
    rows, dim = tokens.shape
    half = rows - SEG
    width = w_query.shape[1]
    units = w_up.shape[1]
    chunk = units // 4
    any_space = pl.BlockSpec(memory_space=pl.ANY)
    in_vmem = pl.BlockSpec(memory_space=pltpu.VMEM)

    weights = (w_query, w_key, w_value, w_out, w_up, w_down)
    total = rows + half
    square = (rows, dim)
    wide = (rows, units)
    pairs = width // PAIR
    made = [
        shape((total, dim), BF16),
        *[shape(w.shape, BF16) for w in weights],
        shape(square, BF16),
        shape((total, dim), BF16),
        shape((total, dim), BF16),
        shape((4 * pairs, SEG, SEG), BF16),
        shape((4 * pairs, SEG, half), BF16),
        shape(square, BF16),
        shape(square, BF16),
        shape((rows, 1), F32),
        shape(square, BF16),
        *[shape(wide, BF16)] * 4,
        shape(square, F32),
        shape(square, BF16),
        shape(square, BF16),
        shape((3, dim), F32),
    ]
    (
        x, wq_o, wk_o, wv_o, wo_o, wu_o, wd_o, query, keys, values, probs_a, probs_m, ctx, normed1, inverse1, hidden,
        act_i, act_o, slope_i, slope_o, second, low, output, vec2,
    ) = pl.pallas_call(
        forward_body,
        out_shape=made,
        in_specs=[any_space] * 8 + [in_vmem] * 9 + [pl.BlockSpec(memory_space=pltpu.SMEM)] * 2,
        out_specs=[any_space] * (len(made) - 1) + [in_vmem],
        scratch_shapes=[
            pltpu.VMEM((total, dim), BF16),
            pltpu.VMEM(square, BF16),
            pltpu.VMEM((2, dim, 3 * width), BF16),
            pltpu.VMEM((2 * width, dim), BF16),
            pltpu.VMEM((2, dim, units), BF16),
            pltpu.VMEM((2, units, dim), BF16),
            pltpu.VMEM(square, BF16),
            *[pltpu.VMEM((total, dim), BF16)] * 2,
            pltpu.VMEM((3, 2, SEG, SEG), BF16),
            pltpu.VMEM((3, 2, SEG, half), BF16),
            *[pltpu.VMEM(square, BF16)] * 2,
            pltpu.VMEM((rows, 1), F32),
            pltpu.VMEM(square, BF16),
            pltpu.VMEM(square, F32),
            *[pltpu.VMEM((2, *wide), BF16)] * 2,
            *[pltpu.VMEM(square, BF16)] * 2,
            pltpu.VMEM((rows, 1), F32),
            pltpu.VMEM((SEG, SEG), F32),
            pltpu.VMEM((SEG, half), F32),
            pltpu.VMEM((24, width), F32),
            pltpu.VMEM((8, 128), F32),
            pltpu.VMEM((24, width), F32),
            *[pltpu.VMEM((8, 128), F32)] * 2,
            pltpu.SemaphoreType.DMA((88,)),
            pltpu.SemaphoreType.DMA((88,)),
            pltpu.SemaphoreType.DMA((64,)),
            pltpu.SemaphoreType.DMA((2,)),
        ],
        compiler_params=pltpu.CompilerParams(
            collective_id=1, has_side_effects=True, vmem_limit_bytes=VMEM_LIMIT
        ),
        name="forward",
    )(
        tokens, cotangent, *weights, b_query, b_value, b_up, b_out, norm1_gain, norm1_bias, b_down, norm2_gain, norm2_bias,
        buckets, lengths,
    )

    levels = depth.bit_length() - 1
    more = max(levels - 2, 0)
    size = 3 * dim
    links = levels + 3
    remote = 16 * (levels + 10) + links + 2
    sums, top, vec, in_mid, out_mid = pl.pallas_call(
        functools.partial(backward_body, depth),
        out_shape=[
            shape((4, size, width), BF16),
            shape((rows, dim), F32),
            shape((24, width), F32),
            shape((half, dim), BF16),
            shape((half, dim), BF16),
        ],
        in_specs=[any_space] * 29 + [in_vmem] * 2,
        out_specs=[any_space] * 2 + [in_vmem] + [any_space] * 2,
        scratch_shapes=[
            *[pltpu.VMEM((rows, dim), BF16)] * 2,
            pltpu.VMEM((8, rows, dim), BF16),
            pltpu.VMEM((rows + half, dim), F32),
            *[pltpu.VMEM((4, size, width), BF16)] * 2,
            *[pltpu.VMEM((2, size, width), BF16)] * 3,
            pltpu.VMEM((size, width), BF16),
            pltpu.VMEM((size // 2, width), BF16),
            pltpu.VMEM((size // 4, width), BF16),
            pltpu.VMEM((max(more, 1), size // 4 if more else 16, width), BF16),
            pltpu.VMEM((rows, dim), BF16),
            pltpu.VMEM((rows, 1), F32),
            *[pltpu.VMEM((rows, dim), BF16)] * 3,
            pltpu.VMEM((rows + half, dim), BF16),
            pltpu.VMEM((2, 2, SEG, SEG), BF16),
            pltpu.VMEM((2, 2, SEG, half), BF16),
            pltpu.VMEM((rows + half, 3 * width), BF16),
            pltpu.VMEM((24, width), F32),
            pltpu.VMEM((2 * links, 24, width), F32),
            pltpu.VMEM((half, dim), BF16),
            pltpu.SemaphoreType.DMA((remote,)),
            pltpu.SemaphoreType.DMA((remote,)),
            pltpu.SemaphoreType.DMA((80,)),
            pltpu.SemaphoreType.DMA((4,)),
        ],
        compiler_params=pltpu.CompilerParams(
            collective_id=2, has_side_effects=True, vmem_limit_bytes=VMEM_LIMIT
        ),
        name="backward",
    )(
        low, hidden, act_i, act_o, slope_i, slope_o, w_up, wu_o, w_down, wd_o, second, normed1, inverse1,
        w_out, wo_o, ctx, x, query, keys, values, probs_a, probs_m, w_query, w_key, w_value, wq_o, wk_o, wv_o,
        output, norm1_gain, vec2,
    )
    quarter = dim // 4
    const = lambda *dims: pl.BlockSpec(dims, lambda j, pos: (0,) * len(dims))
    full_block = lambda j, pos: (jnp.where(pos[2] == 0, jnp.minimum(j, 1), jnp.clip(j - 1, 0, 1)), 0)
    row_block = pl.BlockSpec((half, dim), lambda j, pos: (jnp.minimum(j, 2), 0))
    by_rows = lambda n, m: pl.BlockSpec((n, m), lambda j, pos: (pos[0] ^ j, 0))
    (
        output, input_grad, w_query_grad, w_key_grad, w_value_grad, w_out_grad, w_up_grad, w_down_grad,
        b_query_grad, b_value_grad, b_up_grad, norm1_gain_grad, norm1_bias_grad, b_out_grad,
        norm2_gain_grad, norm2_bias_grad, b_down_grad,
    ) = call(
        final_body,
        (4,),
        pos,
        [sums, top, output, top, output, in_mid, out_mid, vec],
        [
            pl.BlockSpec((1, size, width), lambda j, pos: (j, 0, 0)),
            pl.BlockSpec((half, dim), full_block),
            pl.BlockSpec((half, dim), full_block),
            *[pl.BlockSpec((half, dim), lambda j, pos: (2, 0))] * 2,
            whole(in_mid),
            whole(out_mid),
            whole(vec),
        ],
        [
            shape((rows, dim), BF16),
            shape((rows, dim), F32),
            *[shape((dim, width), F32)] * 3,
            shape((width, dim), F32),
            shape((dim, units), F32),
            shape((units, dim), F32),
            *[shape((n,), F32) for n in (width, width, units, *[dim] * 6)],
        ],
        [
            row_block,
            row_block,
            *[by_rows(quarter, width)] * 3,
            const(width, dim),
            pl.BlockSpec((dim, chunk), lambda j, pos: (0, pos[0] ^ j)),
            by_rows(chunk, dim),
            *[const(n) for n in (width, width, units, *[dim] * 6)],
        ],
        [pltpu.VMEM((dim, width), F32)],
        0,
        "final",
    )
    return (
        output,
        input_grad,
        w_query_grad,
        b_query_grad,
        w_key_grad,
        w_value_grad,
        b_value_grad,
        w_out_grad,
        b_out_grad,
        norm1_gain_grad,
        norm1_bias_grad,
        w_up_grad,
        b_up_grad,
        w_down_grad,
        b_down_grad,
        norm2_gain_grad,
        norm2_bias_grad,
    )


def solution(mesh):
    depth = mesh.shape["dp"] // 4
    inner = Mesh(mesh.devices.reshape(depth, 2, 2, mesh.shape["mp"]), ("z", "x", "c", "y"))
    dp = ("z", "x", "c")
    every = (*dp, "y")
    placed = (
        P(every, None),
        P(dp, None),
        P(dp),
        P(None, "y"),
        P("y"),
        P(None, "y"),
        P(None, "y"),
        P("y"),
        P("y", None),
        P(),
        P(),
        P(),
        P(None, "y"),
        P("y"),
        P("y", None),
        P(),
        P(),
        P(),
        P(every, None),
    )
    return jax.shard_map(
        functools.partial(shards, depth),
        mesh=inner,
        in_specs=placed,
        out_specs=(
            P(every, None),
            P(every, None),
            P(None, "y"),
            P("y"),
            P(None, "y"),
            P(None, "y"),
            P("y"),
            P("y", None),
            P(),
            P(),
            P(),
            P(None, "y"),
            P("y"),
            P("y", None),
            P(),
            P(),
            P(),
        ),
        check_vma=False,
    )
```

```python
import functools

import jax
import jax.numpy as jnp
from jax import lax
from jax.experimental import pallas as pl
from jax.experimental.pallas import tpu as pltpu
from jax.sharding import Mesh, PartitionSpec as P

HEAD_DIM = 64
SEG = 512
PAIR = 2 * HEAD_DIM
NEG = -1e30
EPS = 1e-12
ROOT_HALF = 0.7071067811865476
INV_ROOT_TWO_PI = 0.3989422804014327
F32 = jnp.float32
BF16 = jnp.bfloat16
VMEM_LIMIT = 60 * 1024 * 1024
TILE = 256
CHUNK = 192
HOP_US = 3.2
BACK_HOP_US = 3.5
PACE = 1.15
BACK_PACE = 1.2
X_FIRST = (1, 3, 5, 7)
DIRECT = (10, 11, 12, 13, 14)
MESH_IDS = pl.DeviceIdType.MESH


def mm(left, right):
    return lax.dot_general(left, right, (((1,), (0,)), ((), ())), preferred_element_type=F32)


def mm_nt(left, right):
    return lax.dot_general(left, right, (((1,), (1,)), ((), ())), preferred_element_type=F32)


def mm_tn(left, right):
    return lax.dot_general(left, right, (((0,), (0,)), ((), ())), preferred_element_type=F32)


def call(body, grid, pos, inputs, in_specs, out_shape, out_specs, scratch, flops, name):
    moved = sum(v.size * v.dtype.itemsize for v in inputs) + sum(
        v.size * v.dtype.itemsize for v in out_shape
    )
    return pl.pallas_call(
        body,
        grid_spec=pltpu.PrefetchScalarGridSpec(
            num_scalar_prefetch=1,
            grid=grid,
            in_specs=in_specs,
            out_specs=out_specs,
            scratch_shapes=scratch,
        ),
        out_shape=out_shape,
        compiler_params=pltpu.CompilerParams(
            dimension_semantics=("arbitrary",) * len(grid), vmem_limit_bytes=VMEM_LIMIT
        ),
        cost_estimate=pl.CostEstimate(flops=flops, bytes_accessed=moved, transcendentals=0),
        name=name,
    )(pos, *inputs)


def whole(array):
    zeros = (0,) * array.ndim
    return pl.BlockSpec(array.shape, lambda j, pos: zeros)


def shape(dims, kind):
    return jax.ShapeDtypeStruct(dims, kind)


def gelu_parts(inner):
    erf = lax.erf(inner * ROOT_HALF)
    below = 0.5 + 0.5 * erf
    density = jnp.exp(inner * inner * -0.5) * INV_ROOT_TWO_PI
    return inner * below, below + inner * density


def row_ids(info, at, places):
    bucket = info[at : at + 1, 0:1]
    span = jnp.where(bucket < 0.5, 1.0 * SEG, jnp.where(bucket < 1.5, 0.5 * SEG, 0.25 * SEG))
    row = jnp.zeros_like(places)
    size = jnp.zeros_like(places) + info[at : at + 1, 1:2]
    for slot in range(1, 4):
        later = places >= span * slot
        row = jnp.where(later, 1.0 * slot, row)
        size = jnp.where(later, info[at : at + 1, slot + 1 : slot + 2], size)
    return row, places - row * span < size


def wide_row(ref, row):
    return jnp.concatenate([ref[row : row + 1], ref[row + 1 : row + 2]], axis=1)


class Copies:
    def __init__(self, send, recv, local):
        self.send, self.recv, self.local = send, recv, local
        self.remote_count = self.local_count = 0

    def to(self, src, dst, **device):
        n = self.remote_count
        self.remote_count += 1
        return pltpu.make_async_remote_copy(
            src_ref=src,
            dst_ref=dst,
            send_sem=self.send.at[n],
            recv_sem=self.recv.at[n],
            device_id=device,
            device_id_type=MESH_IDS,
        )

    def here(self, src, dst):
        n = self.local_count
        self.local_count += 1
        return pltpu.make_async_copy(src, dst, self.local.at[n])


def coords():
    return tuple(lax.axis_index(a) for a in ("z", "x", "c", "y"))


def greet(devices):
    barrier = pltpu.get_barrier_semaphore()
    for device in devices:
        pl.semaphore_signal(barrier, inc=1, device_id=device, device_id_type=MESH_IDS)
    pl.semaphore_wait(barrier, len(devices))


def forward_body(
    tokens, cot_h, wq, wk, wv, wo, wu, wd, b_q, b_v, b_u, b_o, gain1, bias1, b_d, gain2, bias2, buckets, lengths,
    x_o, wq_o, wk_o, wv_o, wo_o, wu_o, wd_o, q_o, k_o, v_o, pa_o, pm_o, ctx_o, normed_o, inv_o, hidden_o,
    act_io, act_oo, slope_io, slope_oo, second_o, low_o, out_o, vec_o,
    x_s, cot, w3, wo_s, wu_s, wd_s, q_s, k_s, v_s, p_a, p_m, ctx, normed, inv, hidden, acc, act, slope, low, out_s,
    keep, mask_a, mask_m, bias, info, bias_r, info_r, info_s, send, recv, local, crossed,
):
    z, x, c, y = coords()
    copies = Copies(send, recv, local)
    rows, dim = cot.shape
    shared = 2 + wu.shape[1] // wq.shape[1]

    def const(n):
        return wide_row(bias, shared + 2 * n)

    half = rows - SEG
    width = wq.shape[1]
    pairs = width // PAIR
    same = c == y
    full = pl.ds(pl.multiple_of(y * half, half), SEG)
    mid = pl.ds(pl.multiple_of((1 - y) * SEG, half), half)
    own_at, sib_at = pl.ds(SEG, half), pl.ds(SEG + half, half)
    loads, stores = {}, []

    def load(name, *moves):
        loads[name] = [copies.here(src, dst) for src, dst in moves]
        for copy in loads[name]:
            copy.start()

    def loaded(name):
        for copy in loads.pop(name, ()):
            copy.wait()

    def store(src, dst):
        copy = copies.here(src, dst)
        copy.start()
        stores.append(copy)
        return copy

    load(
        "qkv",
        (tokens.at[full], x_s.at[pl.ds(0, SEG)]),
        *[(w, w3.at[0, :, pl.ds(n * width, width)]) for n, w in enumerate((wq, wk, wv))],
    )
    x_own = copies.here(tokens.at[mid], x_s.at[own_at])
    cot_own = copies.here(cot_h.at[mid], cot.at[own_at])

    @pl.when(same)
    def _():
        x_own.start()
        cot_own.start()

    row = 0
    for ref in (b_q, b_v, b_u, b_o, gain1, bias1, b_d, gain2, bias2):
        for n in range(ref.shape[0] // width):
            bias[row : row + 1] = ref[n * width : (n + 1) * width].astype(F32).reshape(1, width)
            row += 1
    bias[row:] = jnp.zeros((bias.shape[0] - row, width), F32)
    lane = lax.broadcasted_iota(jnp.int32, (1, info.shape[1]), 1)
    info[...] = jnp.zeros_like(info)
    for n, block in enumerate((2 * y, 1)):
        value = jnp.where(lane == 0, buckets[block], 0)
        for slot in range(4):
            value = jnp.where(lane == slot + 1, lengths[block, slot], value)
        info[n : n + 1] = value.astype(F32)
    greet([{"y": 1 - y}, {"x": 1 - x}, {"c": 1 - c}, {"z": z + 1 - 2 * (z % 2)}, {"c": 1 - c, "y": 1 - y}])

    x_y = copies.to(tokens.at[mid], x_s.at[sib_at], y=1 - y)
    x_c1 = copies.to(x_s.at[own_at], x_s.at[sib_at], c=1 - c)
    x_c2 = copies.to(x_s.at[sib_at], x_s.at[own_at], c=1 - c)
    cot_d = pltpu.make_async_remote_copy(
        src_ref=cot_h.at[mid], dst_ref=cot.at[own_at], send_sem=crossed.at[0], recv_sem=crossed.at[1],
        device_id={"c": 1 - c, "y": 1 - y}, device_id_type=MESH_IDS,
    )
    info_copy = copies.to(info, info_r, c=1 - c)
    bias_copy = copies.to(bias, bias_r, y=1 - y)

    @pl.when(jnp.logical_not(same))
    def _():
        x_y.start()

    info_copy.start()
    bias_copy.start()

    z_next = z + 1 - 2 * (z % 2)
    zb = z % 2

    def rows_of(ref, first, count, part, columns=None):
        def cut(p, sub=0, subs=1):
            n = count // subs
            at = pl.ds(pl.multiple_of(first + (2 * c + p) * part + sub * n, 16), n)
            return ref.at[at] if columns is None else ref.at[at, columns]

        return cut

    def columns_of(ref, first, count):
        def cut(p, sub=0, subs=1):
            n, m = ref.shape[1] // 4, count // subs
            row = pl.multiple_of(first + sub * m, 16)
            return ref.at[pl.ds(row, m), pl.ds(pl.multiple_of((2 * c + p) * n, 128), n)]

        return cut

    arrays = []
    part = dim // 4
    for n, w in enumerate((wq, wk, wv)):
        cols = pl.ds(n * width, width)
        arrays.append(("qkv", "yxz", 3.1, rows_of(w, 0, part, part), rows_of(w3.at[1], 0, part, part, cols)))
    part = width // 4
    arrays.append(("wo", "yx", 3.1, rows_of(wo, 0, part, part), rows_of(wo_s, width, part, part)))
    for n in range(2):
        m = dim // 2
        arrays.append(("wu", "yxz", 6.2, columns_of(wu, n * m, m), columns_of(wu_s.at[1], n * m, m)))
    part = wd.shape[0] // 4
    for how, first, m in (("yxz", 0, 2), ("yx", 2, 1), ("yz", 3, 1)):
        first, m = first * part // 4, m * part // 4
        cuts = rows_of(wd, first, m, part), rows_of(wd_s.at[1], first, m, part)
        arrays.append(("wd", how, 12.4 * m / part, *cuts))
    over = {}

    def pass_on(n, hop, cut, **device):
        over[n, hop] = copies.to(cut, cut, **device)
        over[n, hop].start()

    def start(n):
        _, how, _, mine, there = arrays[n]
        if how == "yxz":
            src, dst = mine(x, zb, 2), there(x, zb, 2)
        else:
            p = x if how == "yx" else zb
            src, dst = mine(p), there(p)
        over[n, "y"] = copies.to(src, dst, y=1 - y)
        over[n, "y"].start()

    def from_y(n):
        _, how, _, _, there = arrays[n]
        over[n, "y"].wait_recv()
        cut = there(x, zb, 2) if how == "yxz" else there(x if how == "yx" else zb)
        if how != "yz":
            pass_on(n, "x", cut, x=1 - x)
        if how != "yx":
            pass_on(n, "z", cut, z=z_next)
        pass_on(n, "cy", cut, c=1 - c)

    def from_x(n):
        _, how, _, _, there = arrays[n]
        over[n, "x"].wait_recv()
        if how == "yxz":
            pass_on(n, "xz", there(1 - x, 2 * zb + 1, 4), z=z_next)
            pass_on(n, "cx", there(1 - x, zb, 2), c=1 - c)
        else:
            pass_on(n, "cx", there(1 - x), c=1 - c)

    def from_z(n):
        _, how, _, _, there = arrays[n]
        over[n, "z"].wait_recv()
        if how == "yxz":
            pass_on(n, "zx", there(x, 2 * (1 - zb), 4), x=1 - x)
            pass_on(n, "cz", there(x, 1 - zb, 2), c=1 - c)
        else:
            pass_on(n, "cz", there(1 - zb), c=1 - c)

    def from_both(n):
        over[n, "zx"].wait_recv()
        over[n, "xz"].wait_recv()
        pass_on(n, "cb", arrays[n][4](1 - x, 1 - zb, 2), c=1 - c)

    def mid_rows():
        @pl.when(same)
        def _():
            x_own.wait()
            x_y.wait_recv()
            x_c1.start()
            x_c2.start()

    tasks = [(8.5, mid_rows, ())]
    clock = 3.0 + 4.1
    ready = []
    for n, (_, how, us, _, _) in enumerate(arrays):
        start(n)
        clock += us / 2 if how == "yxz" else us
        first = clock + HOP_US
        tasks.append((first, from_y, (n,)))
        for link in how[1:]:
            ready.append((first, link, n, us / 2 if how == "yxz" else us, 1))
    free = {"x": 0.0, "z": 0.0}
    both = {}
    while ready:
        item = min(ready, key=lambda v: (max(v[0], free[v[1]]), v[2]))
        ready.remove(item)
        time, link, n, us, hop = item
        free[link] = max(time, free[link]) + us
        come = free[link] + HOP_US
        if hop == 2:
            both.setdefault(n, []).append(come)
            if len(both[n]) == 2:
                tasks.append((max(both[n]), from_both, (n,)))
        else:
            tasks.append((come, from_x if link == "x" else from_z, (n,)))
            if arrays[n][1] == "yxz":
                ready.append((come, "z" if link == "x" else "x", n, us / 2, 2))
    tasks.sort(key=lambda t: t[0])

    @pl.when(jnp.logical_not(same))
    def _():
        cot_d.start()

    come = set()

    def run_until(time):
        while tasks and tasks[0][0] <= time:
            _, task, its = tasks.pop(0)
            task(*its)

    def need(name):
        if name in come:
            return
        come.add(name)
        while any(its and arrays[its[0]][0] == name for _, task, its in tasks):
            _, task, its = tasks.pop(0)
            task(*its)
        for n, array in enumerate(arrays):
            if array[0] == name:
                for hop in ("cy", "cx", "cz", "cb"):
                    if (n, hop) in over:
                        over[n, hop].wait_recv()

    load("wo", (wo, wo_s.at[pl.ds(0, width)]))
    load("wu", (wu, wu_s.at[0]))
    load("wd", (wd, wd_s.at[0]))
    load("cot", (cot_h.at[full], cot.at[pl.ds(0, SEG)]))

    work = []

    def step(us, body, *arguments):
        work.append((us * PACE, body, arguments))

    now = [2.0]

    def poll(us):
        now[0] += us * PACE
        run_until(now[0])

    def mask_of(mask, at, count):
        places = lax.broadcasted_iota(jnp.int32, (SEG, 1), 0)
        across = lax.broadcasted_iota(jnp.int32, (1, count), 1)
        if at == 1:
            places = (places + half * c) % SEG
            across = across + half * c
        key_row, valid = row_ids(info_s, at, places.astype(F32))
        query_row, _ = row_ids(info_s, at, across.astype(F32))
        allowed = jnp.where(valid, key_row, -1.0) == query_row
        mask[...] = jnp.where(allowed, 0.0, NEG)
        keep[at * SEG : at * SEG + count] = jnp.where(valid[:count], 1.0, 0.0)

    def project(other, first, count):
        if not other and first == 0:
            loaded("qkv")
            info_s[...] = info[...]
            mask_of(mask_a, 0, SEG)
        if not other and first == SEG:
            info_copy.wait_recv()
            info_s[...] = jnp.where(same, info[...], info_r[...])
            mask_of(mask_m, 1, half)

            @pl.when(jnp.logical_not(same))
            def _():
                x_c1.wait_recv()
                x_c2.wait_recv()

            store(x_s, x_o)
        if other:
            bias_copy.wait_recv()
            need("qkv")
            for n, w in enumerate((wq_o, wk_o, wv_o)):
                store(w3.at[1, :, pl.ds(n * width, width)], w)
        vector = bias_r if other else bias
        cols = slice(width, 2 * width) if other else slice(0, width)
        for r in range(first, first + count, TILE):
            at = slice(r, r + TILE)
            qkv = mm(x_s[at], w3[1 if other else 0])
            if r < rows:
                q_s[at, cols] = ((qkv[:, :width] + vector[0:1]) * HEAD_DIM**-0.5).astype(BF16)
            k_s[at, cols] = qkv[:, width : 2 * width].astype(BF16)
            v_s[at, cols] = (qkv[:, 2 * width :] + vector[1:2]).astype(BF16)
            poll(0.6)

    used = {}

    def attend(pair, middle):
        first, count, mask, probs, out = (SEG, half, mask_m, p_m, pm_o) if middle else (0, SEG, mask_a, p_a, pa_o)
        at = slice(first, first + count)
        ks = slice(first, first + SEG)
        cols = slice(pair * PAIR, (pair + 1) * PAIR)
        s = pair % 3
        if (middle, s) in used:
            used[middle, s].wait()
        lane = lax.broadcasted_iota(jnp.int32, (1, PAIR), 1) // HEAD_DIM
        query, keys = q_s[at, cols], k_s[ks, cols]
        values_t = v_s[ks, cols].astype(F32).T.astype(BF16)
        parts = []
        for h in range(2):
            query_h = jnp.where(lane == h, query, jnp.zeros((), BF16))
            scores = mm_nt(keys, query_h) + mask[...]
            top = jnp.max(scores, axis=0, keepdims=True)
            grown = jnp.exp(scores - top)
            prob = (grown * (1.0 / jnp.sum(grown, axis=0, keepdims=True))).astype(BF16)
            probs[s, h] = prob
            parts.append(mm(values_t[h * HEAD_DIM : (h + 1) * HEAD_DIM], prob))
            if h == 0:
                poll(0.4 if middle else 0.75)
        ctx[at, cols] = jnp.concatenate(parts, axis=0).T.astype(BF16)
        used[middle, s] = copies.here(probs.at[s], out.at[pl.ds(2 * pair, 2)])
        used[middle, s].start()

    def stored_qkv():
        for src, dst in ((q_s, q_o), (k_s, k_o), (v_s, v_o), (ctx, ctx_o)):
            store(src, dst)

    def normalize(value):
        centre = value - jnp.mean(value, axis=-1, keepdims=True)
        inverse = lax.rsqrt(jnp.mean(centre * centre, axis=-1, keepdims=True) + EPS)
        return centre * inverse, inverse

    def first_norm():
        loaded("wo")
        need("wo")
        store(wo_s.at[pl.ds(width, width)], wo_o)
        for r in range(0, rows, TILE):
            at = slice(r, r + TILE)
            poll(0.8)
            normal, inverse = normalize(x_s[at].astype(F32) + mm(ctx[at], wo_s[...]) + const(0))
            normed[at] = normal.astype(BF16)
            inv[at] = inverse
            hidden[at] = (normal * const(1) + const(2)).astype(BF16)
        store(normed, normed_o)
        store(inv, inv_o)
        store(hidden, hidden_o)

    def up(other, h):
        if h == 0:
            if other:
                need("wu")
                store(wu_s.at[1], wu_o)
            else:
                loaded("wu")
        s = 1 if other else 0
        vector = bias_r if other else bias
        cols = slice(h * dim, (h + 1) * dim)
        shift = wide_row(vector, 2 + 2 * h)
        for r in range(0, rows, TILE):
            at = slice(r, r + TILE)
            active, steep = gelu_parts(mm(hidden[at], wu_s[s, :, cols]) + shift)
            act[s, at, cols] = active.astype(BF16)
            slope[s, at, cols] = steep.astype(BF16)
            poll(0.75)
        if h == 1:
            store(act.at[s], act_oo if other else act_io)
            store(slope.at[s], slope_oo if other else slope_io)

    def down(other):
        if other:
            need("wd")
            store(wd_s.at[1], wd_o)
        else:
            loaded("wd")
        for r in range(0, rows, TILE):
            at = slice(r, r + TILE)
            if other:
                acc[at] += mm(act[1, at], wd_s[1])
            else:
                acc[at] = mm(act[0, at], wd_s[0])
            poll(0.75)

    def second_norm():
        loaded("cot")

        @pl.when(same)
        def _():
            cot_own.wait()

        @pl.when(jnp.logical_not(same))
        def _():
            cot_d.wait_recv()

        sums = [0.0, 0.0, 0.0]
        for r in range(0, rows, TILE):
            at = slice(r, r + TILE)
            normal, inverse = normalize(hidden[at].astype(F32) + acc[at] + const(3))
            g = const(4)
            out_s[at] = ((normal * g + const(5)) * keep[at]).astype(BF16)
            upstream = cot[at].astype(F32) * keep[at]
            scaled = upstream * g
            grad = inverse * (
                scaled
                - jnp.mean(scaled, axis=-1, keepdims=True)
                - normal * jnp.mean(scaled * normal, axis=-1, keepdims=True)
            )
            acc[at] = grad
            low[at] = grad.astype(BF16)
            sums[0] += jnp.sum(upstream * normal, axis=0, keepdims=True)
            sums[1] += jnp.sum(upstream, axis=0, keepdims=True)
            sums[2] += jnp.sum(grad, axis=0, keepdims=True)
            for src, dst in ((acc, second_o), (low, low_o), (out_s, out_o)):
                store(src.at[pl.ds(r, TILE)], dst.at[pl.ds(r, TILE)])
        for i, value in enumerate(sums):
            vec_o[i : i + 1] = value

    step(1.5, project, False, 0, SEG)
    for pair in range(pairs):
        step(1.4, attend, pair, False)
    step(1.8, project, False, SEG, SEG)
    for pair in range(pairs):
        step(0.7, attend, pair, True)
    step(2.4, project, True, 0, rows + half)
    for pair in range(pairs, 2 * pairs):
        step(1.4, attend, pair, False)
        step(0.7, attend, pair, True)
    step(0.2, stored_qkv)
    step(2.5, first_norm)
    step(2.2, up, False, 0)
    step(2.2, up, False, 1)
    step(2.2, down, False)
    step(2.2, up, True, 0)
    step(2.2, up, True, 1)
    step(2.2, down, True)
    step(2.0, second_norm)
    starts = {(project, False, SEG, SEG): 12.0, (project, True, 0, rows + half): 23.0, (up, True, 0): 37.0, (down, True): 47.0}
    clock = 2.0
    for us, body, arguments in work:
        clock = max(clock, starts.get((body, *arguments), 0.0))
        run_until(clock)
        now[0] = clock
        body(*arguments)
        clock += us
    run_until(1e9)

    @pl.when(same)
    def _():
        x_c1.wait_send()
        x_c2.wait_send()

    @pl.when(jnp.logical_not(same))
    def _():
        x_y.wait_send()
        cot_d.wait_send()

    info_copy.wait_send()
    bias_copy.wait_send()
    for copy in over.values():
        copy.wait_send()
    for copy in stores + list(used.values()):
        copy.wait()


LINK_US = 6.2 / 384


def plan(parts, x_first, direct, levels, split, ready_e, ready_i):
    free = {"y": 0.0, "x": 0.0, "z": 0.0, "far": 0.0}
    back = [("fz", n) for n in range(split - 1, -1, -1)] + ["fx"]
    route = {
        "y": ["y", "x"] + [("z", n) for n in range(levels)] + back,
        "q": ["y", "x", "zq"] + [("z", n) for n in range(split, levels)] + ["fq", "fx"],
        "e": ["ex"] + [("ez", n) for n in range(split)] + ["ey"],
        "i": ["x"] + [("z", n) for n in range(levels)] + back,
    }
    link_of = {"y": "y", "ey": "y", "x": "x", "ex": "x", "fx": "x", "zq": "far", "fq": "far"}
    for n in range(levels):
        for name in ("z", "ez", "fz"):
            link_of[name, n] = "z" if n == 0 else "far"
    share = {"zq": 1.0, "fq": 1.0, "y": 2.0, "ey": 0.25, "x": 1.0, "ex": 1.0, "fx": 1.0}
    order, ready, joined, held = [], [], {}, {}
    for n, k in enumerate(parts):
        if k in x_first:
            ready.append((ready_e[k], "e", 0, n, k))
            ready.append((ready_i[k], "i", 0, n, k))
        else:
            ready.append((ready_e[k], "q" if k in direct else "y", 0, n, k))
    while ready:

        def key(item):
            stage = route[item[1]][item[2]]
            return max(item[0], free[link_of[stage]]), stage in back or stage == "fq", item[3]

        item = min(ready, key=key)
        ready.remove(item)
        time, name, at, n, k = item
        stage = route[name][at]
        start = key(item)[0]
        us = parts[k] * LINK_US * share.get(stage, 0.5)
        free[link_of[stage]] = start + us
        order.append((start, stage, k))
        come = start + us + BACK_HOP_US
        if stage == "fx":
            order.append((come, "end", k))
        elif stage == "ey":
            joined[k] = come
            if k in held:
                ready.append((max(come, held[k]), "i", 1 + split, n, k))
        elif name == "i" and at == split:
            held[k] = come
            if k in joined:
                ready.append((max(come, joined[k]), "i", 1 + split, n, k))
        else:
            if stage == "y":
                come = max(come, ready_i[k])
            ready.append((come, name, at + 1, n, k))
    return sorted(order, key=lambda v: v[0])


def backward_body(
    depth,
    low_h, hidden_h, act_i, act_o, slope_i, slope_o, wu_i, wu_o, wd_i, wd_o, second_h, normed_h, inv_h,
    wo_i, wo_o, ctx_h, x_h, q_h, k_h, v_h, pa_h, pm_h, wq_i, wk_i, wv_i, wq_o, wk_o, wv_o, output_h, gain, vec2,
    sums_o, top_o, vec_o, in_o, out_o,
    low, hidden, slots, total, b_e, b_i, c_e, c_i, y_r, x_r, z_a, z_b, zx_r, normed, inv, wo, ctx, dctx, x_s,
    p_a, p_m, d3, vecs, vec_r, mid_r, send, recv, local, crossed,
):
    z, x, c, y = coords()
    copies = Copies(send, recv, local)
    steps = []
    while 2 ** len(steps) < depth:
        steps.append(2 ** len(steps))
    levels = len(steps)
    split = min(2, levels)
    bits = [(z // s) % 2 for s in steps]
    z_partner = [z + s - 2 * s * b for s, b in zip(steps, bits)]
    near = [{"c": 1 - c}, {"y": 1 - y}, {"x": 1 - x}] + [{"z": p} for p in z_partner]
    quad = []
    if split == 2:
        for flips in ((1, 0), (0, 1), (1, 1)):
            theirs = [b + f - 2 * f * b for b, f in zip(bits, flips)]
            quad.append((z + theirs[0] - bits[0] + 2 * (theirs[1] - bits[1]), theirs))
    same = c == y
    rows, dim = low.shape
    half = rows - SEG
    width = b_e.shape[2]
    quarter = dim // 4
    ffn_rows = 2 * dim
    first_row, parts = {}, {}
    ffn_chunks = ffn_rows // CHUNK
    for n in range(ffn_chunks):
        first_row[n], parts[n] = n * CHUNK, CHUNK
    qkv_chunks, out_chunks = [], []
    row = ffn_rows
    while row < ffn_rows + 4 * quarter:
        end = ffn_rows + (3 if row < ffn_rows + 3 * quarter else 4) * quarter
        n = len(parts)
        first_row[n], parts[n] = row, min(128, end - row)
        (qkv_chunks if row < ffn_rows + 3 * quarter else out_chunks).append(n)
        row += parts[n]
    every, waited, x_first, direct = [], set(), set(), set()

    def at(k):
        return pl.ds(first_row[k], parts[k])

    def go(copy):
        copy.start()
        every.append(copy)
        return copy

    def arrived(copy):
        copy.wait_recv()
        waited.add(id(copy))

    loads = {}

    def load(name, *pairs):
        loads[name] = [copies.here(src, dst) for src, dst in pairs]
        for copy in loads[name]:
            copy.start()

    def loaded(name):
        for copy in loads.pop(name, ()):
            copy.wait()

    chunks = [(False, 1 - c), (False, c), (True, 1 - c), (True, c)]

    def load_ffn(n, kind):
        own, h = chunks[n]
        cut = pl.ds(pl.multiple_of(h * dim, 128), dim)
        refs = {"wu": (wu_i, wu_o), "wd": (wd_i, wd_o), "act": (act_i, act_o), "slope": (slope_i, slope_o)}
        ref = refs[kind][0 if own else 1]
        slot_at = 2 * ("wu", "wd", "act", "slope").index(kind) + n % 2
        load((kind, n), (ref.at[cut] if kind == "wd" else ref.at[:, cut], slots.at[slot_at]))

    load("low", (low_h, low))
    load_ffn(0, "act")
    load_ffn(1, "act")
    load_ffn(0, "wd")
    load_ffn(0, "slope")
    load("hidden", (hidden_h, hidden))
    load_ffn(1, "wd")
    load_ffn(1, "slope")
    load("second", (second_h, total.at[pl.ds(0, rows)]))
    load_ffn(0, "wu")
    load_ffn(1, "wu")
    greet(near + [{"z": p} for p, _ in quad[2:]] + [{"c": 1 - c, "y": 1 - y}])

    out_d = pltpu.make_async_remote_copy(
        src_ref=output_h.at[pl.ds(SEG, half)], dst_ref=out_o, send_sem=crossed.at[0], recv_sem=crossed.at[1],
        device_id={"c": 1 - c, "y": 1 - y}, device_id_type=MESH_IDS,
    )
    mid_b = [slots.at[0, pl.ds(n * half, half)] for n in range(2)]
    in_d = pltpu.make_async_remote_copy(
        src_ref=mid_b[1], dst_ref=in_o, send_sem=crossed.at[2], recv_sem=crossed.at[3],
        device_id={"c": 1 - c, "y": 1 - y}, device_id_type=MESH_IDS,
    )

    load("mid", (wo_i, wo.at[pl.ds(0, width)]), (wo_o, wo.at[pl.ds(width, width)]), (ctx_h, ctx), (normed_h, normed), (inv_h, inv), (x_h, x_s))

    def add(n, out, *ins):
        tile = next(t for t in (48, 32, 16) if n % t == 0)

        def step(i, _):
            rows_at = pl.ds(pl.multiple_of(i * tile, 16), tile)
            value = ins[0][rows_at].astype(F32)
            for other in ins[1:]:
                value = value + other[rows_at].astype(F32)
            out[rows_at] = value.astype(out.dtype)
            return 0

        lax.fori_loop(0, n // tile, step, 0)

    def add2(n, out, *ins):
        for part in range(2):
            add(n, out.at[part], *[v.at[part] for v in ins])

    got_e, got_i, got_y, got_x, got_z, back_z, put, got_bx = {}, {}, {}, {}, {}, {}, {}, {}

    def cores(own, k):
        buf, there, got = (b_i, c_i, got_i) if own else (b_e, c_e, got_e)
        got[k] = go(copies.to(buf.at[pl.ds(2, 2), at(k)], there.at[:, at(k)], c=1 - c))

    def to_y(k):
        arrived(got_e[k])
        mine = b_e.at[pl.ds(0, 2), at(k)]
        add2(parts[k], mine, mine, c_e.at[:, at(k)])
        got_y[k] = go(copies.to(mine, y_r.at[:, at(k)], y=1 - y))

    def to_x(k):
        arrived(got_i[k])
        mine = b_i.at[pl.ds(0, 2), at(k)]
        if k in x_first:
            add2(parts[k], mine, mine, c_i.at[:, at(k)])
        else:
            arrived(got_y[k])
            add2(parts[k], mine, mine, c_i.at[:, at(k)], y_r.at[:, at(k)])
        got_x[k] = go(copies.to(b_i.at[1, at(k)], x_r.at[at(k)], x=1 - x))

    def base(k, level):
        row, size = first_row[k], parts[k]
        for n in range(min(level, split)):
            size //= 2
            row = row + bits[n] * size
        return row, size

    def slot(k, level):
        cut = 2 ** (level + 1)
        return (z_a, z_b)[level].at[pl.ds(first_row[k] // cut, parts[k] // cut)]

    def extra(k, n):
        return zx_r.at[n, pl.ds(first_row[k] // 4, parts[k] // 4)]

    got_q, back_q = {}, {}

    def quad_slot(k, n):
        size = parts[k] // 4
        if n < 2:
            return z_a.at[pl.ds(first_row[k] // 2 + n * size, size)]
        return z_b.at[pl.ds(first_row[k] // 4, size)]

    def to_quad(k):
        arrived(got_x[k])
        mine = b_i.at[0, at(k)]
        add(parts[k], mine, mine, x_r.at[at(k)])
        size = parts[k] // 4
        for n, (partner, theirs) in enumerate(quad):
            row = first_row[k] + theirs[0] * 2 * size + theirs[1] * size
            away = b_i.at[0, pl.ds(pl.multiple_of(row, 16), size)]
            got_q[k, n] = go(copies.to(away, quad_slot(k, n), z=partner))

    def from_quad(k):
        put[k].wait()
        for n in range(3):
            arrived(back_q[k, n])
        after_z(k)

    got_ex, got_ez = {}, {}

    def e_x(k):
        arrived(got_e[k])
        mine = b_e.at[pl.ds(0, 2), at(k)]
        add2(parts[k], mine, mine, c_e.at[:, at(k)])
        got_ex[k] = go(copies.to(b_e.at[1, at(k)], y_r.at[1, at(k)], x=1 - x))

    def e_z(k, level):
        row, size = base(k, level)
        region = lambda first, n: pl.ds(pl.multiple_of(first, 16), n)
        mine = b_e.at[0, region(row, size)]
        if level == 0:
            arrived(got_ex[k])
            add(size, mine, mine, y_r.at[1, at(k)])
        else:
            arrived(got_ez[k, level - 1])
            before = base(k, level - 1)[0]
            add(size, mine, mine, y_r.at[0, region(before + (1 - bits[level - 1]) * size, size)])
        if level < split:
            size //= 2
            away = b_e.at[0, region(row + (1 - bits[level]) * size, size)]
            place = y_r.at[0, region(row + bits[level] * size, size)]
            got_ez[k, level] = go(copies.to(away, place, z=z_partner[level]))
        else:
            got_y[k] = go(copies.to(mine, y_r.at[0, region(row, size)], y=1 - y))

    def to_z(k, level):
        row, size = base(k, level)
        mine = b_i.at[0, pl.ds(pl.multiple_of(row, 16), size)]
        if level == 0:
            arrived(got_x[k])
            add(size, mine, mine, x_r.at[at(k)])
        elif level == split and k in direct:
            for n in range(3):
                arrived(got_q[k, n])
            add(size, mine, mine, *[quad_slot(k, n) for n in range(3)])
        else:
            if level > split:
                got_z[k, level - 1].wait()
            else:
                arrived(got_z[k, level - 1])
            came = [slot(k, level - 1) if level <= split else extra(k, level - 1 - split)]
            if k in x_first and level == split:
                arrived(got_y[k])
                came.append(y_r.at[0, pl.ds(pl.multiple_of(row, 16), size)])
            add(size, mine, mine, *came)
        if level < split:
            size //= 2
            out = b_i.at[0, pl.ds(pl.multiple_of(row + (1 - bits[level]) * size, 16), size)]
            got_z[k, level] = go(copies.to(out, slot(k, level), z=z_partner[level]))
        elif level < levels:
            got_z[k, level] = copies.to(mine, extra(k, level - split), z=z_partner[level])
            got_z[k, level].start()
        else:
            place = sums_o.at[0, pl.ds(pl.multiple_of(row, 16), size)]
            put[k] = copies.here(mine, place)
            put[k].start()
            if k in direct:
                for n, (partner, _) in enumerate(quad):
                    back_q[k, n] = go(copies.to(mine, place, z=partner))
            elif split:
                back_z[k, split - 1] = go(copies.to(mine, place, z=z_partner[split - 1]))

    def from_z(k, level):
        if level == max(split, 1) - 1:
            put[k].wait()
        if split:
            arrived(back_z[k, level])
        if level > 0:
            row, size = base(k, level)
            place = sums_o.at[0, pl.ds(pl.multiple_of(row, 16), size)]
            back_z[k, level - 1] = go(copies.to(place, place, z=z_partner[level - 1]))
        else:
            after_z(k)

    def after_z(k):
        mine = sums_o.at[0, at(k)]
        got_bx[k] = go(copies.to(mine, sums_o.at[1, at(k)], x=1 - x))
        go(copies.to(mine, sums_o.at[2, at(k)], c=1 - c))

    def from_x(k):
        arrived(got_bx[k])
        go(copies.to(sums_o.at[1, at(k)], sums_o.at[3, at(k)], c=1 - c))

    vec_copies = {}

    def vec_start(n):
        source = vecs if n == 0 else vec_r.at[2 * n - 1]
        vec_copies[n] = go(copies.to(source, vec_r.at[2 * n], **near[n]))

    def vec_next(n):
        arrived(vec_copies[n])
        value = (vecs if n == 0 else vec_r.at[2 * n - 1])[...] + vec_r[2 * n]
        if n == len(near) - 1:
            vec_o[...] = value
        else:
            vec_r[2 * n + 1] = value
            vec_start(n + 1)

    work = []

    def step(us, body, *arguments):
        work.append((us * BACK_PACE, body, arguments))

    now = [3.0]

    def run_until(time):
        while tasks and tasks[0][0] <= time:
            _, task, its = tasks.pop(0)
            task(*its)

    def poll(us):
        now[0] += us * BACK_PACE
        run_until(now[0])

    def put_columns(buf, row, left, right, keep):
        for r in range(0, dim, TILE):
            grads = mm_tn(left[:, r : r + TILE], right[...]).astype(BF16)
            for part in range(2):
                rel = (0 if keep else 2) + (part + x) % 2
                buf[rel, row + r : row + r + TILE] = grads[:, part * width : (part + 1) * width]
            poll(0.45)

    def put_rows(buf, group, p, grads):
        rel = 2 * ((p // 2 + c) % 2) + (p % 2 + x) % 2
        buf[rel, ffn_rows + group * quarter : ffn_rows + (group + 1) * quarter] = grads

    inner_at = (d3.at[pl.ds(0, rows), pl.ds(0, dim)], dctx)

    def inner_grad(n):
        own, h = chunks[n]
        loaded(("wd", n))
        loaded(("slope", n))
        s = n % 2
        bias = 0.0
        for r in range(0, rows, TILE):
            at = slice(r, r + TILE)
            grad = (mm_nt(low[at], slots[2 + s]) * slots[6 + s, at].astype(F32)).astype(BF16)
            inner_at[s][at] = grad
            bias += jnp.sum(grad.astype(F32), axis=0, keepdims=True)
            poll(0.5)
        for part in range(2):
            row = 4 * (y if own else 1 - y) + 2 * h + part
            vecs[pl.ds(row, 1)] = bias[:, part * width : (part + 1) * width]
        if n < 2:
            load_ffn(n + 2, "wd")
            load_ffn(n + 2, "slope")

    def hidden_grad(n):
        loaded("second")
        loaded(("wu", n))
        for r in range(0, rows, TILE):
            at = slice(r, r + TILE)
            total[at] += mm_nt(inner_at[n % 2][at], slots[n % 2])
            poll(0.45)
        if n < 2:
            load_ffn(n + 2, "wu")
        if n == 3:
            load_attention()

    def up_grad(n):
        own = chunks[n][0]
        loaded("hidden")
        put_columns(b_i if own else b_e, 0, hidden, inner_at[n % 2], n % 2 == 1)
        if n % 2 == 0:
            for k in range(ffn_chunks // 2):
                cores(own, k)

    def down_grad(n):
        own = chunks[n][0]
        loaded("low")
        loaded(("act", n))
        put_columns(b_i if own else b_e, dim, low, slots.at[4 + n % 2], n % 2 == 1)
        if n % 2 == 0:
            for k in range(ffn_chunks // 2, ffn_chunks):
                cores(own, k)
        if n < 2:
            load_ffn(n + 2, "act")

    def load_attention():
        left, right = pl.ds(0, width), pl.ds(width, width)
        load(
            "att",
            (q_h, slots.at[0]),
            (k_h.at[pl.ds(0, SEG)], slots.at[2, pl.ds(0, SEG)]),
            (k_h.at[pl.ds(SEG, SEG)], slots.at[4, pl.ds(0, SEG)]),
            (v_h.at[pl.ds(0, SEG)], slots.at[6, pl.ds(0, SEG)]),
            (v_h.at[pl.ds(SEG, SEG)], slots.at[1, pl.ds(0, SEG)]),
        )
        load(
            "att_w",
            (wq_i, slots.at[3, :, left]),
            (wk_i, slots.at[3, :, right]),
            (wv_i, slots.at[5, :, left]),
            (wv_o, slots.at[5, :, right]),
            (wq_o, slots.at[7, :, left]),
            (wk_o, slots.at[7, :, right]),
        )
        load_probs(0)
        load_probs(1)

    pairs = width // PAIR
    pair_order = [pairs + n for n in range(pairs)] + list(range(pairs))

    def load_probs(n):
        pair = pair_order[n]
        load(
            ("p", n),
            (pa_h.at[pl.ds(2 * pair, 2)], p_a.at[n % 2]),
            (pm_h.at[pl.ds(2 * pair, 2)], p_m.at[n % 2]),
        )

    def out_back():
        loaded("mid")
        sums = [0.0, 0.0, 0.0]
        gain_row = gain[...].astype(F32).reshape(1, dim)
        for r in range(0, rows, TILE):
            tile = slice(r, r + TILE)
            grad_in = total[tile]
            n = normed[tile].astype(F32)
            scaled = grad_in * gain_row
            grad = inv[tile] * (
                scaled
                - jnp.mean(scaled, axis=-1, keepdims=True)
                - n * jnp.mean(scaled * n, axis=-1, keepdims=True)
            )
            sums[0] += jnp.sum(grad_in * n, axis=0, keepdims=True)
            sums[1] += jnp.sum(grad_in, axis=0, keepdims=True)
            sums[2] += jnp.sum(grad, axis=0, keepdims=True)
            total[tile] = grad
            low[tile] = grad.astype(BF16)
        for i, value in enumerate(sums):
            for part in range(2):
                cut = slice(part * width, (part + 1) * width)
                vecs[12 + 2 * i + part : 13 + 2 * i + part] = value[:, cut]
                vecs[18 + 2 * i + part : 19 + 2 * i + part] = vec2[i : i + 1, cut]
        total[rows:] = jnp.zeros((half, dim), F32)
        d3[rows:, :width] = jnp.zeros((half, width), BF16)

    def out_grads():
        for pair in range(2):
            grads = mm_tn(low[:, 2 * pair * quarter : 2 * (pair + 1) * quarter], ctx[...]).astype(BF16)
            for n in range(2):
                at = slice(n * quarter, (n + 1) * quarter)
                put_rows(b_i, 3, 2 * pair + n, grads[at, :width])
                put_rows(b_e, 3, 2 * pair + n, grads[at, width:])
            poll(0.7)
        for k in out_chunks:
            cores(False, k)
            cores(True, k)

    def context_grad():
        for r in range(0, rows, TILE):
            at = slice(r, r + TILE)
            dctx[at] = mm_nt(low[at], wo[...]).astype(BF16)
            poll(0.4)

    def attend(n):
        pair = pair_order[n]
        cols = slice(pair * PAIR, (pair + 1) * PAIR)
        local_at = (pair % pairs) * PAIR
        if n == 0:
            loaded("att")
        loaded(("p", n))
        lane = lax.broadcasted_iota(jnp.int32, (1, PAIR), 1) // HEAD_DIM
        zero = jnp.zeros((), BF16)
        for first, count, key_first, k_slot, v_slot, probs_ref in (
            (0, SEG, 0, 2, 6, p_a),
            (SEG, half, SEG, 4, 1, p_m),
        ):
            q_at = slice(first, first + count)
            ks = slice(key_first, key_first + SEG)
            grad2, query2 = dctx[q_at, cols], slots[0, q_at, cols]
            keys, values = slots[k_slot, :SEG, cols], slots[v_slot, :SEG, cols]
            delta_t = (grad2.astype(F32) * ctx[q_at, cols].astype(F32)).T
            values_grad = keys_grad = query_grad = 0.0
            for h in range(2):
                grad_h = jnp.where(lane == h, grad2, zero)
                query_h = jnp.where(lane == h, query2, zero)
                keys_h = jnp.where(lane == h, keys, zero)
                probs = probs_ref[n % 2, h]
                delta = jnp.sum(delta_t[h * HEAD_DIM : (h + 1) * HEAD_DIM], axis=0, keepdims=True)
                prob_grad = mm_nt(values, grad_h)
                score_grad = (probs.astype(F32) * (prob_grad - delta)).astype(BF16)
                values_grad += mm(probs, grad_h)
                keys_grad += mm(score_grad, query_h)
                query_grad += mm_tn(score_grad, keys_h)
                poll(0.7 if first == 0 else 0.35)
            for part, value, out_at in (
                (0, query_grad * HEAD_DIM**-0.5, q_at),
                (1, keys_grad, ks),
                (2, values_grad, ks),
            ):
                d3[out_at, part * width + local_at : part * width + local_at + PAIR] = value.astype(BF16)
        if n + 2 < 2 * pairs:
            load_probs(n + 2)

    def input_part(own):
        loaded("att_w")
        main = 3 if own else 7
        last = slice(0, width) if own else slice(width, 2 * width)
        for r in range(0, rows + half, TILE):
            at = slice(r, r + TILE)
            total[at] += mm_nt(d3[at, : 2 * width], slots[main]) + mm_nt(
                d3[at, 2 * width :], slots[5, :, last]
            )
            poll(0.7)

    def weight_part(own):
        buf = b_i if own else b_e
        for pair in range(2):
            grads = mm_tn(x_s[:, 2 * pair * quarter : 2 * (pair + 1) * quarter], d3[...]).astype(BF16)
            for n in range(2):
                at = slice(n * quarter, (n + 1) * quarter)
                for group in range(3):
                    put_rows(buf, group, 2 * pair + n, grads[at, group * width : (group + 1) * width])
            poll(1.4)
        for k in qkv_chunks:
            cores(own, k)
        row = y if own else 1 - y
        vecs[pl.ds(8 + row, 1)] = jnp.sum(d3[:rows, :width].astype(F32), axis=0, keepdims=True)
        vecs[pl.ds(10 + row, 1)] = jnp.sum(d3[:, 2 * width :].astype(F32), axis=0, keepdims=True)

    done = []

    def leave(first, count):
        copy = copies.here(total.at[pl.ds(first, count)], top_o.at[pl.ds(first, count)])
        copy.start()
        done.append(copy)

    def finish():
        mid_b[0][...] = total[rows:].astype(BF16)
        done.append(go(copies.to(mid_b[0], mid_r, c=1 - c)))
        leave(0, SEG)
        vec_start(0)

    def middle():
        arrived(done[0])
        value = total[SEG:rows] + mid_r[...].astype(F32)
        total[SEG:rows] = value
        mid_b[1][...] = value.astype(BF16)
        leave(SEG, half)

        @pl.when(jnp.logical_not(same))
        def _():
            in_d.start()
            out_d.start()

    ready_e, ready_i = {}, {}
    clock = 3.0
    for n in (0, 2):
        step(1.4, down_grad, n)
        step(1.4, down_grad, n + 1)
        step(1.5, inner_grad, n)
        step(1.4, up_grad, n)
        step(1.5, inner_grad, n + 1)
        step(1.4, up_grad, n + 1)
        step(1.3, hidden_grad, n)
        step(1.3, hidden_grad, n + 1)
    step(1.6, out_back)
    step(1.4, out_grads)
    step(1.2, context_grad)
    for n in range(2 * pairs):
        step(2.1, attend, n)
        if n % pairs == pairs - 1:
            step(3.0, weight_part, n > pairs)
            step(2.8, input_part, n > pairs)
    step(0.7, finish)
    when = {}
    for us, body, arguments in work:
        clock += us
        when[(body, *arguments)] = clock
    for k in parts:
        if k < ffn_chunks:
            ready = (up_grad, down_grad)[2 * k // ffn_chunks]
            ready_e[k], ready_i[k] = when[ready, 1], when[ready, 3]
        elif k in out_chunks:
            ready_e[k] = ready_i[k] = when[(out_grads,)] + 1.5
        else:
            ready_e[k], ready_i[k] = when[weight_part, False] + 1.5, when[weight_part, True] + 1.5
    chunk_order = {
        k: parts[k] for k in [*range(ffn_chunks // 2, ffn_chunks), *range(ffn_chunks // 2), *out_chunks, *qkv_chunks]
    }
    if split == 2:
        listed = list(chunk_order)
        x_first.update(listed[n] for n in X_FIRST)
        direct.update(listed[n] for n in DIRECT)
    tasks = []
    for time, stage, k in plan(chunk_order, x_first, direct, levels, split, ready_e, ready_i):
        if stage == "y":
            tasks.append((time, to_y, (k,)))
        elif stage == "ex":
            tasks.append((time, e_x, (k,)))
        elif stage == "ey":
            tasks.append((time, e_z, (k, split)))
        elif stage[0] == "ez":
            tasks.append((time, e_z, (k, stage[1])))
        elif stage == "x":
            tasks.append((time, to_x, (k,)))
        elif stage == "end":
            tasks.append((time, from_x, (k,)))
        elif stage == "zq":
            tasks.append((time, to_quad, (k,)))
        elif stage == "fq":
            tasks.append((time, to_z, (k, levels)))
        elif stage == "fx" and k in direct:
            tasks.append((time, from_quad, (k,)))
        elif stage == "fx":
            if not split:
                tasks.append((time, to_z, (k, levels)))
            tasks.append((time, from_z, (k, 0)))
        elif stage[0] == "z":
            tasks.append((time, to_z, (k, stage[1])))
        elif stage[1] == split - 1:
            tasks.append((time, to_z, (k, levels)))
        else:
            tasks.append((time, from_z, (k, stage[1] + 1)))
    end = when[(finish,)]
    last_y = max(time for time, task, _ in tasks if task in (to_y, e_z))
    tasks.append((max(end + 4.0, last_y + 0.1), middle, ()))
    for n in range(len(near)):
        tasks.append((end + 5.0 + 5.0 * n, vec_next, (n,)))
    tasks.sort(key=lambda t: t[0])
    clock = 3.0
    for us, body, arguments in work:
        run_until(clock)
        now[0] = clock
        body(*arguments)
        clock += us
    run_until(1e9)

    @pl.when(jnp.logical_not(same))
    def _():
        out_d.wait()
        in_d.wait()

    for copy in done[1:]:
        copy.wait()
    for copy in every:
        copy.wait_send()
        if id(copy) not in waited:
            copy.wait_recv()


def final_body(
    pos_ref, sums, top, output, top_mid, output_mid, in_mid, out_mid, vec,
    out_o, in_o, q_o, k_o, v_o, wo_o, up_o, down_o, bq_o, bv_o, bu_o, n1g_o, n1b_o, bo_o, n2g_o, n2b_o, bd_o, tmp,
):
    j = pl.program_id(0)
    dim = up_o.shape[0]
    quarter, width = q_o.shape
    same = pos_ref[1] == pos_ref[2]
    is_mid = jnp.where(pos_ref[2] == 0, j >= 2, j == 0)

    @pl.when(is_mid & same)
    def _():
        out_o[...] = output_mid[...]
        in_o[...] = top_mid[...]

    @pl.when(is_mid & jnp.logical_not(same))
    def _():
        out_o[...] = out_mid[...]
        in_o[...] = in_mid[...].astype(F32)

    @pl.when(jnp.logical_not(is_mid))
    def _():
        out_o[...] = output[...]
        in_o[...] = top[...]

    @pl.when(j == 0)
    def _():
        bq_o[...] = vec[pl.ds(8 + pos_ref[2], 1)].reshape(width)
        bv_o[...] = vec[pl.ds(10 + pos_ref[2], 1)].reshape(width)
        parts = [vec[pl.ds(4 * pos_ref[2] + n, 1)] for n in range(4)]
        bu_o[...] = jnp.concatenate(parts, axis=1).reshape(4 * width)
        for n, ref in enumerate((n1g_o, n1b_o, bo_o, n2g_o, n2b_o, bd_o)):
            ref[...] = wide_row(vec, 12 + 2 * n).reshape(dim)

    up_o[...] = sums[0, :dim].astype(F32)
    down_o[...] = sums[0, dim : 2 * dim].astype(F32).T
    for part, ref in enumerate((q_o, k_o, v_o)):
        at = 2 * dim + part * quarter
        ref[...] = sums[0, at : at + quarter].astype(F32)
    row = pl.multiple_of((pos_ref[0] ^ j) * quarter, 16)
    at = 2 * dim + 3 * quarter
    tmp[pl.ds(row, quarter), :] = sums[0, at : at + quarter].astype(F32)

    @pl.when(j == pl.num_programs(0) - 1)
    def _():
        wo_o[...] = tmp[...].T


def shards(
    depth,
    tokens, lengths, buckets, w_query, b_query, w_key, w_value, b_value, w_out, b_out,
    norm1_gain, norm1_bias, w_up, b_up, w_down, b_down, norm2_gain, norm2_bias, cotangent,
):
    ix, ic, iy = (lax.axis_index(a) for a in ("x", "c", "y"))
    pos = jnp.stack([2 * ic + ix, ic, iy]).astype(jnp.int32)
    rows, dim = tokens.shape
    half = rows - SEG
    width = w_query.shape[1]
    units = w_up.shape[1]
    chunk = units // 4
    any_space = pl.BlockSpec(memory_space=pl.ANY)
    in_vmem = pl.BlockSpec(memory_space=pltpu.VMEM)

    weights = (w_query, w_key, w_value, w_out, w_up, w_down)
    total = rows + half
    square = (rows, dim)
    wide = (rows, units)
    pairs = width // PAIR
    made = [
        shape((total, dim), BF16),
        *[shape(w.shape, BF16) for w in weights],
        shape(square, BF16),
        shape((total, dim), BF16),
        shape((total, dim), BF16),
        shape((4 * pairs, SEG, SEG), BF16),
        shape((4 * pairs, SEG, half), BF16),
        shape(square, BF16),
        shape(square, BF16),
        shape((rows, 1), F32),
        shape(square, BF16),
        *[shape(wide, BF16)] * 4,
        shape(square, F32),
        shape(square, BF16),
        shape(square, BF16),
        shape((3, dim), F32),
    ]
    (
        x, wq_o, wk_o, wv_o, wo_o, wu_o, wd_o, query, keys, values, probs_a, probs_m, ctx, normed1, inverse1, hidden,
        act_i, act_o, slope_i, slope_o, second, low, output, vec2,
    ) = pl.pallas_call(
        forward_body,
        out_shape=made,
        in_specs=[any_space] * 8 + [in_vmem] * 9 + [pl.BlockSpec(memory_space=pltpu.SMEM)] * 2,
        out_specs=[any_space] * (len(made) - 1) + [in_vmem],
        scratch_shapes=[
            pltpu.VMEM((total, dim), BF16),
            pltpu.VMEM(square, BF16),
            pltpu.VMEM((2, dim, 3 * width), BF16),
            pltpu.VMEM((2 * width, dim), BF16),
            pltpu.VMEM((2, dim, units), BF16),
            pltpu.VMEM((2, units, dim), BF16),
            pltpu.VMEM(square, BF16),
            *[pltpu.VMEM((total, dim), BF16)] * 2,
            pltpu.VMEM((3, 2, SEG, SEG), BF16),
            pltpu.VMEM((3, 2, SEG, half), BF16),
            *[pltpu.VMEM(square, BF16)] * 2,
            pltpu.VMEM((rows, 1), F32),
            pltpu.VMEM(square, BF16),
            pltpu.VMEM(square, F32),
            *[pltpu.VMEM((2, *wide), BF16)] * 2,
            *[pltpu.VMEM(square, BF16)] * 2,
            pltpu.VMEM((rows, 1), F32),
            pltpu.VMEM((SEG, SEG), F32),
            pltpu.VMEM((SEG, half), F32),
            pltpu.VMEM((24, width), F32),
            pltpu.VMEM((8, 128), F32),
            pltpu.VMEM((24, width), F32),
            *[pltpu.VMEM((8, 128), F32)] * 2,
            pltpu.SemaphoreType.DMA((96,)),
            pltpu.SemaphoreType.DMA((96,)),
            pltpu.SemaphoreType.DMA((64,)),
            pltpu.SemaphoreType.DMA((2,)),
        ],
        compiler_params=pltpu.CompilerParams(
            collective_id=1, has_side_effects=True, vmem_limit_bytes=VMEM_LIMIT
        ),
        name="forward",
    )(
        tokens, cotangent, *weights, b_query, b_value, b_up, b_out, norm1_gain, norm1_bias, b_down, norm2_gain, norm2_bias,
        buckets, lengths,
    )

    levels = depth.bit_length() - 1
    more = max(levels - 2, 0)
    size = 3 * dim
    links = levels + 3
    remote = 16 * (levels + 12) + links + 12
    sums, top, vec, in_mid, out_mid = pl.pallas_call(
        functools.partial(backward_body, depth),
        out_shape=[
            shape((4, size, width), BF16),
            shape((rows, dim), F32),
            shape((24, width), F32),
            shape((half, dim), BF16),
            shape((half, dim), BF16),
        ],
        in_specs=[any_space] * 29 + [in_vmem] * 2,
        out_specs=[any_space] * 2 + [in_vmem] + [any_space] * 2,
        scratch_shapes=[
            *[pltpu.VMEM((rows, dim), BF16)] * 2,
            pltpu.VMEM((8, rows, dim), BF16),
            pltpu.VMEM((rows + half, dim), F32),
            *[pltpu.VMEM((4, size, width), BF16)] * 2,
            *[pltpu.VMEM((2, size, width), BF16)] * 3,
            pltpu.VMEM((size, width), BF16),
            pltpu.VMEM((size // 2, width), BF16),
            pltpu.VMEM((size // 4, width), BF16),
            pltpu.VMEM((max(more, 1), size // 4 if more else 16, width), BF16),
            pltpu.VMEM((rows, dim), BF16),
            pltpu.VMEM((rows, 1), F32),
            *[pltpu.VMEM((rows, dim), BF16)] * 3,
            pltpu.VMEM((rows + half, dim), BF16),
            pltpu.VMEM((2, 2, SEG, SEG), BF16),
            pltpu.VMEM((2, 2, SEG, half), BF16),
            pltpu.VMEM((rows + half, 3 * width), BF16),
            pltpu.VMEM((24, width), F32),
            pltpu.VMEM((2 * links, 24, width), F32),
            pltpu.VMEM((half, dim), BF16),
            pltpu.SemaphoreType.DMA((remote,)),
            pltpu.SemaphoreType.DMA((remote,)),
            pltpu.SemaphoreType.DMA((80,)),
            pltpu.SemaphoreType.DMA((4,)),
        ],
        compiler_params=pltpu.CompilerParams(
            collective_id=2, has_side_effects=True, vmem_limit_bytes=VMEM_LIMIT
        ),
        name="backward",
    )(
        low, hidden, act_i, act_o, slope_i, slope_o, w_up, wu_o, w_down, wd_o, second, normed1, inverse1,
        w_out, wo_o, ctx, x, query, keys, values, probs_a, probs_m, w_query, w_key, w_value, wq_o, wk_o, wv_o,
        output, norm1_gain, vec2,
    )
    quarter = dim // 4
    const = lambda *dims: pl.BlockSpec(dims, lambda j, pos: (0,) * len(dims))
    full_block = lambda j, pos: (jnp.where(pos[2] == 0, jnp.minimum(j, 1), jnp.clip(j - 1, 0, 1)), 0)
    row_block = pl.BlockSpec((half, dim), lambda j, pos: (jnp.minimum(j, 2), 0))
    by_rows = lambda n, m: pl.BlockSpec((n, m), lambda j, pos: (pos[0] ^ j, 0))
    (
        output, input_grad, w_query_grad, w_key_grad, w_value_grad, w_out_grad, w_up_grad, w_down_grad,
        b_query_grad, b_value_grad, b_up_grad, norm1_gain_grad, norm1_bias_grad, b_out_grad,
        norm2_gain_grad, norm2_bias_grad, b_down_grad,
    ) = call(
        final_body,
        (4,),
        pos,
        [sums, top, output, top, output, in_mid, out_mid, vec],
        [
            pl.BlockSpec((1, size, width), lambda j, pos: (j, 0, 0)),
            pl.BlockSpec((half, dim), full_block),
            pl.BlockSpec((half, dim), full_block),
            *[pl.BlockSpec((half, dim), lambda j, pos: (2, 0))] * 2,
            whole(in_mid),
            whole(out_mid),
            whole(vec),
        ],
        [
            shape((rows, dim), BF16),
            shape((rows, dim), F32),
            *[shape((dim, width), F32)] * 3,
            shape((width, dim), F32),
            shape((dim, units), F32),
            shape((units, dim), F32),
            *[shape((n,), F32) for n in (width, width, units, *[dim] * 6)],
        ],
        [
            row_block,
            row_block,
            *[by_rows(quarter, width)] * 3,
            const(width, dim),
            pl.BlockSpec((dim, chunk), lambda j, pos: (0, pos[0] ^ j)),
            by_rows(chunk, dim),
            *[const(n) for n in (width, width, units, *[dim] * 6)],
        ],
        [pltpu.VMEM((dim, width), F32)],
        0,
        "final",
    )
    return (
        output,
        input_grad,
        w_query_grad,
        b_query_grad,
        w_key_grad,
        w_value_grad,
        b_value_grad,
        w_out_grad,
        b_out_grad,
        norm1_gain_grad,
        norm1_bias_grad,
        w_up_grad,
        b_up_grad,
        w_down_grad,
        b_down_grad,
        norm2_gain_grad,
        norm2_bias_grad,
    )


def solution(mesh):
    depth = mesh.shape["dp"] // 4
    inner = Mesh(mesh.devices.reshape(depth, 2, 2, mesh.shape["mp"]), ("z", "x", "c", "y"))
    dp = ("z", "x", "c")
    every = (*dp, "y")
    placed = (
        P(every, None),
        P(dp, None),
        P(dp),
        P(None, "y"),
        P("y"),
        P(None, "y"),
        P(None, "y"),
        P("y"),
        P("y", None),
        P(),
        P(),
        P(),
        P(None, "y"),
        P("y"),
        P("y", None),
        P(),
        P(),
        P(),
        P(every, None),
    )
    return jax.shard_map(
        functools.partial(shards, depth),
        mesh=inner,
        in_specs=placed,
        out_specs=(
            P(every, None),
            P(every, None),
            P(None, "y"),
            P("y"),
            P(None, "y"),
            P(None, "y"),
            P("y"),
            P("y", None),
            P(),
            P(),
            P(),
            P(None, "y"),
            P("y"),
            P("y", None),
            P(),
            P(),
            P(),
        ),
        check_vma=False,
    )
```

```python
import functools

import jax
import jax.numpy as jnp
from jax import lax
from jax.experimental import pallas as pl
from jax.experimental.pallas import tpu as pltpu
from jax.sharding import Mesh, PartitionSpec as P

HEAD_DIM = 64
SEG = 512
PAIR = 2 * HEAD_DIM
NEG = -1e30
EPS = 1e-12
ROOT_HALF = 0.7071067811865476
INV_ROOT_TWO_PI = 0.3989422804014327
F32 = jnp.float32
BF16 = jnp.bfloat16
VMEM_LIMIT = 60 * 1024 * 1024
TILE = 256
CHUNK = 192
HOP_US = 3.2
BACK_HOP_US = 3.2
PACE = 1.15
BACK_PACE = 1.2
X_FIRST = (1, 3, 5, 7)
DIRECT = (8, 9, 10, 11, 12, 13, 14)
MESH_IDS = pl.DeviceIdType.MESH


def mm(left, right):
    return lax.dot_general(left, right, (((1,), (0,)), ((), ())), preferred_element_type=F32)


def mm_nt(left, right):
    return lax.dot_general(left, right, (((1,), (1,)), ((), ())), preferred_element_type=F32)


def mm_tn(left, right):
    return lax.dot_general(left, right, (((0,), (0,)), ((), ())), preferred_element_type=F32)


def call(body, grid, pos, inputs, in_specs, out_shape, out_specs, scratch, flops, name):
    moved = sum(v.size * v.dtype.itemsize for v in inputs) + sum(
        v.size * v.dtype.itemsize for v in out_shape
    )
    return pl.pallas_call(
        body,
        grid_spec=pltpu.PrefetchScalarGridSpec(
            num_scalar_prefetch=1,
            grid=grid,
            in_specs=in_specs,
            out_specs=out_specs,
            scratch_shapes=scratch,
        ),
        out_shape=out_shape,
        compiler_params=pltpu.CompilerParams(
            dimension_semantics=("arbitrary",) * len(grid), vmem_limit_bytes=VMEM_LIMIT
        ),
        cost_estimate=pl.CostEstimate(flops=flops, bytes_accessed=moved, transcendentals=0),
        name=name,
    )(pos, *inputs)


def whole(array):
    zeros = (0,) * array.ndim
    return pl.BlockSpec(array.shape, lambda j, pos: zeros)


def shape(dims, kind):
    return jax.ShapeDtypeStruct(dims, kind)


def gelu_parts(inner):
    erf = lax.erf(inner * ROOT_HALF)
    below = 0.5 + 0.5 * erf
    density = jnp.exp(inner * inner * -0.5) * INV_ROOT_TWO_PI
    return inner * below, below + inner * density


def row_ids(info, at, places):
    bucket = info[at : at + 1, 0:1]
    span = jnp.where(bucket < 0.5, 1.0 * SEG, jnp.where(bucket < 1.5, 0.5 * SEG, 0.25 * SEG))
    row = jnp.zeros_like(places)
    size = jnp.zeros_like(places) + info[at : at + 1, 1:2]
    for slot in range(1, 4):
        later = places >= span * slot
        row = jnp.where(later, 1.0 * slot, row)
        size = jnp.where(later, info[at : at + 1, slot + 1 : slot + 2], size)
    return row, places - row * span < size


def wide_row(ref, row):
    return jnp.concatenate([ref[row : row + 1], ref[row + 1 : row + 2]], axis=1)


class Copies:
    def __init__(self, send, recv, local):
        self.send, self.recv, self.local = send, recv, local
        self.remote_count = self.local_count = 0

    def to(self, src, dst, **device):
        n = self.remote_count
        self.remote_count += 1
        return pltpu.make_async_remote_copy(
            src_ref=src,
            dst_ref=dst,
            send_sem=self.send.at[n],
            recv_sem=self.recv.at[n],
            device_id=device,
            device_id_type=MESH_IDS,
        )

    def here(self, src, dst):
        n = self.local_count
        self.local_count += 1
        return pltpu.make_async_copy(src, dst, self.local.at[n])


def coords():
    return tuple(lax.axis_index(a) for a in ("z", "x", "c", "y"))


def greet(devices):
    barrier = pltpu.get_barrier_semaphore()
    for device in devices:
        pl.semaphore_signal(barrier, inc=1, device_id=device, device_id_type=MESH_IDS)
    pl.semaphore_wait(barrier, len(devices))


def forward_body(
    tokens, cot_h, wq, wk, wv, wo, wu, wd, b_q, b_v, b_u, b_o, gain1, bias1, b_d, gain2, bias2, buckets, lengths,
    x_o, wq_o, wk_o, wv_o, wo_o, wu_o, wd_o, q_o, k_o, v_o, pa_o, pm_o, ctx_o, normed_o, inv_o, hidden_o,
    act_io, act_oo, slope_io, slope_oo, second_o, low_o, out_o, vec_o,
    x_s, cot, w3, wo_s, wu_s, wd_s, q_s, k_s, v_s, p_a, p_m, ctx, normed, inv, hidden, acc, act, slope, low, out_s,
    keep, mask_a, mask_m, bias, info, bias_r, info_r, info_s, send, recv, local, crossed,
):
    z, x, c, y = coords()
    copies = Copies(send, recv, local)
    rows, dim = cot.shape
    shared = 2 + wu.shape[1] // wq.shape[1]

    def const(n):
        return wide_row(bias, shared + 2 * n)

    half = rows - SEG
    width = wq.shape[1]
    pairs = width // PAIR
    same = c == y
    full = pl.ds(pl.multiple_of(y * half, half), SEG)
    mid = pl.ds(pl.multiple_of((1 - y) * SEG, half), half)
    own_at, sib_at = pl.ds(SEG, half), pl.ds(SEG + half, half)
    loads, stores = {}, []

    def load(name, *moves):
        loads[name] = [copies.here(src, dst) for src, dst in moves]
        for copy in loads[name]:
            copy.start()

    def loaded(name):
        for copy in loads.pop(name, ()):
            copy.wait()

    def store(src, dst):
        copy = copies.here(src, dst)
        copy.start()
        stores.append(copy)
        return copy

    load(
        "qkv",
        (tokens.at[full], x_s.at[pl.ds(0, SEG)]),
        *[(w, w3.at[0, :, pl.ds(n * width, width)]) for n, w in enumerate((wq, wk, wv))],
    )
    x_own = copies.here(tokens.at[mid], x_s.at[own_at])
    cot_own = copies.here(cot_h.at[mid], cot.at[own_at])

    @pl.when(same)
    def _():
        x_own.start()
        cot_own.start()

    row = 0
    for ref in (b_q, b_v, b_u, b_o, gain1, bias1, b_d, gain2, bias2):
        for n in range(ref.shape[0] // width):
            bias[row : row + 1] = ref[n * width : (n + 1) * width].astype(F32).reshape(1, width)
            row += 1
    bias[row:] = jnp.zeros((bias.shape[0] - row, width), F32)
    lane = lax.broadcasted_iota(jnp.int32, (1, info.shape[1]), 1)
    info[...] = jnp.zeros_like(info)
    for n, block in enumerate((2 * y, 1)):
        value = jnp.where(lane == 0, buckets[block], 0)
        for slot in range(4):
            value = jnp.where(lane == slot + 1, lengths[block, slot], value)
        info[n : n + 1] = value.astype(F32)
    greet([{"y": 1 - y}, {"x": 1 - x}, {"c": 1 - c}, {"z": z + 1 - 2 * (z % 2)}, {"c": 1 - c, "y": 1 - y}])

    x_y = copies.to(tokens.at[mid], x_s.at[sib_at], y=1 - y)
    x_c1 = copies.to(x_s.at[own_at], x_s.at[sib_at], c=1 - c)
    x_c2 = copies.to(x_s.at[sib_at], x_s.at[own_at], c=1 - c)
    cot_d = pltpu.make_async_remote_copy(
        src_ref=cot_h.at[mid], dst_ref=cot.at[own_at], send_sem=crossed.at[0], recv_sem=crossed.at[1],
        device_id={"c": 1 - c, "y": 1 - y}, device_id_type=MESH_IDS,
    )
    info_copy = copies.to(info, info_r, c=1 - c)
    bias_copy = copies.to(bias, bias_r, y=1 - y)

    info_copy.start()
    bias_copy.start()

    z_next = z + 1 - 2 * (z % 2)
    zb = z % 2

    def rows_of(ref, first, count, part, columns=None):
        def cut(p, sub=0, subs=1):
            n = count // subs
            at = pl.ds(pl.multiple_of(first + (2 * c + p) * part + sub * n, 16), n)
            return ref.at[at] if columns is None else ref.at[at, columns]

        return cut

    def columns_of(ref, first, count):
        def cut(p, sub=0, subs=1):
            n, m = ref.shape[1] // 4, count // subs
            row = pl.multiple_of(first + sub * m, 16)
            return ref.at[pl.ds(row, m), pl.ds(pl.multiple_of((2 * c + p) * n, 128), n)]

        return cut

    arrays = []
    part = dim // 4
    for n, w in enumerate((wq, wk, wv)):
        cols = pl.ds(n * width, width)
        arrays.append(("qkv", "yxz", 3.1, rows_of(w, 0, part, part), rows_of(w3.at[1], 0, part, part, cols)))
    part = width // 4
    arrays.append(("wo", "yx", 3.1, rows_of(wo, 0, part, part), rows_of(wo_s, width, part, part)))
    for n in range(2):
        m = dim // 2
        arrays.append(("wu", "yxz", 6.2, columns_of(wu, n * m, m), columns_of(wu_s.at[1], n * m, m)))
    part = wd.shape[0] // 4
    for how, first, m in (("yxz", 0, 2), ("yx", 2, 1), ("yz", 3, 1)):
        first, m = first * part // 4, m * part // 4
        cuts = rows_of(wd, first, m, part), rows_of(wd_s.at[1], first, m, part)
        arrays.append(("wd", how, 12.4 * m / part, *cuts))
    over = {}

    def pass_on(n, hop, cut, **device):
        over[n, hop] = copies.to(cut, cut, **device)
        over[n, hop].start()

    def start(n):
        _, how, _, mine, there = arrays[n]
        if how == "yxz":
            src, dst = mine(x, zb, 2), there(x, zb, 2)
        else:
            p = x if how == "yx" else zb
            src, dst = mine(p), there(p)
        over[n, "y"] = copies.to(src, dst, y=1 - y)
        over[n, "y"].start()

    def from_y(n):
        _, how, _, _, there = arrays[n]
        over[n, "y"].wait_recv()
        cut = there(x, zb, 2) if how == "yxz" else there(x if how == "yx" else zb)
        if how != "yz":
            pass_on(n, "x", cut, x=1 - x)
        if how != "yx":
            pass_on(n, "z", cut, z=z_next)
        pass_on(n, "cy", cut, c=1 - c)

    def from_x(n):
        _, how, _, _, there = arrays[n]
        over[n, "x"].wait_recv()
        if how == "yxz":
            pass_on(n, "xz", there(1 - x, 2 * zb + 1, 4), z=z_next)
            pass_on(n, "cx", there(1 - x, zb, 2), c=1 - c)
        else:
            pass_on(n, "cx", there(1 - x), c=1 - c)

    def from_z(n):
        _, how, _, _, there = arrays[n]
        over[n, "z"].wait_recv()
        if how == "yxz":
            pass_on(n, "zx", there(x, 2 * (1 - zb), 4), x=1 - x)
            pass_on(n, "cz", there(x, 1 - zb, 2), c=1 - c)
        else:
            pass_on(n, "cz", there(1 - zb), c=1 - c)

    def from_both(n):
        over[n, "zx"].wait_recv()
        over[n, "xz"].wait_recv()
        pass_on(n, "cb", arrays[n][4](1 - x, 1 - zb, 2), c=1 - c)

    def mid_rows():
        @pl.when(same)
        def _():
            x_own.wait()
            x_y.wait_recv()
            x_c1.start()
            x_c2.start()

    tasks = [(13.5, mid_rows, ())]
    clock = 3.0
    ready = []
    for n, (_, how, us, _, _) in enumerate(arrays):
        start(n)
        if arrays[n][0] == "qkv" and arrays[n + 1][0] != "qkv":

            @pl.when(jnp.logical_not(same))
            def _():
                x_y.start()

        if n > 0 and arrays[n - 1][0] == "qkv" and arrays[n][0] != "qkv":
            clock += 4.1
        clock += us / 2 if how == "yxz" else us
        first = clock + HOP_US
        tasks.append((first, from_y, (n,)))
        for link in how[1:]:
            ready.append((first, link, n, us / 2 if how == "yxz" else us, 1))
    free = {"x": 0.0, "z": 0.0}
    both = {}
    while ready:
        item = min(ready, key=lambda v: (max(v[0], free[v[1]]), v[2]))
        ready.remove(item)
        time, link, n, us, hop = item
        free[link] = max(time, free[link]) + us
        come = free[link] + HOP_US
        if hop == 2:
            both.setdefault(n, []).append(come)
            if len(both[n]) == 2:
                tasks.append((max(both[n]), from_both, (n,)))
        else:
            tasks.append((come, from_x if link == "x" else from_z, (n,)))
            if arrays[n][1] == "yxz":
                ready.append((come, "z" if link == "x" else "x", n, us / 2, 2))
    tasks.sort(key=lambda t: t[0])

    @pl.when(jnp.logical_not(same))
    def _():
        cot_d.start()

    come = set()

    def run_until(time):
        while tasks and tasks[0][0] <= time:
            _, task, its = tasks.pop(0)
            task(*its)

    def need(name):
        if name in come:
            return
        come.add(name)
        while any(its and arrays[its[0]][0] == name for _, task, its in tasks):
            _, task, its = tasks.pop(0)
            task(*its)
        for n, array in enumerate(arrays):
            if array[0] == name:
                for hop in ("cy", "cx", "cz", "cb"):
                    if (n, hop) in over:
                        over[n, hop].wait_recv()

    load("wo", (wo, wo_s.at[pl.ds(0, width)]))
    load("wu", (wu, wu_s.at[0]))
    load("wd", (wd, wd_s.at[0]))
    load("cot", (cot_h.at[full], cot.at[pl.ds(0, SEG)]))

    work = []

    def step(us, body, *arguments):
        work.append((us * PACE, body, arguments))

    now = [2.0]

    def poll(us):
        now[0] += us * PACE
        run_until(now[0])

    def mask_of(mask, at, count):
        places = lax.broadcasted_iota(jnp.int32, (SEG, 1), 0)
        across = lax.broadcasted_iota(jnp.int32, (1, count), 1)
        if at == 1:
            places = (places + half * c) % SEG
            across = across + half * c
        key_row, valid = row_ids(info_s, at, places.astype(F32))
        query_row, _ = row_ids(info_s, at, across.astype(F32))
        allowed = jnp.where(valid, key_row, -1.0) == query_row
        mask[...] = jnp.where(allowed, 0.0, NEG)
        keep[at * SEG : at * SEG + count] = jnp.where(valid[:count], 1.0, 0.0)

    def project(other, first, count):
        if not other and first == 0:
            loaded("qkv")
            info_s[...] = info[...]
            mask_of(mask_a, 0, SEG)
        if not other and first == SEG:
            info_copy.wait_recv()
            info_s[...] = jnp.where(same, info[...], info_r[...])
            mask_of(mask_m, 1, half)

            @pl.when(jnp.logical_not(same))
            def _():
                x_c1.wait_recv()
                x_c2.wait_recv()

            store(x_s, x_o)
        if other:
            bias_copy.wait_recv()
            need("qkv")
            for n, w in enumerate((wq_o, wk_o, wv_o)):
                store(w3.at[1, :, pl.ds(n * width, width)], w)
        vector = bias_r if other else bias
        cols = slice(width, 2 * width) if other else slice(0, width)
        for r in range(first, first + count, TILE):
            at = slice(r, r + TILE)
            qkv = mm(x_s[at], w3[1 if other else 0])
            if r < rows:
                q_s[at, cols] = ((qkv[:, :width] + vector[0:1]) * HEAD_DIM**-0.5).astype(BF16)
            k_s[at, cols] = qkv[:, width : 2 * width].astype(BF16)
            v_s[at, cols] = (qkv[:, 2 * width :] + vector[1:2]).astype(BF16)
            poll(0.6)

    used = {}

    def attend(pair, middle):
        first, count, mask, probs, out = (SEG, half, mask_m, p_m, pm_o) if middle else (0, SEG, mask_a, p_a, pa_o)
        at = slice(first, first + count)
        ks = slice(first, first + SEG)
        cols = slice(pair * PAIR, (pair + 1) * PAIR)
        s = pair % 3
        if (middle, s) in used:
            used[middle, s].wait()
        lane = lax.broadcasted_iota(jnp.int32, (1, PAIR), 1) // HEAD_DIM
        query, keys = q_s[at, cols], k_s[ks, cols]
        values_t = v_s[ks, cols].astype(F32).T.astype(BF16)
        parts = []
        for h in range(2):
            query_h = jnp.where(lane == h, query, jnp.zeros((), BF16))
            scores = mm_nt(keys, query_h) + mask[...]
            top = jnp.max(scores, axis=0, keepdims=True)
            grown = jnp.exp(scores - top)
            prob = (grown * (1.0 / jnp.sum(grown, axis=0, keepdims=True))).astype(BF16)
            probs[s, h] = prob
            parts.append(mm(values_t[h * HEAD_DIM : (h + 1) * HEAD_DIM], prob))
            if h == 0:
                poll(0.4 if middle else 0.75)
        ctx[at, cols] = jnp.concatenate(parts, axis=0).T.astype(BF16)
        used[middle, s] = copies.here(probs.at[s], out.at[pl.ds(2 * pair, 2)])
        used[middle, s].start()

    def stored_qkv():
        for src, dst in ((q_s, q_o), (k_s, k_o), (v_s, v_o), (ctx, ctx_o)):
            store(src, dst)

    def normalize(value):
        centre = value - jnp.mean(value, axis=-1, keepdims=True)
        inverse = lax.rsqrt(jnp.mean(centre * centre, axis=-1, keepdims=True) + EPS)
        return centre * inverse, inverse

    def first_norm():
        loaded("wo")
        need("wo")
        store(wo_s.at[pl.ds(width, width)], wo_o)
        for r in range(0, rows, TILE):
            at = slice(r, r + TILE)
            poll(0.8)
            normal, inverse = normalize(x_s[at].astype(F32) + mm(ctx[at], wo_s[...]) + const(0))
            normed[at] = normal.astype(BF16)
            inv[at] = inverse
            hidden[at] = (normal * const(1) + const(2)).astype(BF16)
        store(normed, normed_o)
        store(inv, inv_o)
        store(hidden, hidden_o)

    def up(other, h):
        if h == 0:
            if other:
                need("wu")
                store(wu_s.at[1], wu_o)
            else:
                loaded("wu")
        s = 1 if other else 0
        vector = bias_r if other else bias
        cols = slice(h * dim, (h + 1) * dim)
        shift = wide_row(vector, 2 + 2 * h)
        for r in range(0, rows, TILE):
            at = slice(r, r + TILE)
            active, steep = gelu_parts(mm(hidden[at], wu_s[s, :, cols]) + shift)
            act[s, at, cols] = active.astype(BF16)
            slope[s, at, cols] = steep.astype(BF16)
            poll(0.75)
        if h == 1:
            store(act.at[s], act_oo if other else act_io)
            store(slope.at[s], slope_oo if other else slope_io)

    def down(other):
        if other:
            need("wd")
            store(wd_s.at[1], wd_o)
        else:
            loaded("wd")
        for r in range(0, rows, TILE):
            at = slice(r, r + TILE)
            if other:
                acc[at] += mm(act[1, at], wd_s[1])
            else:
                acc[at] = mm(act[0, at], wd_s[0])
            poll(0.75)

    def second_norm():
        loaded("cot")

        @pl.when(same)
        def _():
            cot_own.wait()

        @pl.when(jnp.logical_not(same))
        def _():
            cot_d.wait_recv()

        sums = [0.0, 0.0, 0.0]
        for r in range(0, rows, TILE):
            at = slice(r, r + TILE)
            normal, inverse = normalize(hidden[at].astype(F32) + acc[at] + const(3))
            g = const(4)
            out_s[at] = ((normal * g + const(5)) * keep[at]).astype(BF16)
            upstream = cot[at].astype(F32) * keep[at]
            scaled = upstream * g
            grad = inverse * (
                scaled
                - jnp.mean(scaled, axis=-1, keepdims=True)
                - normal * jnp.mean(scaled * normal, axis=-1, keepdims=True)
            )
            acc[at] = grad
            low[at] = grad.astype(BF16)
            sums[0] += jnp.sum(upstream * normal, axis=0, keepdims=True)
            sums[1] += jnp.sum(upstream, axis=0, keepdims=True)
            sums[2] += jnp.sum(grad, axis=0, keepdims=True)
            for src, dst in ((acc, second_o), (low, low_o), (out_s, out_o)):
                store(src.at[pl.ds(r, TILE)], dst.at[pl.ds(r, TILE)])
        for i, value in enumerate(sums):
            vec_o[i : i + 1] = value

    step(1.5, project, False, 0, SEG)
    for pair in range(pairs):
        step(1.4, attend, pair, False)
    step(1.8, project, False, SEG, SEG)
    for pair in range(pairs):
        step(0.7, attend, pair, True)
    step(2.4, project, True, 0, rows + half)
    for pair in range(pairs, 2 * pairs):
        step(1.4, attend, pair, False)
        step(0.7, attend, pair, True)
    step(0.2, stored_qkv)
    step(2.5, first_norm)
    step(2.2, up, False, 0)
    step(2.2, up, False, 1)
    step(2.2, down, False)
    step(2.2, up, True, 0)
    step(2.2, up, True, 1)
    step(2.2, down, True)
    step(2.0, second_norm)
    starts = {(project, False, SEG, SEG): 16.0, (project, True, 0, rows + half): 20.0, (up, True, 0): 37.0, (down, True): 47.0}
    clock = 2.0
    for us, body, arguments in work:
        clock = max(clock, starts.get((body, *arguments), 0.0))
        run_until(clock)
        now[0] = clock
        body(*arguments)
        clock += us
    run_until(1e9)

    @pl.when(same)
    def _():
        x_c1.wait_send()
        x_c2.wait_send()

    @pl.when(jnp.logical_not(same))
    def _():
        x_y.wait_send()
        cot_d.wait_send()

    info_copy.wait_send()
    bias_copy.wait_send()
    for copy in over.values():
        copy.wait_send()
    for copy in stores + list(used.values()):
        copy.wait()


LINK_US = 6.2 / 384


def plan(parts, x_first, direct, levels, split, ready_e, ready_i):
    free = {"y": 0.0, "x": 0.0, "z": 0.0, "far": 0.0}
    back = [("fz", n) for n in range(split - 1, -1, -1)] + ["fx"]
    route = {
        "y": ["y", "x"] + [("z", n) for n in range(levels)] + back,
        "q": ["y", "x", "zq"] + [("z", n) for n in range(split, levels)] + ["fq", "fx"],
        "e": ["ex"] + [("ez", n) for n in range(split)] + ["ey"],
        "i": ["x"] + [("z", n) for n in range(levels)] + back,
    }
    link_of = {"y": "y", "ey": "y", "x": "x", "ex": "x", "fx": "x", "zq": "far", "fq": "far"}
    for n in range(levels):
        for name in ("z", "ez", "fz"):
            link_of[name, n] = "z" if n == 0 else "far"
    share = {"zq": 1.0, "fq": 1.0, "y": 2.0, "ey": 0.25, "x": 1.0, "ex": 1.0, "fx": 1.0}
    order, ready, joined, held = [], [], {}, {}
    for n, k in enumerate(parts):
        if k in x_first:
            ready.append((ready_e[k], "e", 0, n, k))
            ready.append((ready_i[k], "i", 0, n, k))
        else:
            ready.append((ready_e[k], "q" if k in direct else "y", 0, n, k))
    while ready:

        def key(item):
            stage = route[item[1]][item[2]]
            return max(item[0], free[link_of[stage]]), stage in back or stage == "fq", item[3]

        item = min(ready, key=key)
        ready.remove(item)
        time, name, at, n, k = item
        stage = route[name][at]
        start = key(item)[0]
        us = parts[k] * LINK_US * share.get(stage, 0.5)
        free[link_of[stage]] = start + us
        order.append((start, stage, k))
        come = start + us + BACK_HOP_US
        if stage == "fx":
            order.append((come, "end", k))
        elif stage == "ey":
            joined[k] = come
            if k in held:
                ready.append((max(come, held[k]), "i", 1 + split, n, k))
        elif name == "i" and at == split:
            held[k] = come
            if k in joined:
                ready.append((max(come, joined[k]), "i", 1 + split, n, k))
        else:
            if stage == "y":
                come = max(come, ready_i[k])
            ready.append((come, name, at + 1, n, k))
    return sorted(order, key=lambda v: v[0])


def backward_body(
    depth,
    low_h, hidden_h, act_i, act_o, slope_i, slope_o, wu_i, wu_o, wd_i, wd_o, second_h, normed_h, inv_h,
    wo_i, wo_o, ctx_h, x_h, q_h, k_h, v_h, pa_h, pm_h, wq_i, wk_i, wv_i, wq_o, wk_o, wv_o, output_h, gain, vec2,
    sums_o, top_o, vec_o, in_o, out_o,
    low, hidden, slots, total, b_e, b_i, c_e, c_i, y_r, x_r, z_a, z_b, zx_r, normed, inv, wo, ctx, dctx, x_s,
    p_a, p_m, d3, vecs, vec_r, mid_r, send, recv, local, crossed,
):
    z, x, c, y = coords()
    copies = Copies(send, recv, local)
    steps = []
    while 2 ** len(steps) < depth:
        steps.append(2 ** len(steps))
    levels = len(steps)
    split = min(2, levels)
    bits = [(z // s) % 2 for s in steps]
    z_partner = [z + s - 2 * s * b for s, b in zip(steps, bits)]
    near = [{"c": 1 - c}, {"y": 1 - y}, {"x": 1 - x}] + [{"z": p} for p in z_partner]
    quad = []
    if split == 2:
        for flips in ((1, 0), (0, 1), (1, 1)):
            theirs = [b + f - 2 * f * b for b, f in zip(bits, flips)]
            quad.append((z + theirs[0] - bits[0] + 2 * (theirs[1] - bits[1]), theirs))
    same = c == y
    rows, dim = low.shape
    half = rows - SEG
    width = b_e.shape[2]
    quarter = dim // 4
    ffn_rows = 2 * dim
    first_row, parts = {}, {}
    ffn_chunks = ffn_rows // CHUNK
    for n in range(ffn_chunks):
        first_row[n], parts[n] = n * CHUNK, CHUNK
    qkv_chunks, out_chunks = [], []
    row = ffn_rows
    while row < ffn_rows + 4 * quarter:
        end = ffn_rows + (3 if row < ffn_rows + 3 * quarter else 4) * quarter
        n = len(parts)
        first_row[n], parts[n] = row, min(128, end - row)
        (qkv_chunks if row < ffn_rows + 3 * quarter else out_chunks).append(n)
        row += parts[n]
    every, waited, x_first, direct = [], set(), set(), set()

    def at(k):
        return pl.ds(first_row[k], parts[k])

    def go(copy):
        copy.start()
        every.append(copy)
        return copy

    def arrived(copy):
        copy.wait_recv()
        waited.add(id(copy))

    loads = {}

    def load(name, *pairs):
        loads[name] = [copies.here(src, dst) for src, dst in pairs]
        for copy in loads[name]:
            copy.start()

    def loaded(name):
        for copy in loads.pop(name, ()):
            copy.wait()

    chunks = [(False, 1 - c), (False, c), (True, 1 - c), (True, c)]

    def load_ffn(n, kind):
        own, h = chunks[n]
        cut = pl.ds(pl.multiple_of(h * dim, 128), dim)
        refs = {"wu": (wu_i, wu_o), "wd": (wd_i, wd_o), "act": (act_i, act_o), "slope": (slope_i, slope_o)}
        ref = refs[kind][0 if own else 1]
        slot_at = 2 * ("wu", "wd", "act", "slope").index(kind) + n % 2
        load((kind, n), (ref.at[cut] if kind == "wd" else ref.at[:, cut], slots.at[slot_at]))

    load("low", (low_h, low))
    load_ffn(0, "act")
    load_ffn(1, "act")
    load_ffn(0, "wd")
    load_ffn(0, "slope")
    load("hidden", (hidden_h, hidden))
    load_ffn(1, "wd")
    load_ffn(1, "slope")
    load("second", (second_h, total.at[pl.ds(0, rows)]))
    load_ffn(0, "wu")
    load_ffn(1, "wu")
    greet(near + [{"z": p} for p, _ in quad[2:]] + [{"c": 1 - c, "y": 1 - y}])

    out_d = pltpu.make_async_remote_copy(
        src_ref=output_h.at[pl.ds(SEG, half)], dst_ref=out_o, send_sem=crossed.at[0], recv_sem=crossed.at[1],
        device_id={"c": 1 - c, "y": 1 - y}, device_id_type=MESH_IDS,
    )
    mid_b = [slots.at[0, pl.ds(n * half, half)] for n in range(2)]
    in_d = pltpu.make_async_remote_copy(
        src_ref=mid_b[1], dst_ref=in_o, send_sem=crossed.at[2], recv_sem=crossed.at[3],
        device_id={"c": 1 - c, "y": 1 - y}, device_id_type=MESH_IDS,
    )

    load("mid", (wo_i, wo.at[pl.ds(0, width)]), (wo_o, wo.at[pl.ds(width, width)]), (ctx_h, ctx), (normed_h, normed), (inv_h, inv), (x_h, x_s))

    def add(n, out, *ins):
        tile = next(t for t in (48, 32, 16) if n % t == 0)

        def step(i, _):
            rows_at = pl.ds(pl.multiple_of(i * tile, 16), tile)
            value = ins[0][rows_at].astype(F32)
            for other in ins[1:]:
                value = value + other[rows_at].astype(F32)
            out[rows_at] = value.astype(out.dtype)
            return 0

        lax.fori_loop(0, n // tile, step, 0)

    def add2(n, out, *ins):
        for part in range(2):
            add(n, out.at[part], *[v.at[part] for v in ins])

    got_e, got_i, got_y, got_x, got_z, back_z, put, got_bx = {}, {}, {}, {}, {}, {}, {}, {}

    def cores(own, k):
        buf, there, got = (b_i, c_i, got_i) if own else (b_e, c_e, got_e)
        got[k] = go(copies.to(buf.at[pl.ds(2, 2), at(k)], there.at[:, at(k)], c=1 - c))

    def to_y(k):
        arrived(got_e[k])
        mine = b_e.at[pl.ds(0, 2), at(k)]
        add2(parts[k], mine, mine, c_e.at[:, at(k)])
        got_y[k] = go(copies.to(mine, y_r.at[:, at(k)], y=1 - y))

    def to_x(k):
        arrived(got_i[k])
        mine = b_i.at[pl.ds(0, 2), at(k)]
        if k in x_first:
            add2(parts[k], mine, mine, c_i.at[:, at(k)])
        else:
            arrived(got_y[k])
            add2(parts[k], mine, mine, c_i.at[:, at(k)], y_r.at[:, at(k)])
        got_x[k] = go(copies.to(b_i.at[1, at(k)], x_r.at[at(k)], x=1 - x))

    def base(k, level):
        row, size = first_row[k], parts[k]
        for n in range(min(level, split)):
            size //= 2
            row = row + bits[n] * size
        return row, size

    def slot(k, level):
        cut = 2 ** (level + 1)
        return (z_a, z_b)[level].at[pl.ds(first_row[k] // cut, parts[k] // cut)]

    def extra(k, n):
        return zx_r.at[n, pl.ds(first_row[k] // 4, parts[k] // 4)]

    got_q, back_q = {}, {}

    def quad_slot(k, n):
        size = parts[k] // 4
        if n < 2:
            return z_a.at[pl.ds(first_row[k] // 2 + n * size, size)]
        return z_b.at[pl.ds(first_row[k] // 4, size)]

    def to_quad(k):
        arrived(got_x[k])
        mine = b_i.at[0, at(k)]
        add(parts[k], mine, mine, x_r.at[at(k)])
        size = parts[k] // 4
        for n, (partner, theirs) in enumerate(quad):
            row = first_row[k] + theirs[0] * 2 * size + theirs[1] * size
            away = b_i.at[0, pl.ds(pl.multiple_of(row, 16), size)]
            got_q[k, n] = go(copies.to(away, quad_slot(k, n), z=partner))

    def from_quad(k):
        put[k].wait()
        for n in range(3):
            arrived(back_q[k, n])
        after_z(k)

    got_ex, got_ez = {}, {}

    def e_x(k):
        arrived(got_e[k])
        mine = b_e.at[pl.ds(0, 2), at(k)]
        add2(parts[k], mine, mine, c_e.at[:, at(k)])
        got_ex[k] = go(copies.to(b_e.at[1, at(k)], y_r.at[1, at(k)], x=1 - x))

    def e_z(k, level):
        row, size = base(k, level)
        region = lambda first, n: pl.ds(pl.multiple_of(first, 16), n)
        mine = b_e.at[0, region(row, size)]
        if level == 0:
            arrived(got_ex[k])
            add(size, mine, mine, y_r.at[1, at(k)])
        else:
            arrived(got_ez[k, level - 1])
            before = base(k, level - 1)[0]
            add(size, mine, mine, y_r.at[0, region(before + (1 - bits[level - 1]) * size, size)])
        if level < split:
            size //= 2
            away = b_e.at[0, region(row + (1 - bits[level]) * size, size)]
            place = y_r.at[0, region(row + bits[level] * size, size)]
            got_ez[k, level] = go(copies.to(away, place, z=z_partner[level]))
        else:
            got_y[k] = go(copies.to(mine, y_r.at[0, region(row, size)], y=1 - y))

    def to_z(k, level):
        row, size = base(k, level)
        mine = b_i.at[0, pl.ds(pl.multiple_of(row, 16), size)]
        if level == 0:
            arrived(got_x[k])
            add(size, mine, mine, x_r.at[at(k)])
        elif level == split and k in direct:
            for n in range(3):
                arrived(got_q[k, n])
            add(size, mine, mine, *[quad_slot(k, n) for n in range(3)])
        else:
            if level > split:
                got_z[k, level - 1].wait()
            else:
                arrived(got_z[k, level - 1])
            came = [slot(k, level - 1) if level <= split else extra(k, level - 1 - split)]
            if k in x_first and level == split:
                arrived(got_y[k])
                came.append(y_r.at[0, pl.ds(pl.multiple_of(row, 16), size)])
            add(size, mine, mine, *came)
        if level < split:
            size //= 2
            out = b_i.at[0, pl.ds(pl.multiple_of(row + (1 - bits[level]) * size, 16), size)]
            got_z[k, level] = go(copies.to(out, slot(k, level), z=z_partner[level]))
        elif level < levels:
            got_z[k, level] = copies.to(mine, extra(k, level - split), z=z_partner[level])
            got_z[k, level].start()
        else:
            place = sums_o.at[0, pl.ds(pl.multiple_of(row, 16), size)]
            put[k] = copies.here(mine, place)
            put[k].start()
            if k in direct:
                for n, (partner, _) in enumerate(quad):
                    back_q[k, n] = go(copies.to(mine, place, z=partner))
            elif split:
                back_z[k, split - 1] = go(copies.to(mine, place, z=z_partner[split - 1]))

    def from_z(k, level):
        if level == max(split, 1) - 1:
            put[k].wait()
        if split:
            arrived(back_z[k, level])
        if level > 0:
            row, size = base(k, level)
            place = sums_o.at[0, pl.ds(pl.multiple_of(row, 16), size)]
            back_z[k, level - 1] = go(copies.to(place, place, z=z_partner[level - 1]))
        else:
            after_z(k)

    def after_z(k):
        mine = sums_o.at[0, at(k)]
        got_bx[k] = go(copies.to(mine, sums_o.at[1, at(k)], x=1 - x))
        go(copies.to(mine, sums_o.at[2, at(k)], c=1 - c))

    def from_x(k):
        arrived(got_bx[k])
        go(copies.to(sums_o.at[1, at(k)], sums_o.at[3, at(k)], c=1 - c))

    vec_copies = {}

    def vec_start(n):
        source = vecs if n == 0 else vec_r.at[2 * n - 1]
        vec_copies[n] = go(copies.to(source, vec_r.at[2 * n], **near[n]))

    def vec_next(n):
        arrived(vec_copies[n])
        value = (vecs if n == 0 else vec_r.at[2 * n - 1])[...] + vec_r[2 * n]
        if n == len(near) - 1:
            vec_o[...] = value
        else:
            vec_r[2 * n + 1] = value
            vec_start(n + 1)

    work = []

    def step(us, body, *arguments):
        work.append((us * BACK_PACE, body, arguments))

    now = [3.0]

    def run_until(time):
        while tasks and tasks[0][0] <= time:
            _, task, its = tasks.pop(0)
            task(*its)

    def poll(us):
        now[0] += us * BACK_PACE
        run_until(now[0])

    def put_columns(buf, row, left, right, keep):
        for r in range(0, dim, TILE):
            grads = mm_tn(left[:, r : r + TILE], right[...]).astype(BF16)
            for part in range(2):
                rel = (0 if keep else 2) + (part + x) % 2
                buf[rel, row + r : row + r + TILE] = grads[:, part * width : (part + 1) * width]
            poll(0.45)

    def put_rows(buf, group, p, grads):
        rel = 2 * ((p // 2 + c) % 2) + (p % 2 + x) % 2
        buf[rel, ffn_rows + group * quarter : ffn_rows + (group + 1) * quarter] = grads

    inner_at = (d3.at[pl.ds(0, rows), pl.ds(0, dim)], dctx)

    def inner_grad(n):
        own, h = chunks[n]
        loaded(("wd", n))
        loaded(("slope", n))
        s = n % 2
        bias = 0.0
        for r in range(0, rows, TILE):
            at = slice(r, r + TILE)
            grad = (mm_nt(low[at], slots[2 + s]) * slots[6 + s, at].astype(F32)).astype(BF16)
            inner_at[s][at] = grad
            bias += jnp.sum(grad.astype(F32), axis=0, keepdims=True)
            poll(0.5)
        for part in range(2):
            row = 4 * (y if own else 1 - y) + 2 * h + part
            vecs[pl.ds(row, 1)] = bias[:, part * width : (part + 1) * width]
        if n < 2:
            load_ffn(n + 2, "wd")
            load_ffn(n + 2, "slope")

    def hidden_grad(n):
        loaded("second")
        loaded(("wu", n))
        for r in range(0, rows, TILE):
            at = slice(r, r + TILE)
            total[at] += mm_nt(inner_at[n % 2][at], slots[n % 2])
            poll(0.45)
        if n < 2:
            load_ffn(n + 2, "wu")
        if n == 3:
            load_attention()

    def up_grad(n):
        own = chunks[n][0]
        loaded("hidden")
        put_columns(b_i if own else b_e, 0, hidden, inner_at[n % 2], n % 2 == 1)
        if n % 2 == 0:
            for k in range(ffn_chunks // 2):
                cores(own, k)

    def down_grad(n):
        own = chunks[n][0]
        loaded("low")
        loaded(("act", n))
        put_columns(b_i if own else b_e, dim, low, slots.at[4 + n % 2], n % 2 == 1)
        if n % 2 == 0:
            for k in range(ffn_chunks // 2, ffn_chunks):
                cores(own, k)
        if n < 2:
            load_ffn(n + 2, "act")

    def load_attention():
        left, right = pl.ds(0, width), pl.ds(width, width)
        load(
            "att",
            (q_h, slots.at[0]),
            (k_h.at[pl.ds(0, SEG)], slots.at[2, pl.ds(0, SEG)]),
            (k_h.at[pl.ds(SEG, SEG)], slots.at[4, pl.ds(0, SEG)]),
            (v_h.at[pl.ds(0, SEG)], slots.at[6, pl.ds(0, SEG)]),
            (v_h.at[pl.ds(SEG, SEG)], slots.at[1, pl.ds(0, SEG)]),
        )
        load(
            "att_w",
            (wq_i, slots.at[3, :, left]),
            (wk_i, slots.at[3, :, right]),
            (wv_i, slots.at[5, :, left]),
            (wv_o, slots.at[5, :, right]),
            (wq_o, slots.at[7, :, left]),
            (wk_o, slots.at[7, :, right]),
        )
        load_probs(0)
        load_probs(1)

    pairs = width // PAIR
    pair_order = [pairs + n for n in range(pairs)] + list(range(pairs))

    def load_probs(n):
        pair = pair_order[n]
        load(
            ("p", n),
            (pa_h.at[pl.ds(2 * pair, 2)], p_a.at[n % 2]),
            (pm_h.at[pl.ds(2 * pair, 2)], p_m.at[n % 2]),
        )

    def out_back():
        loaded("mid")
        sums = [0.0, 0.0, 0.0]
        gain_row = gain[...].astype(F32).reshape(1, dim)
        for r in range(0, rows, TILE):
            tile = slice(r, r + TILE)
            grad_in = total[tile]
            n = normed[tile].astype(F32)
            scaled = grad_in * gain_row
            grad = inv[tile] * (
                scaled
                - jnp.mean(scaled, axis=-1, keepdims=True)
                - n * jnp.mean(scaled * n, axis=-1, keepdims=True)
            )
            sums[0] += jnp.sum(grad_in * n, axis=0, keepdims=True)
            sums[1] += jnp.sum(grad_in, axis=0, keepdims=True)
            sums[2] += jnp.sum(grad, axis=0, keepdims=True)
            total[tile] = grad
            low[tile] = grad.astype(BF16)
        for i, value in enumerate(sums):
            for part in range(2):
                cut = slice(part * width, (part + 1) * width)
                vecs[12 + 2 * i + part : 13 + 2 * i + part] = value[:, cut]
                vecs[18 + 2 * i + part : 19 + 2 * i + part] = vec2[i : i + 1, cut]
        total[rows:] = jnp.zeros((half, dim), F32)
        d3[rows:, :width] = jnp.zeros((half, width), BF16)

    def out_grads():
        for pair in range(2):
            grads = mm_tn(low[:, 2 * pair * quarter : 2 * (pair + 1) * quarter], ctx[...]).astype(BF16)
            for n in range(2):
                at = slice(n * quarter, (n + 1) * quarter)
                put_rows(b_i, 3, 2 * pair + n, grads[at, :width])
                put_rows(b_e, 3, 2 * pair + n, grads[at, width:])
            poll(0.7)
        for k in out_chunks:
            cores(False, k)
            cores(True, k)

    def context_grad():
        for r in range(0, rows, TILE):
            at = slice(r, r + TILE)
            dctx[at] = mm_nt(low[at], wo[...]).astype(BF16)
            poll(0.4)

    def attend(n):
        pair = pair_order[n]
        cols = slice(pair * PAIR, (pair + 1) * PAIR)
        local_at = (pair % pairs) * PAIR
        if n == 0:
            loaded("att")
        loaded(("p", n))
        lane = lax.broadcasted_iota(jnp.int32, (1, PAIR), 1) // HEAD_DIM
        zero = jnp.zeros((), BF16)
        for first, count, key_first, k_slot, v_slot, probs_ref in (
            (0, SEG, 0, 2, 6, p_a),
            (SEG, half, SEG, 4, 1, p_m),
        ):
            q_at = slice(first, first + count)
            ks = slice(key_first, key_first + SEG)
            grad2, query2 = dctx[q_at, cols], slots[0, q_at, cols]
            keys, values = slots[k_slot, :SEG, cols], slots[v_slot, :SEG, cols]
            delta_t = (grad2.astype(F32) * ctx[q_at, cols].astype(F32)).T
            values_grad = keys_grad = query_grad = 0.0
            for h in range(2):
                grad_h = jnp.where(lane == h, grad2, zero)
                query_h = jnp.where(lane == h, query2, zero)
                keys_h = jnp.where(lane == h, keys, zero)
                probs = probs_ref[n % 2, h]
                delta = jnp.sum(delta_t[h * HEAD_DIM : (h + 1) * HEAD_DIM], axis=0, keepdims=True)
                prob_grad = mm_nt(values, grad_h)
                score_grad = (probs.astype(F32) * (prob_grad - delta)).astype(BF16)
                values_grad += mm(probs, grad_h)
                keys_grad += mm(score_grad, query_h)
                query_grad += mm_tn(score_grad, keys_h)
                poll(0.7 if first == 0 else 0.35)
            for part, value, out_at in (
                (0, query_grad * HEAD_DIM**-0.5, q_at),
                (1, keys_grad, ks),
                (2, values_grad, ks),
            ):
                d3[out_at, part * width + local_at : part * width + local_at + PAIR] = value.astype(BF16)
        if n + 2 < 2 * pairs:
            load_probs(n + 2)

    def input_part(own):
        loaded("att_w")
        main = 3 if own else 7
        last = slice(0, width) if own else slice(width, 2 * width)
        for r in range(0, rows + half, TILE):
            at = slice(r, r + TILE)
            total[at] += mm_nt(d3[at, : 2 * width], slots[main]) + mm_nt(
                d3[at, 2 * width :], slots[5, :, last]
            )
            poll(0.7)

    def weight_part(own):
        buf = b_i if own else b_e
        for pair in range(2):
            grads = mm_tn(x_s[:, 2 * pair * quarter : 2 * (pair + 1) * quarter], d3[...]).astype(BF16)
            for n in range(2):
                at = slice(n * quarter, (n + 1) * quarter)
                for group in range(3):
                    put_rows(buf, group, 2 * pair + n, grads[at, group * width : (group + 1) * width])
            poll(1.4)
        for k in qkv_chunks:
            cores(own, k)
        row = y if own else 1 - y
        vecs[pl.ds(8 + row, 1)] = jnp.sum(d3[:rows, :width].astype(F32), axis=0, keepdims=True)
        vecs[pl.ds(10 + row, 1)] = jnp.sum(d3[:, 2 * width :].astype(F32), axis=0, keepdims=True)
        if own:
            vec_start(0)

    done = []

    def leave(first, count):
        copy = copies.here(total.at[pl.ds(first, count)], top_o.at[pl.ds(first, count)])
        copy.start()
        done.append(copy)

    def finish():
        mid_b[0][...] = total[rows:].astype(BF16)
        done.append(go(copies.to(mid_b[0], mid_r, c=1 - c)))
        leave(0, SEG)

    def middle():
        arrived(done[0])
        value = total[SEG:rows] + mid_r[...].astype(F32)
        total[SEG:rows] = value
        mid_b[1][...] = value.astype(BF16)
        leave(SEG, half)

        @pl.when(jnp.logical_not(same))
        def _():
            in_d.start()
            out_d.start()

    ready_e, ready_i = {}, {}
    clock = 3.0
    for n in (0, 2):
        step(1.4, down_grad, n)
        step(1.4, down_grad, n + 1)
        step(1.5, inner_grad, n)
        step(1.4, up_grad, n)
        step(1.5, inner_grad, n + 1)
        step(1.4, up_grad, n + 1)
        step(1.3, hidden_grad, n)
        step(1.3, hidden_grad, n + 1)
    step(1.6, out_back)
    step(1.4, out_grads)
    step(1.2, context_grad)
    for n in range(2 * pairs):
        step(2.1, attend, n)
        if n % pairs == pairs - 1:
            step(3.0, weight_part, n > pairs)
            step(2.8, input_part, n > pairs)
    step(0.7, finish)
    when = {}
    for us, body, arguments in work:
        clock += us
        when[(body, *arguments)] = clock
    for k in parts:
        if k < ffn_chunks:
            ready = (up_grad, down_grad)[2 * k // ffn_chunks]
            ready_e[k], ready_i[k] = when[ready, 1], when[ready, 3]
        elif k in out_chunks:
            ready_e[k] = ready_i[k] = when[(out_grads,)] + 1.5
        else:
            ready_e[k], ready_i[k] = when[weight_part, False] + 1.5, when[weight_part, True] + 1.5
    chunk_order = {
        k: parts[k] for k in [*range(ffn_chunks // 2, ffn_chunks), *range(ffn_chunks // 2), *out_chunks, *qkv_chunks]
    }
    if split == 2:
        listed = list(chunk_order)
        x_first.update(listed[n] for n in X_FIRST)
        direct.update(listed[n] for n in DIRECT)
    tasks = []
    for time, stage, k in plan(chunk_order, x_first, direct, levels, split, ready_e, ready_i):
        if stage == "y":
            tasks.append((time, to_y, (k,)))
        elif stage == "ex":
            tasks.append((time, e_x, (k,)))
        elif stage == "ey":
            tasks.append((time, e_z, (k, split)))
        elif stage[0] == "ez":
            tasks.append((time, e_z, (k, stage[1])))
        elif stage == "x":
            tasks.append((time, to_x, (k,)))
        elif stage == "end":
            tasks.append((time, from_x, (k,)))
        elif stage == "zq":
            tasks.append((time, to_quad, (k,)))
        elif stage == "fq":
            tasks.append((time, to_z, (k, levels)))
        elif stage == "fx" and k in direct:
            tasks.append((time, from_quad, (k,)))
        elif stage == "fx":
            if not split:
                tasks.append((time, to_z, (k, levels)))
            tasks.append((time, from_z, (k, 0)))
        elif stage[0] == "z":
            tasks.append((time, to_z, (k, stage[1])))
        elif stage[1] == split - 1:
            tasks.append((time, to_z, (k, levels)))
        else:
            tasks.append((time, from_z, (k, stage[1] + 1)))
    end = when[(finish,)]
    last_y = max(time for time, task, _ in tasks if task in (to_y, e_z))
    tasks.append((max(end + 4.0, last_y + 0.1), middle, ()))
    for n in range(len(near)):
        tasks.append((when[weight_part, True] + 4.0 * (n + 1), vec_next, (n,)))
    tasks.sort(key=lambda t: t[0])
    clock = 3.0
    for us, body, arguments in work:
        run_until(clock)
        now[0] = clock
        body(*arguments)
        clock += us
    run_until(1e9)

    @pl.when(jnp.logical_not(same))
    def _():
        out_d.wait()
        in_d.wait()

    for copy in done[1:]:
        copy.wait()
    for copy in every:
        copy.wait_send()
        if id(copy) not in waited:
            copy.wait_recv()


def final_body(
    pos_ref, sums, top, output, top_mid, output_mid, in_mid, out_mid, vec,
    out_o, in_o, q_o, k_o, v_o, wo_o, up_o, down_o, bq_o, bv_o, bu_o, n1g_o, n1b_o, bo_o, n2g_o, n2b_o, bd_o, tmp,
):
    j = pl.program_id(0)
    dim = up_o.shape[0]
    quarter, width = q_o.shape
    same = pos_ref[1] == pos_ref[2]
    is_mid = jnp.where(pos_ref[2] == 0, j >= 2, j == 0)

    @pl.when(is_mid & same)
    def _():
        out_o[...] = output_mid[...]
        in_o[...] = top_mid[...]

    @pl.when(is_mid & jnp.logical_not(same))
    def _():
        out_o[...] = out_mid[...]
        in_o[...] = in_mid[...].astype(F32)

    @pl.when(jnp.logical_not(is_mid))
    def _():
        out_o[...] = output[...]
        in_o[...] = top[...]

    @pl.when(j == 0)
    def _():
        bq_o[...] = vec[pl.ds(8 + pos_ref[2], 1)].reshape(width)
        bv_o[...] = vec[pl.ds(10 + pos_ref[2], 1)].reshape(width)
        parts = [vec[pl.ds(4 * pos_ref[2] + n, 1)] for n in range(4)]
        bu_o[...] = jnp.concatenate(parts, axis=1).reshape(4 * width)
        for n, ref in enumerate((n1g_o, n1b_o, bo_o, n2g_o, n2b_o, bd_o)):
            ref[...] = wide_row(vec, 12 + 2 * n).reshape(dim)

    up_o[...] = sums[0, :dim].astype(F32)
    down_o[...] = sums[0, dim : 2 * dim].astype(F32).T
    for part, ref in enumerate((q_o, k_o, v_o)):
        at = 2 * dim + part * quarter
        ref[...] = sums[0, at : at + quarter].astype(F32)
    row = pl.multiple_of((pos_ref[0] ^ j) * quarter, 16)
    at = 2 * dim + 3 * quarter
    tmp[pl.ds(row, quarter), :] = sums[0, at : at + quarter].astype(F32)

    @pl.when(j == pl.num_programs(0) - 1)
    def _():
        wo_o[...] = tmp[...].T


def shards(
    depth,
    tokens, lengths, buckets, w_query, b_query, w_key, w_value, b_value, w_out, b_out,
    norm1_gain, norm1_bias, w_up, b_up, w_down, b_down, norm2_gain, norm2_bias, cotangent,
):
    ix, ic, iy = (lax.axis_index(a) for a in ("x", "c", "y"))
    pos = jnp.stack([2 * ic + ix, ic, iy]).astype(jnp.int32)
    rows, dim = tokens.shape
    half = rows - SEG
    width = w_query.shape[1]
    units = w_up.shape[1]
    chunk = units // 4
    any_space = pl.BlockSpec(memory_space=pl.ANY)
    in_vmem = pl.BlockSpec(memory_space=pltpu.VMEM)

    weights = (w_query, w_key, w_value, w_out, w_up, w_down)
    total = rows + half
    square = (rows, dim)
    wide = (rows, units)
    pairs = width // PAIR
    made = [
        shape((total, dim), BF16),
        *[shape(w.shape, BF16) for w in weights],
        shape(square, BF16),
        shape((total, dim), BF16),
        shape((total, dim), BF16),
        shape((4 * pairs, SEG, SEG), BF16),
        shape((4 * pairs, SEG, half), BF16),
        shape(square, BF16),
        shape(square, BF16),
        shape((rows, 1), F32),
        shape(square, BF16),
        *[shape(wide, BF16)] * 4,
        shape(square, F32),
        shape(square, BF16),
        shape(square, BF16),
        shape((3, dim), F32),
    ]
    (
        x, wq_o, wk_o, wv_o, wo_o, wu_o, wd_o, query, keys, values, probs_a, probs_m, ctx, normed1, inverse1, hidden,
        act_i, act_o, slope_i, slope_o, second, low, output, vec2,
    ) = pl.pallas_call(
        forward_body,
        out_shape=made,
        in_specs=[any_space] * 8 + [in_vmem] * 9 + [pl.BlockSpec(memory_space=pltpu.SMEM)] * 2,
        out_specs=[any_space] * (len(made) - 1) + [in_vmem],
        scratch_shapes=[
            pltpu.VMEM((total, dim), BF16),
            pltpu.VMEM(square, BF16),
            pltpu.VMEM((2, dim, 3 * width), BF16),
            pltpu.VMEM((2 * width, dim), BF16),
            pltpu.VMEM((2, dim, units), BF16),
            pltpu.VMEM((2, units, dim), BF16),
            pltpu.VMEM(square, BF16),
            *[pltpu.VMEM((total, dim), BF16)] * 2,
            pltpu.VMEM((3, 2, SEG, SEG), BF16),
            pltpu.VMEM((3, 2, SEG, half), BF16),
            *[pltpu.VMEM(square, BF16)] * 2,
            pltpu.VMEM((rows, 1), F32),
            pltpu.VMEM(square, BF16),
            pltpu.VMEM(square, F32),
            *[pltpu.VMEM((2, *wide), BF16)] * 2,
            *[pltpu.VMEM(square, BF16)] * 2,
            pltpu.VMEM((rows, 1), F32),
            pltpu.VMEM((SEG, SEG), F32),
            pltpu.VMEM((SEG, half), F32),
            pltpu.VMEM((24, width), F32),
            pltpu.VMEM((8, 128), F32),
            pltpu.VMEM((24, width), F32),
            *[pltpu.VMEM((8, 128), F32)] * 2,
            pltpu.SemaphoreType.DMA((96,)),
            pltpu.SemaphoreType.DMA((96,)),
            pltpu.SemaphoreType.DMA((64,)),
            pltpu.SemaphoreType.DMA((2,)),
        ],
        compiler_params=pltpu.CompilerParams(
            collective_id=1, has_side_effects=True, vmem_limit_bytes=VMEM_LIMIT
        ),
        name="forward",
    )(
        tokens, cotangent, *weights, b_query, b_value, b_up, b_out, norm1_gain, norm1_bias, b_down, norm2_gain, norm2_bias,
        buckets, lengths,
    )

    levels = depth.bit_length() - 1
    more = max(levels - 2, 0)
    size = 3 * dim
    links = levels + 3
    remote = 16 * (levels + 12) + links + 12
    sums, top, vec, in_mid, out_mid = pl.pallas_call(
        functools.partial(backward_body, depth),
        out_shape=[
            shape((4, size, width), BF16),
            shape((rows, dim), F32),
            shape((24, width), F32),
            shape((half, dim), BF16),
            shape((half, dim), BF16),
        ],
        in_specs=[any_space] * 29 + [in_vmem] * 2,
        out_specs=[any_space] * 2 + [in_vmem] + [any_space] * 2,
        scratch_shapes=[
            *[pltpu.VMEM((rows, dim), BF16)] * 2,
            pltpu.VMEM((8, rows, dim), BF16),
            pltpu.VMEM((rows + half, dim), F32),
            *[pltpu.VMEM((4, size, width), BF16)] * 2,
            *[pltpu.VMEM((2, size, width), BF16)] * 3,
            pltpu.VMEM((size, width), BF16),
            pltpu.VMEM((size // 2, width), BF16),
            pltpu.VMEM((size // 4, width), BF16),
            pltpu.VMEM((max(more, 1), size // 4 if more else 16, width), BF16),
            pltpu.VMEM((rows, dim), BF16),
            pltpu.VMEM((rows, 1), F32),
            *[pltpu.VMEM((rows, dim), BF16)] * 3,
            pltpu.VMEM((rows + half, dim), BF16),
            pltpu.VMEM((2, 2, SEG, SEG), BF16),
            pltpu.VMEM((2, 2, SEG, half), BF16),
            pltpu.VMEM((rows + half, 3 * width), BF16),
            pltpu.VMEM((24, width), F32),
            pltpu.VMEM((2 * links, 24, width), F32),
            pltpu.VMEM((half, dim), BF16),
            pltpu.SemaphoreType.DMA((remote,)),
            pltpu.SemaphoreType.DMA((remote,)),
            pltpu.SemaphoreType.DMA((80,)),
            pltpu.SemaphoreType.DMA((4,)),
        ],
        compiler_params=pltpu.CompilerParams(
            collective_id=2, has_side_effects=True, vmem_limit_bytes=VMEM_LIMIT
        ),
        name="backward",
    )(
        low, hidden, act_i, act_o, slope_i, slope_o, w_up, wu_o, w_down, wd_o, second, normed1, inverse1,
        w_out, wo_o, ctx, x, query, keys, values, probs_a, probs_m, w_query, w_key, w_value, wq_o, wk_o, wv_o,
        output, norm1_gain, vec2,
    )
    quarter = dim // 4
    const = lambda *dims: pl.BlockSpec(dims, lambda j, pos: (0,) * len(dims))
    full_block = lambda j, pos: (jnp.where(pos[2] == 0, jnp.minimum(j, 1), jnp.clip(j - 1, 0, 1)), 0)
    row_block = pl.BlockSpec((half, dim), lambda j, pos: (jnp.minimum(j, 2), 0))
    by_rows = lambda n, m: pl.BlockSpec((n, m), lambda j, pos: (pos[0] ^ j, 0))
    (
        output, input_grad, w_query_grad, w_key_grad, w_value_grad, w_out_grad, w_up_grad, w_down_grad,
        b_query_grad, b_value_grad, b_up_grad, norm1_gain_grad, norm1_bias_grad, b_out_grad,
        norm2_gain_grad, norm2_bias_grad, b_down_grad,
    ) = call(
        final_body,
        (4,),
        pos,
        [sums, top, output, top, output, in_mid, out_mid, vec],
        [
            pl.BlockSpec((1, size, width), lambda j, pos: (j, 0, 0)),
            pl.BlockSpec((half, dim), full_block),
            pl.BlockSpec((half, dim), full_block),
            *[pl.BlockSpec((half, dim), lambda j, pos: (2, 0))] * 2,
            whole(in_mid),
            whole(out_mid),
            whole(vec),
        ],
        [
            shape((rows, dim), BF16),
            shape((rows, dim), F32),
            *[shape((dim, width), F32)] * 3,
            shape((width, dim), F32),
            shape((dim, units), F32),
            shape((units, dim), F32),
            *[shape((n,), F32) for n in (width, width, units, *[dim] * 6)],
        ],
        [
            row_block,
            row_block,
            *[by_rows(quarter, width)] * 3,
            const(width, dim),
            pl.BlockSpec((dim, chunk), lambda j, pos: (0, pos[0] ^ j)),
            by_rows(chunk, dim),
            *[const(n) for n in (width, width, units, *[dim] * 6)],
        ],
        [pltpu.VMEM((dim, width), F32)],
        0,
        "final",
    )
    return (
        output,
        input_grad,
        w_query_grad,
        b_query_grad,
        w_key_grad,
        w_value_grad,
        b_value_grad,
        w_out_grad,
        b_out_grad,
        norm1_gain_grad,
        norm1_bias_grad,
        w_up_grad,
        b_up_grad,
        w_down_grad,
        b_down_grad,
        norm2_gain_grad,
        norm2_bias_grad,
    )


def solution(mesh):
    depth = mesh.shape["dp"] // 4
    inner = Mesh(mesh.devices.reshape(depth, 2, 2, mesh.shape["mp"]), ("z", "x", "c", "y"))
    dp = ("z", "x", "c")
    every = (*dp, "y")
    placed = (
        P(every, None),
        P(dp, None),
        P(dp),
        P(None, "y"),
        P("y"),
        P(None, "y"),
        P(None, "y"),
        P("y"),
        P("y", None),
        P(),
        P(),
        P(),
        P(None, "y"),
        P("y"),
        P("y", None),
        P(),
        P(),
        P(),
        P(every, None),
    )
    return jax.shard_map(
        functools.partial(shards, depth),
        mesh=inner,
        in_specs=placed,
        out_specs=(
            P(every, None),
            P(every, None),
            P(None, "y"),
            P("y"),
            P(None, "y"),
            P(None, "y"),
            P("y"),
            P("y", None),
            P(),
            P(),
            P(),
            P(None, "y"),
            P("y"),
            P("y", None),
            P(),
            P(),
            P(),
        ),
        check_vma=False,
    )
```
